256 devices in a mesh: seq: 64 (over y, z, x_hi), head: 2 (over x_lo), slide: 2 (over core).
Axes of the slice: x: 4 (x_hi: 2, x_lo: 2; x = x_hi * 2 + x_lo), y: 4, z: 8, core: 2. Of those that a mesh axis runs over, the one named last changes fastest.
Arguments:
- query_rows: bfloat16 [65536, 1536], P(('slide', 'seq'), 'head'), parts along dimension 0, may hold values from -32 to 32
- key_rows: bfloat16 [65536, 1536], P(('slide', 'seq'), 'head'), parts along dimension 0, may hold values from -32 to 32
- value_rows: bfloat16 [65536, 1536], P(('slide', 'seq'), 'head'), parts along dimension 0, may hold values from -6 to 6
- patch_valid: int32 [65536], P(('slide', 'seq')), parts along dimension 0, may hold values 0 or 1
- segment_lengths: int32 [4, 3], replicated, may hold values from 256 to 2048, as said below
- dilation: int32 [4, 3], replicated, may hold values from 1 to 8, as said below
- step_sizes: float32 [24, 65536], P('head', ('slide', 'seq')), parts along dimension 1, may hold values from 0.02 to 0.2
- decay_rates: float32 [24, 65536], P('head', ('slide', 'seq')), parts along dimension 1, may hold values from 0 to 2
- state_in: bfloat16 [65536, 128], P(('slide', 'seq')), parts along dimension 0, may hold values from -6 to 6
- state_out: bfloat16 [65536, 128], P(('slide', 'seq')), parts along dimension 0, may hold values from -0.5 to 0.5
- gate_in: bfloat16 [65536, 1536], P(('slide', 'seq'), 'head'), parts along dimension 0, may hold values from -6 to 6
- skip_weight: float32 [24], P('head'), may hold values from 0.5 to 2
- norm_gain: float32 [1536], P('head'), may hold values from 0.1 to 1.9
Outputs:
- attended: bfloat16 [65536, 1536], P(('slide', 'seq'), 'head'), parts along dimension 0
- scanned: bfloat16 [65536, 1536], P(('slide', 'seq'), 'head'), parts along dimension 0
The draws below stay inside these ranges and needn't reach their ends.
There are 2 independent parts, one for each index of `slide`. The reference program is written for one: setup_inputs(seed, part) draws one part's arguments, and reference() takes and returns one part's arrays. A program takes and returns all parts, laid end to end along the dimension named above; an argument that names none is the same for every part. Nothing has to cross between parts.
Inputs may be any that keep to these rules, and one draw needn't show every extreme that they name: `segment_lengths`: every segment length divides 4 * 512 and is a multiple of the dilation of the same group and configuration; in every group the first configuration's segment length divides 512 and the last configuration's segment length is 2048. `dilation`: powers of two; the first configuration's dilation is 1 in every group, every other configuration's dilation is 2 or more.
All inputs are finite; a program needn't handle non-finite values. No bound on the sum of `patch_valid` on one device may be relied on, other than what follows from the above.
Results may differ from the reference program's by a relative error of at most 0.0075.
Values may be sent and summed in bfloat16 or wider, within the bound.
No kernel may reach another device: no remote copies, remote signals or barrier semaphores. Data moves between devices by JAX's collectives and lax.ppermute only.
A program may use at most 128 MiB of HBM per device.

```python
import math
import jax
import jax.numpy as jnp
from jax import lax

HEADS = 24
HEAD_DIM = 64
STATE = 128
GROUPS = 4
CONFIGS = 3
SPAN_DEV = 4
TOK_DEV = 512
SLIDE_TOKEN_LEN = 32768


def drawn_rows(key, role_index):
    full_shape = (SLIDE_TOKEN_LEN, HEADS, HEAD_DIM)
    own_key = jax.random.fold_in(key, 11 + role_index)
    result = jnp.clip(jax.random.normal(own_key, full_shape, jnp.float32), -6.0, 6.0)
    return result.reshape(SLIDE_TOKEN_LEN, HEADS * HEAD_DIM)


def draw_query_rows(key, part):
    return drawn_rows(key, 0).astype(jnp.bfloat16)


def draw_key_rows(key, part):
    return drawn_rows(key, 1).astype(jnp.bfloat16)


def plan_table(key):
    chosen_group = jax.random.randint(jax.random.fold_in(key, 100), (), 0, GROUPS)
    picks = jax.random.randint(jax.random.fold_in(key, 101), (GROUPS, 4), 0, 2)
    middle_pick = jax.random.randint(jax.random.fold_in(key, 102), (GROUPS,), 0, 4)
    first_group = (jnp.arange(GROUPS, dtype=jnp.int32) == chosen_group).astype(jnp.int32)
    nearest = TOK_DEV // 2 * (1 + picks[:, 0] * (1 - first_group))
    middle_table = jnp.array([TOK_DEV // 2, TOK_DEV, 2 * TOK_DEV, SPAN_DEV * TOK_DEV], jnp.int32)
    middle = middle_table[middle_pick]
    widest = jnp.full((GROUPS,), SPAN_DEV * TOK_DEV, jnp.int32)
    stride_mid = 2 * (1 + picks[:, 2])
    stride_far = 4 * (1 + jnp.maximum(picks[:, 3], first_group))
    lengths = jnp.stack([nearest, middle, widest], axis=1).astype(jnp.int32)
    strides = jnp.stack([jnp.ones((GROUPS,), jnp.int32), stride_mid, stride_far], axis=1).astype(jnp.int32)
    return (lengths, strides)


def draw_segment_lengths(key, part):
    return plan_table(key)[0]


def draw_dilation(key, part):
    return plan_table(key)[1]


def draw_decay_rates(key, part):
    full_shape = (HEADS, SLIDE_TOKEN_LEN)
    fast_share = 0.4
    picks = jax.random.uniform(jax.random.fold_in(key, 1), (HEADS, 1), jnp.float32)
    rapid_decay = picks < fast_share
    brisk_branch = jnp.exp(jax.random.uniform(jax.random.fold_in(key, 2), full_shape, jnp.float32, math.log(1.0 / 60.0), math.log(1.0 / 25.0)))
    gentle_decay = jnp.exp(jax.random.uniform(jax.random.fold_in(key, 3), full_shape, jnp.float32, math.log(0.1), math.log(0.5))) / SLIDE_TOKEN_LEN
    spike_location = jax.random.randint(jax.random.fold_in(key, 4), (3,), 0, SLIDE_TOKEN_LEN)
    spike_length = jnp.exp(jax.random.uniform(jax.random.fold_in(key, 5), (3,), jnp.float32, math.log(0.22), math.log(0.5)))
    token_places = jnp.arange(SLIDE_TOKEN_LEN, dtype=jnp.int32)
    spike_groups = jnp.sum(jnp.where(token_places[None, :] == spike_location[:, None], spike_length[:, None], 0.0), axis=0)
    return jnp.where(rapid_decay, brisk_branch, gentle_decay) + spike_groups[None, :]


def with_ends(values, key, least, high):
    spot = [jax.random.randint(jax.random.fold_in(key, axis), (), 0, length) for axis, length in enumerate(values.shape)]
    longest = values.shape.index(max(values.shape))
    neighbour = spot[:longest] + [(spot[longest] + 1) % values.shape[longest]] + spot[longest + 1:]
    return values.at[tuple(spot)].set(least).at[tuple(neighbour)].set(high)


def steps_of(stream_key, extent, split, low, largest):
    def one(dim, blocks):
        heights = jax.random.uniform(jax.random.fold_in(jax.random.fold_in(stream_key, 6), dim), (blocks,), jnp.float32, low / len(split), largest / len(split))
        return jnp.repeat(jnp.exp(heights), extent[dim] // blocks).reshape((-1,) + (1,) * (len(extent) - dim - 1))

    level = one(*split[0])
    for cut in split[1:]:
        level = level * one(*cut)
    return level


def gaussian(key, shape, spread, limit, split=(), held_as=jnp.bfloat16):
    loudness = steps_of(key, shape, split, -0.22, 0.18) if split else 1.0
    drawn = jax.random.normal(key, shape, jnp.float32) * spread * loudness
    return jnp.minimum(jnp.maximum(drawn, -limit), limit).astype(held_as)


def setup_inputs(seed: int = 0, part: int = 0) -> dict:
    key_list = jax.random.split(jax.random.key(seed), 14)
    own_keys = jax.random.split(jax.random.fold_in(key_list[13], part), 14)
    return {
        "query_rows": draw_query_rows(jax.random.fold_in(jax.random.fold_in(key_list[13], part), 71), part),
        "key_rows": draw_key_rows(jax.random.fold_in(jax.random.fold_in(key_list[13], part), 71), part),
        "value_rows": gaussian(own_keys[2], (SLIDE_TOKEN_LEN, HEADS * HEAD_DIM), 1.0, 6.0, ((0, 64), (1, 2))),
        "patch_valid": with_ends((jax.random.randint(own_keys[3], (SLIDE_TOKEN_LEN,), 0, 8) < 7).astype(jnp.int32), jax.random.fold_in(own_keys[3], 1), 0, 1),
        "segment_lengths": draw_segment_lengths(jax.random.fold_in(key_list[13], 71), part),
        "dilation": draw_dilation(jax.random.fold_in(key_list[13], 71), part),
        "step_sizes": jnp.clip(jnp.exp(math.log(0.2) - 2.3025851 * jax.random.uniform(own_keys[6], (HEADS, SLIDE_TOKEN_LEN), jnp.float32) ** steps_of(own_keys[6], (HEADS, SLIDE_TOKEN_LEN), ((0, 2), (1, 64)), -0.2, 0.2)), 0.02, 0.2),
        "decay_rates": draw_decay_rates(jax.random.fold_in(jax.random.fold_in(key_list[13], part), 71), part),
        "state_in": gaussian(own_keys[8], (SLIDE_TOKEN_LEN, STATE), 1.0, 6.0, ((0, 64),)),
        "state_out": gaussian(own_keys[9], (SLIDE_TOKEN_LEN, STATE), STATE ** -0.5, 0.5, ((0, 64),)),
        "gate_in": gaussian(own_keys[10], (SLIDE_TOKEN_LEN, HEADS * HEAD_DIM), 1.0, 6.0, ((0, 64), (1, 2))),
        "skip_weight": jnp.clip(jnp.exp(math.log(2.0) - 1.3862944 * jax.random.uniform(key_list[11], (HEADS,), jnp.float32) ** steps_of(key_list[11], (HEADS,), ((0, 2),), -0.2, 0.2)), 0.5, 2.0),
        "norm_gain": jnp.clip(1.0 + 0.18 * jax.random.normal(key_list[12], (HEADS * HEAD_DIM,), jnp.float32), 0.1, 1.9),
    }


def admitted_count(query_pos, key_pos, key_valid, head_ids, widths, strides):
    offsets = head_ids[:, None] % strides
    counted = jnp.zeros((head_ids.shape[0], query_pos.shape[0], key_pos.shape[0]), jnp.float32)
    for config in range(CONFIGS):
        seg_width = widths[:, config][:, None]
        stride_now = strides[:, config][:, None]
        offset_now = offsets[:, config][:, None]
        query_seg = query_pos[None, :] // seg_width
        key_seg = key_pos[None, :] // seg_width
        query_on = query_pos[None, :] % stride_now == offset_now
        key_on = key_pos[None, :] % stride_now == offset_now
        joined = (query_seg[:, :, None] == key_seg[:, None, :]) & query_on[:, :, None] & key_on[:, None, :]
        counted = counted + joined.astype(jnp.float32)
    opened = (key_valid[None, :] > 0) | (query_pos[:, None] == key_pos[None, :])
    return counted * opened[None].astype(jnp.float32)

def reference(query_rows, key_rows, value_rows, patch_valid, segment_lengths, dilation, step_sizes, decay_rates, state_in, state_out, gate_in, skip_weight, norm_gain):
    score_scale = HEAD_DIM ** (-0.5)
    head_ids = jnp.arange(HEADS, dtype=jnp.int32)
    group_ids = head_ids // (HEADS // GROUPS)
    widths = segment_lengths[group_ids]
    strides = dilation[group_ids]
    window = SPAN_DEV * TOK_DEV

    def one_block(block_idx):
        row_start = (block_idx * TOK_DEV).astype(jnp.int32)
        key_start = (block_idx // SPAN_DEV * window).astype(jnp.int32)
        query_blk = lax.dynamic_slice_in_dim(query_rows, row_start, TOK_DEV, 0).reshape(TOK_DEV, HEADS, HEAD_DIM).astype(jnp.float32)
        key_blk = lax.dynamic_slice_in_dim(key_rows, key_start, window, 0).reshape(window, HEADS, HEAD_DIM).astype(jnp.float32)
        value_blk = lax.dynamic_slice_in_dim(value_rows, key_start, window, 0).reshape(window, HEADS, HEAD_DIM).astype(jnp.float32)
        valid_keys = lax.dynamic_slice_in_dim(patch_valid, key_start, window, 0)
        valid_here = lax.dynamic_slice_in_dim(patch_valid, row_start, TOK_DEV, 0).astype(jnp.float32)
        query_pos = row_start + jnp.arange(TOK_DEV, dtype=jnp.int32)
        key_pos = key_start + jnp.arange(window, dtype=jnp.int32)
        scores = jnp.einsum('thd,shd->hts', query_blk, key_blk) * score_scale
        counted = admitted_count(query_pos, key_pos, valid_keys, head_ids, widths, strides)
        admits = counted > 0
        row_top = lax.optimization_barrier(jnp.max(jnp.where(admits, scores, -jnp.inf), axis=-1, keepdims=True))
        weights = counted * jnp.exp(jnp.where(admits, scores, row_top) - row_top)
        row_total = lax.optimization_barrier(jnp.sum(weights, axis=-1))
        rounded = lax.optimization_barrier(weights.astype(jnp.bfloat16)).astype(jnp.float32)
        mixing = jnp.einsum('hts,shd->thd', rounded, value_blk)
        result = mixing / row_total.T[:, :, None] * valid_here[:, None, None]
        return result.reshape(TOK_DEV, HEADS * HEAD_DIM).astype(jnp.bfloat16)
    block_count = SLIDE_TOKEN_LEN // TOK_DEV
    attended = lax.map(one_block, jnp.arange(block_count, dtype=jnp.int32)).reshape(SLIDE_TOKEN_LEN, HEADS * HEAD_DIM)
    highest = lax.Precision.HIGHEST
    inputs_all = value_rows.reshape(block_count, TOK_DEV, HEADS, HEAD_DIM).astype(jnp.float32)
    steps_blk = step_sizes.reshape(HEADS, block_count, TOK_DEV).transpose(1, 0, 2)
    rates_blk = decay_rates.reshape(HEADS, block_count, TOK_DEV).transpose(1, 0, 2)
    valid_blk = patch_valid.reshape(block_count, TOK_DEV).astype(jnp.float32)
    into_blk = state_in.reshape(block_count, TOK_DEV, STATE).astype(jnp.float32)
    read_blk = state_out.reshape(block_count, TOK_DEV, STATE).astype(jnp.float32)
    gate_blk = gate_in.reshape(block_count, TOK_DEV, HEADS, HEAD_DIM).astype(jnp.float32)
    token_places = jnp.arange(TOK_DEV, dtype=jnp.int32)
    causal = token_places[:, None] >= token_places[None, :]

    def advance(carried, pieces):
        inputs_now, steps_now, rates_now, valid_now, into_now, read_now, gate_now = pieces
        log_decay = -jnp.cumsum(rates_now, axis=1)
        driven = inputs_now * (steps_now.T * valid_now[:, None])[:, :, None]
        coupling = jnp.dot(read_now, into_now.T, precision=highest)
        decays = jnp.exp(jnp.where(causal[None], log_decay[:, :, None] - log_decay[:, None, :], -jnp.inf))
        within = jnp.einsum('hts,shp->thp', decays * coupling[None], driven, precision=highest)
        from_before = jnp.exp(log_decay).T[:, :, None] * jnp.einsum('tn,hpn->thp', read_now, carried, precision=highest)
        readout = within + from_before + skip_weight[None, :, None] * inputs_now
        gated_out = readout * jax.nn.silu(gate_now)
        normed = gated_out * lax.rsqrt(lax.optimization_barrier(jnp.mean(gated_out * gated_out, axis=-1, keepdims=True)) + 1e-05) * norm_gain.reshape(HEADS, HEAD_DIM)
        to_end = jnp.exp(log_decay[:, -1:] - log_decay)
        end_state = jnp.einsum('shp,sn->hpn', driven * to_end.T[:, :, None], into_now, precision=highest)
        carried = jnp.exp(log_decay[:, -1])[:, None, None] * carried + end_state
        return (carried, normed.reshape(TOK_DEV, HEADS * HEAD_DIM).astype(jnp.bfloat16))
    initial = jnp.zeros((HEADS, HEAD_DIM, STATE), jnp.float32)
    final_state, scanned = lax.scan(advance, initial, (inputs_all, steps_blk, rates_blk, valid_blk, into_blk, read_blk, gate_blk))
    scanned = scanned.reshape(SLIDE_TOKEN_LEN, HEADS * HEAD_DIM)
    return (attended, scanned)
```

```python
import functools
import math

import jax
import jax.numpy as jnp
import numpy as np
from jax import lax
from jax.experimental import pallas as pl
from jax.experimental.pallas import tpu as pltpu
from jax.sharding import PartitionSpec as P

HEAD_DIM = 64
STATE = 128
HEADS_PER_GROUP = 6
SPAN_DEV = 4
ROWS = 512
HALF = 256
PAIRS = 6
HEADS_HERE = 12
QUARTER = 192
PIECE = 208
NEG = -1e30
F32 = jnp.float32
BF16 = jnp.bfloat16

LN2_HI = float(np.float32(jnp.bfloat16(math.log(2.0))))
LN2_LO = float(np.float32(jnp.bfloat16(math.log(2.0) - LN2_HI)))
LN3_HI = float(np.float32(jnp.bfloat16(math.log(3.0))))
LN3_LO = float(np.float32(jnp.bfloat16(math.log(3.0) - LN3_HI)))

VMEM = pl.BlockSpec(memory_space=pltpu.VMEM)
SMEM = pl.BlockSpec(memory_space=pltpu.SMEM)


def iota(shape, dim):
    return lax.broadcasted_iota(jnp.int32, shape, dim)


def dot(a, b):
    return lax.dot_general(a, b, (((1,), (0,)), ((), ())), preferred_element_type=F32)


def dot_t(a, b):
    return lax.dot_general(a, b, (((1,), (1,)), ((), ())), preferred_element_type=F32)


def t_dot(a, b):
    return lax.dot_general(a, b, (((0,), (0,)), ((), ())), preferred_element_type=F32)


def one(mask, kind=F32):
    return jnp.where(mask, 1.0, 0.0).astype(kind)


def residue_of(block):
    return ((block & 1) << 2) | (block & 2) | (block >> 2)


def sorting():
    row = iota((ROWS, ROWS), 0)
    token = 8 * (row & 63) + residue_of(row >> 6)
    return one(iota((ROWS, ROWS), 1) == token, BF16)


def split(x, parts):
    out = []
    for _ in range(parts):
        head = x.astype(BF16)
        out.append(head)
        x = x - head.astype(F32)
    return out


def params(mib=40):
    return pltpu.CompilerParams(vmem_limit_bytes=mib * 1024 * 1024)


def pack_kernel(k_ref, v_ref, valid_ref, out_ref):
    sort = sorting()
    low = (iota((HALF, 2 * HEAD_DIM * PAIRS), 1) & 127) < HEAD_DIM
    for at, ref in ((0, k_ref), (HALF, v_ref)):
        rows = dot(sort, ref[...])
        out_ref[at : at + HALF, :] = jnp.where(low, rows[:HALF], rows[HALF:]).astype(BF16)
    valid = jnp.broadcast_to(valid_ref[...].astype(F32), (16, ROWS)).astype(BF16)
    line = dot_t(valid, sort)
    out_ref[ROWS : ROWS + 16, :] = jnp.concatenate(
        [line, jnp.zeros((16, 2 * HEAD_DIM * PAIRS - ROWS), F32)], axis=1
    ).astype(BF16)


def plan_bias(head, seg_ref, dil_ref, near):
    group = head // HEADS_PER_GROUP
    r1, r2 = dil_ref[group, 1], dil_ref[group, 2]
    w0, w1 = seg_ref[group, 0], seg_ref[group, 1]
    shape = (128, 128)
    key, lane = iota(shape, 0), iota(shape, 1)
    query = lane & 15
    if near is None:
        key_at, query_at = residue_of(key >> 1), residue_of(query >> 1)
    else:
        key_at = residue_of((key >> 1) & 3) + (head & 1)
        query_at = residue_of((query >> 1) & 3) + (head & 1)
    same = (key & 1) == (query & 1)
    key_off, query_off = key_at - head, query_at - head

    def on(stride):
        return (key_off & (stride - 1)) + (query_off & (stride - 1)) == 0

    if near is None:
        count = (
            one(same | (w0 >= ROWS)) + one(on(r1) & (same | (w1 >= ROWS))) + one(on(r2))
        )
    else:
        reach = 2 * ROWS if near else 4 * ROWS
        count = one(on(r1) & (w1 >= reach)) + one(on(r2))
    high = jnp.where(count == 0, NEG, jnp.where(count == 2, LN2_HI, jnp.where(count == 3, LN3_HI, 0.0)))
    low = jnp.where(count == 2, LN2_LO, jnp.where(count == 3, LN3_LO, 0.0))
    value = jnp.where(lane < 16, high, jnp.where(lane < 32, low, 0.0))
    return jnp.where(key < 16, value, 0.0).astype(BF16)


def query_side(rows):
    row, lane = iota((rows, 128), 0), iota((rows, 128), 1)
    return one(((row >> 5) == (lane & 15)) & (lane < 32) | (lane == 32), BF16)


def key_side(rows):
    row, lane = iota((rows, 128), 0), iota((rows, 128), 1)
    return one((row >> 5) == lane, BF16)


def local_kernel(
    q_ref, k_ref, v_ref, valid_ref, seg_ref, dil_ref, rank_ref,
    qe_ref, oe_ref, le_ref, me_ref, oo_ref,
    sort_ref, vbias_ref, vcol_ref,
):
    pair = pl.program_id(0)

    @pl.when(pair == 0)
    def _():
        sort_ref[...] = sorting()
        valid = jnp.broadcast_to(valid_ref[...].astype(F32), (128, ROWS)).astype(BF16)
        column = dot_t(sort_ref[...], valid)
        vcol_ref[...] = column
        vbias_ref[...] = jnp.where(iota((ROWS, 128), 1) == 32, (1.0 - column) * NEG, 0.0)

    sort = sort_ref[...]
    packed = dot(sort, jnp.concatenate([q_ref[...], k_ref[...], v_ref[...]], axis=1))
    query = packed[:, :128] * (HEAD_DIM**-0.5)
    key = packed[:, 128:256].astype(BF16)
    value = jnp.concatenate([packed[:, 256:].astype(BF16), jnp.ones((ROWS, 128), BF16)], axis=1)
    lane = iota((ROWS, 128), 1)
    q_side, k_side = query_side(ROWS), key_side(ROWS)
    results = []
    for part in range(2):
        head = rank_ref[0] * HEADS_HERE + 2 * pair + part
        mine = (lane < HEAD_DIM) if part == 0 else (lane >= HEAD_DIM)
        bias = dot(k_side, plan_bias(head, seg_ref, dil_ref, None))
        mine_query = jnp.where(mine, query, 0.0)
        left = jnp.concatenate([mine_query.astype(BF16), q_side], axis=1)
        right = jnp.concatenate([key, (bias + vbias_ref[...]).astype(BF16)], axis=1)
        own = jnp.sum(
            mine_query * key.astype(F32) + jnp.where(lane == 32, 0.0, q_side.astype(F32) * bias),
            axis=1,
            keepdims=True,
        )
        scores = dot_t(left, right)
        scores = jnp.where(iota((ROWS, ROWS), 0) == iota((ROWS, ROWS), 1), own, scores)
        top = jnp.max(scores, axis=1, keepdims=True)
        weights = jnp.exp(scores - top).astype(BF16)
        results.append((dot(weights, value), top))
    low = lane < HEAD_DIM
    (out0, top0), (out1, top1) = results
    out = jnp.where(low, out0[:, :128], out1[:, :128])
    total = jnp.where(low, out0[:, 128:], out1[:, 128:])
    top = jnp.where(low, top0, top1)
    low = low[:HALF]
    qe_ref[...] = jnp.where(low, query[:HALF], query[HALF:]).astype(BF16)
    oe_ref[...] = jnp.where(low, out[:HALF], out[HALF:])
    le_ref[...] = jnp.where(low, total[:HALF], total[HALF:])
    me_ref[...] = jnp.where(low, top[:HALF], top[HALF:])
    done = out / total * vcol_ref[...]
    oo_ref[...] = jnp.where(low, done[HALF:], done[:HALF]).astype(BF16)


def remote_kernel(
    qe_ref, oe_ref, le_ref, me_ref, oo_ref,
    k1_ref, v1_ref, k2_ref, v2_ref, k3_ref, v3_ref, f1_ref, f2_ref, f3_ref,
    valid_ref, seg_ref, dil_ref, rank_ref,
    out_ref, sort_ref, vcol_ref, vbias_ref,
):
    pair = pl.program_id(0)
    keys = 3 * HALF

    @pl.when(pair == 0)
    def _():
        sort_ref[...] = sorting()
        valid = jnp.broadcast_to(valid_ref[...].astype(F32), (128, ROWS)).astype(BF16)
        vcol_ref[...] = dot_t(sort_ref[...], valid)
        spread = one((iota((16, 128), 0) == 0) & (iota((16, 128), 1) == 32), BF16)
        for at, ref in enumerate((f1_ref, f2_ref, f3_ref)):
            for parity in range(2):
                line = (1.0 - ref[:, parity * HALF : (parity + 1) * HALF].astype(F32)) * NEG
                vbias_ref[parity, at * HALF : (at + 1) * HALF, :] = t_dot(line.astype(BF16), spread)

    key = jnp.concatenate([k1_ref[...], k2_ref[...], k3_ref[...]], axis=0)
    value = jnp.concatenate([v1_ref[...], v2_ref[...], v3_ref[...]], axis=0)
    value = jnp.concatenate([value, jnp.ones((keys, 128), BF16)], axis=1)
    lane = iota((HALF, 128), 1)
    q_side, k_side = query_side(HALF), key_side(HALF)
    results = []
    for part in range(2):
        head = rank_ref[0] * HEADS_HERE + 2 * pair + part
        mine = (lane < HEAD_DIM) if part == 0 else (lane >= HEAD_DIM)
        close = dot(k_side, plan_bias(head, seg_ref, dil_ref, True))
        far = dot(k_side, plan_bias(head, seg_ref, dil_ref, False))
        bias = jnp.concatenate([close, far, far], axis=0) + vbias_ref[part]
        left = jnp.concatenate([jnp.where(mine, qe_ref[...], jnp.zeros((), BF16)), q_side], axis=1)
        right = jnp.concatenate([key, bias.astype(BF16)], axis=1)
        scores = dot_t(left, right)
        before = me_ref[:, part * HEAD_DIM : part * HEAD_DIM + 1]
        top = jnp.maximum(jnp.max(scores, axis=1, keepdims=True), before)
        weights = jnp.exp(scores - top).astype(BF16)
        results.append((dot(weights, value), top))
    low = lane < HEAD_DIM
    (out0, top0), (out1, top1) = results
    rescale = jnp.exp(me_ref[...] - jnp.where(low, top0, top1))
    out = jnp.where(low, out0[:, :128], out1[:, :128]) + oe_ref[...] * rescale
    total = jnp.where(low, out0[:, 128:], out1[:, 128:]) + le_ref[...] * rescale
    valid = jnp.where(low, vcol_ref[:HALF, :], vcol_ref[HALF:, :])
    done = (out / total * valid).astype(BF16)
    other = oo_ref[...]
    rows = jnp.concatenate([jnp.where(low, done, other), jnp.where(low, other, done)], axis=0)
    out_ref[...] = t_dot(sort_ref[...], rows).astype(BF16)


def state_kernel(v_ref, steps_ref, rates_ref, valid_ref, into_ref, place_ref, *out_refs):
    full_ref = out_refs[4]
    later = one(iota((ROWS, ROWS), 0) > iota((ROWS, ROWS), 1), BF16)
    rates = jnp.concatenate([rates_ref[...], jnp.zeros((4, ROWS), F32)], axis=0)
    sums = dot(jnp.concatenate(split(rates, 3), axis=0), later)
    to_end = sums[:16] + sums[16:32] + sums[32:]
    steps = jnp.concatenate([steps_ref[...], jnp.zeros((4, ROWS), F32)], axis=0)
    weight = jnp.exp(-to_end) * steps * valid_ref[...].astype(F32)
    width = HEADS_HERE * HEAD_DIM
    spread = one((iota((32, width), 0) & 15) == (iota((32, width), 1) >> 6), BF16)
    scale = t_dot(jnp.concatenate(split(weight, 2), axis=0), spread)
    driven = (v_ref[...].astype(F32) * scale).astype(BF16)
    full_ref[...] = t_dot(driven, into_ref[...])
    decay = jnp.exp(-jnp.sum(rates, axis=1, keepdims=True))
    decay = jnp.concatenate(split(jnp.broadcast_to(decay, (16, STATE)), 2), axis=0)
    row, source = iota((16, 32), 0), iota((16, 32), 1)
    for step in range(4):
        part = place_ref[0] ^ step
        wanted = jnp.where(row < 3, part * 3 + row, jnp.where(row < 6, 13 + part * 3 + row, -1))
        start = pl.multiple_of(part * QUARTER, 64)
        out_refs[step][:QUARTER, :] = full_ref[pl.ds(start, QUARTER), :].astype(BF16)
        out_refs[step][QUARTER:, :] = dot(one(source == wanted, BF16), decay).astype(BF16)


def decay_rows(ref_value):
    tail = ref_value[QUARTER:].astype(F32)
    return [tail[k : k + 1] + tail[k + 3 : k + 4] for k in range(3)]


def spread_rows(decays):
    return jnp.concatenate([jnp.broadcast_to(d, (HEAD_DIM, STATE)) for d in decays], axis=0)


def pack_piece(state, decays):
    high, low = zip(*(split(d, 2) for d in decays))
    tail = jnp.concatenate(
        [d.astype(F32) for d in high + low] + [jnp.zeros((10, STATE), F32)], axis=0
    )
    return jnp.concatenate([state, tail], axis=0).astype(BF16)


def block_kernel(place_ref, a0, a1, a2, a3, total_ref, before_ref, fade_ref, held):
    for step, ref in enumerate((a0, a1, a2, a3)):
        held[place_ref[0] ^ step] = ref[...].astype(F32)
    state = jnp.zeros((QUARTER, STATE), F32)
    decays = [jnp.ones((1, STATE), F32)] * 3
    for at in range(4):
        before_ref[at] = state
        fade_ref[at] = spread_rows(decays)
        now = decay_rows(held[at])
        state = state * spread_rows(now) + held[at, :QUARTER, :]
        decays = [a * b for a, b in zip(decays, now)]
    total_ref[...] = pack_piece(state, decays)


def chain(place, held):
    state = jnp.zeros((QUARTER, STATE), F32)
    decays = [jnp.ones((1, STATE), F32)] * 3
    before, before_decays = state, decays
    for at in range(4):
        here = place == at
        before = jnp.where(here, state, before)
        before_decays = [jnp.where(here, a, b) for a, b in zip(decays, before_decays)]
        now = decay_rows(held[at])
        state = state * spread_rows(now) + held[at, :QUARTER, :]
        decays = [a * b for a, b in zip(decays, now)]
    return before, before_decays, state, decays


def line_kernel(place_ref, a0, a1, a2, a3, total_ref, before_ref, fade_ref, held):
    for step, ref in enumerate((a0, a1, a2, a3)):
        held[(place_ref[1] - step) & 3] = ref[...].astype(F32)
    before, before_decays, state, decays = chain(place_ref[1], held)
    before_ref[...] = before
    fade_ref[...] = spread_rows(before_decays)
    total_ref[...] = pack_piece(state, decays)


def plane_kernel(place_ref, a0, a1, a2, a3, line_before, line_fade, block_before, block_fade, *rest):
    outs, held = rest[:4], rest[4]
    for step, ref in enumerate((a0, a1, a2, a3)):
        held[(place_ref[2] - step) & 3] = ref[...].astype(F32)
    before = chain(place_ref[2], held)[0]
    start = line_fade[...] * before + line_before[...]
    for step in range(4):
        part = place_ref[0] ^ step
        outs[step][...] = (block_fade[part] * start + block_before[part]).astype(BF16)


def within_kernel(
    v_ref, gate_ref, steps_ref, rates_ref, valid_ref, into_ref, read_ref, skip_ref,
    base_ref, lift_ref, couple_ref, col_ref, row_ref,
):
    pair = pl.program_id(0)

    @pl.when(pair == 0)
    def _():
        couple_ref[...] = dot_t(read_ref[...], into_ref[...])
        upto = one(iota((ROWS, ROWS), 0) <= iota((ROWS, ROWS), 1), BF16)
        rates = jnp.concatenate([rates_ref[...], jnp.zeros((4, ROWS), F32)], axis=0)
        sums = dot(jnp.concatenate(split(rates, 3), axis=0), upto)
        fall = -(sums[:16] + sums[16:32] + sums[32:])
        steps = jnp.concatenate([steps_ref[...], jnp.ones((4, ROWS), F32)], axis=0)
        col_ref[...] = fall
        row_ref[...] = jnp.where(valid_ref[...] > 0, fall - jnp.log(steps), -NEG)

    value = v_ref[...]
    lane = iota((ROWS, 128), 1)
    results = []
    falls = []
    tile = 128
    causal = iota((tile, tile), 0) >= iota((tile, tile), 1)
    for part in range(2):
        head = 2 * pair + part
        fall = jnp.broadcast_to(col_ref[pl.ds(head, 1), :], (128, ROWS)).T
        line = row_ref[pl.ds(head, 1), :]
        pieces = []
        for at in range(ROWS // tile):
            fall_now = fall[at * tile : (at + 1) * tile]
            weights = []
            for src in range(at + 1):
                gap = fall_now - line[:, src * tile : (src + 1) * tile]
                if src == at:
                    gap = jnp.where(causal, gap, NEG)
                weights.append(
                    (
                        jnp.exp(gap)
                        * couple_ref[at * tile : (at + 1) * tile, src * tile : (src + 1) * tile]
                    ).astype(BF16)
                )
            pieces.append(dot(jnp.concatenate(weights, axis=1), value[: (at + 1) * tile]))
        results.append(jnp.concatenate(pieces, axis=0))
        falls.append(fall)
    low = lane < HEAD_DIM
    gate = gate_ref[...].astype(F32)
    gate = gate / (1.0 + jnp.exp(-gate))
    skip = jnp.where(low, skip_ref[2 * pair], skip_ref[2 * pair + 1])
    within = jnp.where(low, results[0], results[1])
    base_ref[...] = (within + skip * value.astype(F32)) * gate
    lift_ref[...] = jnp.exp(jnp.where(low, falls[0], falls[1])) * gate


def finish_kernel(place_ref, f0, f1, f2, f3, read_ref, base_ref, lift_ref, gain_ref, out_ref, held):
    @pl.when(pl.program_id(0) == 0)
    def _():
        for step, ref in enumerate((f0, f1, f2, f3)):
            part = place_ref[0] ^ step
            held[pl.ds(pl.multiple_of(part * QUARTER, 64), QUARTER), :] = ref[...]

    start = pl.multiple_of(pl.program_id(0) * 128, 128)
    carried = dot_t(read_ref[...], held[pl.ds(start, 128), :])
    gated = base_ref[...] + lift_ref[...] * carried
    together = one((iota((128, 128), 0) >> 6) == (iota((128, 128), 1) >> 6), BF16)
    high, low = split(gated * gated, 2)
    mean = (dot(high, together) + dot(low, together)) * (1.0 / HEAD_DIM)
    out_ref[...] = (gated * lax.rsqrt(mean + 1e-05) * gain_ref[...]).astype(BF16)


def per_device(
    query_rows,
    key_rows,
    value_rows,
    patch_valid,
    segment_lengths,
    dilation,
    step_sizes,
    decay_rates,
    state_in,
    state_out,
    gate_in,
    skip_weight,
    norm_gain,
):
    width = HEADS_HERE * HEAD_DIM
    count = lax.axis_size("seq")
    seq_rank = lax.axis_index("seq").astype(jnp.int32)
    rank = jnp.reshape(lax.axis_index("head").astype(jnp.int32), (1,))
    place = jnp.stack([seq_rank & 3, (seq_rank >> 2) & 3, seq_rank >> 4])
    valid = patch_valid.reshape(1, ROWS)
    gain = norm_gain.reshape(1, width)

    def shape(*dims, kind=BF16):
        return jax.ShapeDtypeStruct(dims, kind)

    def cross(block, mask):
        return lax.ppermute(block, "seq", [(i, i ^ mask) for i in range(count)])

    def turn(block, step, span):
        unit, inner = span // 4, span
        route = [(i, i // inner * inner + (i % inner + step * unit) % inner) for i in range(count)]
        return lax.ppermute(block, "seq", route)

    packed = pl.pallas_call(
        pack_kernel,
        out_shape=shape(ROWS + 16, width),
        in_specs=[VMEM] * 3,
        out_specs=VMEM,
        compiler_params=params(),
        name="pack",
    )(key_rows, value_rows, valid)
    arrived = [cross(packed, mask) for mask in range(1, SPAN_DEV)]

    pieces = pl.pallas_call(
        state_kernel,
        out_shape=[shape(PIECE, STATE)] * 4,
        in_specs=[VMEM] * 5 + [SMEM],
        out_specs=[VMEM] * 4,
        scratch_shapes=[pltpu.VMEM((width, STATE), F32)],
        compiler_params=params(),
        name="state",
    )(value_rows, step_sizes, decay_rates, valid, state_in, place)
    pieces = [pieces[0]] + [cross(pieces[mask], mask) for mask in range(1, SPAN_DEV)]
    hold = [pltpu.VMEM((4, PIECE, STATE), F32)]
    total, block_before, block_fade = pl.pallas_call(
        block_kernel,
        out_shape=[shape(PIECE, STATE), shape(4, QUARTER, STATE, kind=F32), shape(4, QUARTER, STATE, kind=F32)],
        in_specs=[SMEM] + [VMEM] * 4,
        out_specs=[VMEM] * 3,
        scratch_shapes=hold,
        compiler_params=params(),
        name="block",
    )(place, *pieces)
    totals = [total] + [turn(total, step, 16) for step in range(1, 4)]
    total, line_before, line_fade = pl.pallas_call(
        line_kernel,
        out_shape=[shape(PIECE, STATE), shape(QUARTER, STATE, kind=F32), shape(QUARTER, STATE, kind=F32)],
        in_specs=[SMEM] + [VMEM] * 4,
        out_specs=[VMEM] * 3,
        scratch_shapes=hold,
        compiler_params=params(),
        name="line",
    )(place, *totals)
    totals = [total] + [turn(total, step, 64) for step in range(1, 4)]
    carried = pl.pallas_call(
        plane_kernel,
        out_shape=[shape(QUARTER, STATE)] * 4,
        in_specs=[SMEM] + [VMEM] * 8,
        out_specs=[VMEM] * 4,
        scratch_shapes=hold,
        compiler_params=params(),
        name="plane",
    )(place, *totals, line_before, line_fade, block_before, block_fade)
    carried = [carried[0]] + [cross(carried[mask], mask) for mask in range(1, SPAN_DEV)]

    def lanes(rows, row_block=0):
        return pl.BlockSpec((rows, 128), lambda pair: (row_block, pair))

    def whole(*dims):
        return pl.BlockSpec(dims, lambda pair: (0,) * len(dims))

    kept = pl.pallas_call(
        local_kernel,
        grid=(PAIRS,),
        out_shape=[shape(HALF, width)] + [shape(HALF, width, kind=F32)] * 3 + [shape(HALF, width)],
        in_specs=[lanes(ROWS)] * 3 + [whole(1, ROWS), SMEM, SMEM, SMEM],
        out_specs=[lanes(HALF)] * 5,
        scratch_shapes=[pltpu.VMEM((ROWS, ROWS), BF16), pltpu.VMEM((ROWS, 128), F32), pltpu.VMEM((ROWS, 128), F32)],
        compiler_params=params(),
        name="local",
    )(query_rows, key_rows, value_rows, valid, segment_lengths, dilation, rank)

    base, lift = pl.pallas_call(
        within_kernel,
        grid=(PAIRS,),
        out_shape=[shape(ROWS, width, kind=F32)] * 2,
        in_specs=[lanes(ROWS)] * 2
        + [whole(HEADS_HERE, ROWS)] * 2
        + [whole(1, ROWS), whole(ROWS, STATE), whole(ROWS, STATE), SMEM],
        out_specs=[lanes(ROWS)] * 2,
        scratch_shapes=[pltpu.VMEM((ROWS, ROWS), F32), pltpu.VMEM((16, ROWS), F32), pltpu.VMEM((16, ROWS), F32)],
        compiler_params=params(),
        name="within",
    )(value_rows, gate_in, step_sizes, decay_rates, valid, state_in, state_out, skip_weight)

    scanned = pl.pallas_call(
        finish_kernel,
        grid=(PAIRS,),
        out_shape=shape(ROWS, width),
        in_specs=[SMEM]
        + [whole(QUARTER, STATE)] * 4
        + [whole(ROWS, STATE), lanes(ROWS), lanes(ROWS), lanes(1)],
        out_specs=lanes(ROWS),
        scratch_shapes=[pltpu.VMEM((width, STATE), BF16)],
        compiler_params=params(),
        name="finish",
    )(place, *carried, state_out, base, lift, gain)

    flags = pl.BlockSpec((16, width), lambda pair: (ROWS // 16, 0))
    attended = pl.pallas_call(
        remote_kernel,
        grid=(PAIRS,),
        out_shape=shape(ROWS, width),
        in_specs=[lanes(HALF)] * 5
        + [lanes(HALF), lanes(HALF, 1)] * 3
        + [flags] * 3
        + [whole(1, ROWS), SMEM, SMEM, SMEM],
        out_specs=lanes(ROWS),
        scratch_shapes=[
            pltpu.VMEM((ROWS, ROWS), BF16),
            pltpu.VMEM((ROWS, 128), F32),
            pltpu.VMEM((2, 3 * HALF, 128), F32),
        ],
        compiler_params=params(),
        name="remote",
    )(
        *kept,
        *[block for block in arrived for _ in range(2)],
        *arrived,
        valid,
        segment_lengths,
        dilation,
        rank,
    )
    return (attended, scanned)


def solution(mesh):
    return jax.shard_map(
        per_device,
        mesh=mesh,
        in_specs=(
            P(("slide", "seq"), "head"),
            P(("slide", "seq"), "head"),
            P(("slide", "seq"), "head"),
            P(("slide", "seq")),
            P(),
            P(),
            P("head", ("slide", "seq")),
            P("head", ("slide", "seq")),
            P(("slide", "seq"), None),
            P(("slide", "seq"), None),
            P(("slide", "seq"), "head"),
            P("head"),
            P("head"),
        ),
        out_specs=(P(("slide", "seq"), "head"), P(("slide", "seq"), "head")),
        check_vma=False,
    )
```

```python
import functools
import math

import jax
import jax.numpy as jnp
import numpy as np
from jax import lax
from jax.experimental import pallas as pl
from jax.experimental.pallas import tpu as pltpu
from jax.sharding import PartitionSpec as P

HEAD_DIM = 64
STATE = 128
HEADS_PER_GROUP = 6
SPAN_DEV = 4
ROWS = 512
HALF = 256
PAIRS = 6
HEADS_HERE = 12
QUARTER = 192
WIDTH = HEADS_HERE * HEAD_DIM
PIECE = 208
NEG = -1e30
F32 = jnp.float32
BF16 = jnp.bfloat16

LN2_HI = float(np.float32(jnp.bfloat16(math.log(2.0))))
LN2_LO = float(np.float32(jnp.bfloat16(math.log(2.0) - LN2_HI)))
LN3_HI = float(np.float32(jnp.bfloat16(math.log(3.0))))
LN3_LO = float(np.float32(jnp.bfloat16(math.log(3.0) - LN3_HI)))

VMEM = pl.BlockSpec(memory_space=pltpu.VMEM)
SMEM = pl.BlockSpec(memory_space=pltpu.SMEM)


def iota(shape, dim):
    return lax.broadcasted_iota(jnp.int32, shape, dim)


def dot(a, b):
    return lax.dot_general(a, b, (((1,), (0,)), ((), ())), preferred_element_type=F32)


def dot_t(a, b):
    return lax.dot_general(a, b, (((1,), (1,)), ((), ())), preferred_element_type=F32)


def t_dot(a, b):
    return lax.dot_general(a, b, (((0,), (0,)), ((), ())), preferred_element_type=F32)


def one(mask, kind=F32):
    return jnp.where(mask, 1.0, 0.0).astype(kind)


def residue_of(block):
    return ((block & 1) << 2) | (block & 2) | (block >> 2)


def sorting():
    row = iota((ROWS, ROWS), 0)
    token = 8 * (row & 63) + residue_of(row >> 6)
    return one(iota((ROWS, ROWS), 1) == token, BF16)


def unsorting():
    column = iota((ROWS, ROWS), 1)
    token = 8 * (column & 63) + residue_of(column >> 6)
    return one(iota((ROWS, ROWS), 0) == token, BF16)


def split(x, parts):
    out = []
    for _ in range(parts):
        head = x.astype(BF16)
        out.append(head)
        x = x - head.astype(F32)
    return out


def params(mib=14):
    return pltpu.CompilerParams(vmem_limit_bytes=mib * 1024 * 1024)


def pack_kernel(k_ref, v_ref, valid_ref, out_ref):
    sort = sorting()
    unsort = unsorting()
    low = (iota((HALF, WIDTH), 1) & 127) < HEAD_DIM
    rows = dot(sort, k_ref[...])
    out_ref[:HALF, :] = jnp.where(low, rows[:HALF], rows[HALF:]).astype(BF16)
    columns = t_dot(v_ref[...], unsort)
    even = (iota((WIDTH, HALF), 0) & 127) < HEAD_DIM
    columns = jnp.where(even, columns[:, :HALF], columns[:, HALF:]).astype(BF16)
    for at in range(0, WIDTH, HALF):
        out_ref[HALF:ROWS, at : at + HALF] = columns[at : at + HALF]
    valid = jnp.broadcast_to(valid_ref[...].astype(F32), (16, ROWS)).astype(BF16)
    line = dot_t(valid, sort)
    out_ref[ROWS : ROWS + 16, :] = jnp.concatenate(
        [line, jnp.zeros((16, WIDTH - ROWS), F32)], axis=1
    ).astype(BF16)


def log_count(count):
    high = jnp.where(count == 0, NEG, jnp.where(count == 2, LN2_HI, jnp.where(count == 3, LN3_HI, 0.0)))
    low = jnp.where(count == 2, LN2_LO, jnp.where(count == 3, LN3_LO, 0.0))
    return high, low


def plan_of(head, seg_ref, dil_ref):
    group = head // HEADS_PER_GROUP
    return dil_ref[group, 1], dil_ref[group, 2], seg_ref[group, 0], seg_ref[group, 1]


def local_plan(head, seg_ref, dil_ref):
    r1, r2, w0, w1 = plan_of(head, seg_ref, dil_ref)
    key, query = iota((16, ROWS), 0), iota((16, ROWS), 1) >> 5
    same = (key & 1) == (query & 1)
    key_off, query_off = residue_of(key >> 1) - head, residue_of(query >> 1) - head

    def on(stride):
        return (key_off & (stride - 1)) + (query_off & (stride - 1)) == 0

    count = one(same | (w0 >= ROWS)) + one(on(r1) & (same | (w1 >= ROWS))) + one(on(r2))
    return jnp.concatenate([*log_count(count), jnp.ones((16, ROWS), F32)], axis=0)


def remote_plan(head, seg_ref, dil_ref):
    r1, r2, _, w1 = plan_of(head, seg_ref, dil_ref)
    row = iota((8, HALF), 0)
    shift = (head & 1) - head
    key_off = residue_of(row & 3) + shift
    query_off = residue_of(iota((8, HALF), 1) >> 6) + shift

    def on(stride):
        return (key_off & (stride - 1)) + (query_off & (stride - 1)) == 0

    parts = []
    for reach in (2 * ROWS, 4 * ROWS):
        high, low = log_count(one(on(r1) & (w1 >= reach)) + one(on(r2)))
        parts.append(jnp.where(row < 4, high, low))
    return jnp.concatenate(parts + [jnp.ones((16, HALF), F32)], axis=0)


def own_bias(head, dil_ref):
    group = head // HEADS_PER_GROUP
    off = residue_of(iota((1, ROWS), 1) >> 6) - head
    count = 1 + jnp.where((off & (dil_ref[group, 1] - 1)) == 0, 1, 0)
    count = count + jnp.where((off & (dil_ref[group, 2] - 1)) == 0, 1, 0)
    return jnp.where(count == 1, 0.0, jnp.where(count == 2, LN2_HI + LN2_LO, LN3_HI + LN3_LO))


def softmax_columns(keys, queries, values, own, before):
    scores = dot(keys, queries)
    if own is not None:
        tile = 128
        diagonal = iota((tile, tile), 0) == iota((tile, tile), 1)
        rows = []
        for at in range(0, scores.shape[0], tile):
            line = scores[at : at + tile]
            here = jnp.where(diagonal, own[:, at : at + tile], line[:, at : at + tile])
            parts = [line[:, :at], here, line[:, at + tile :]]
            rows.append(jnp.concatenate([x for x in parts if x.shape[1]], axis=1))
        scores = jnp.concatenate(rows, axis=0)
    top = jnp.max(scores, axis=0, keepdims=True)
    if before is not None:
        top = jnp.maximum(top, before)
    values = jnp.concatenate([values, jnp.ones((16, values.shape[1]), BF16)], axis=0)
    out = dot(values, jnp.exp(scores - top).astype(BF16))
    return out[:HEAD_DIM], out[HEAD_DIM : HEAD_DIM + 1], top


def all_queries(rows, part, plan):
    blank = jnp.zeros((HEAD_DIM, rows.shape[1]), BF16)
    pieces = [rows, blank] if part == 0 else [blank, rows]
    rest = jnp.zeros((128 - plan.shape[0], rows.shape[1]), BF16)
    return jnp.concatenate(pieces + [plan.astype(BF16), rest], axis=0)


def local_kernel(
    q_ref, k_ref, v_ref, valid_ref, seg_ref, dil_ref, rank_ref,
    qe_ref, plan_ref, oe_ref, stat_ref, oo_ref, ve_ref,
    unsort_ref, sq_ref, sk_ref, sv_ref,
):
    unsort_ref[...] = unsorting()
    valid = jnp.broadcast_to(valid_ref[...].astype(F32), (128, ROWS)).astype(BF16)
    flags = dot(valid, unsort_ref[...])
    ve_ref[...] = flags[:8]
    row, lane = iota((ROWS, 128), 0), iota((ROWS, 128), 1)
    key_side = one(((row >> 5) == (lane & 15)) & (lane < 32))
    key_side = jnp.where(lane == 32, (1.0 - flags.T) * NEG, key_side).astype(BF16)
    sq_ref[...] = t_dot(q_ref[...], unsort_ref[...]) * (HEAD_DIM**-0.5)
    sk_ref[...] = t_dot(k_ref[...], unsort_ref[...])
    sv_ref[...] = t_dot(v_ref[...], unsort_ref[...]).astype(BF16)
    for pair in range(PAIRS):
        both = slice(pair * 128, (pair + 1) * 128)
        key = sk_ref[both, :].T.astype(BF16)
        keys = jnp.concatenate([key, key_side], axis=1)
        stats = []
        for part in range(2):
            head = rank_ref[0] * HEADS_HERE + 2 * pair + part
            start = pair * 128 + part * HEAD_DIM
            now = slice(start, start + HEAD_DIM)
            query = sq_ref[now, :]
            queries = all_queries(query.astype(BF16), part, local_plan(head, seg_ref, dil_ref))
            own = jnp.sum(query * sk_ref[now, :], axis=0, keepdims=True) + own_bias(head, dil_ref)
            out, total, top = softmax_columns(keys, queries, sv_ref[now, :], own, None)
            inside = slice(part * HALF, (part + 1) * HALF)
            outside = slice((1 - part) * HALF, (2 - part) * HALF)
            qe_ref[now, :] = query[:, inside].astype(BF16)
            oe_ref[now, :] = out[:, inside]
            oo_ref[now, :] = (out[:, outside] / total[:, outside] * flags[:1, outside]).astype(BF16)
            stats += [top[:, inside], total[:, inside]]
            at = (2 * pair + part) * 32
            plan_ref[at : at + 32, :] = remote_plan(head, seg_ref, dil_ref).astype(BF16)
        stat_ref[pair * 8 : pair * 8 + 8, :] = jnp.concatenate(stats + [jnp.zeros((4, HALF), F32)], axis=0)


def remote_kernel(
    qe_ref, plan_ref, oe_ref, stat_ref, oo_ref, ve_ref, kv1_ref, kv2_ref, kv3_ref,
    out_ref, rows_ref,
):
    blocks = (kv1_ref, kv2_ref, kv3_ref)
    spread = one((iota((16, 128), 0) == 0) & (iota((16, 128), 1) == 16), BF16)
    row, lane = iota((HALF, 128), 0), iota((HALF, 128), 1)
    sides = []
    for parity in range(2):
        pieces = []
        for at, ref in enumerate(blocks):
            flags = ref[ROWS : ROWS + 16, parity * HALF : (parity + 1) * HALF].astype(F32)
            line = ((1.0 - flags) * NEG).astype(BF16)
            wanted = (lane & 3) == (row >> 6)
            wanted = wanted & (lane < 8) if at == 0 else wanted & (lane >= 8) & (lane < 16)
            pieces.append(t_dot(line, spread) + one(wanted))
        sides.append(jnp.concatenate(pieces, axis=0).astype(BF16))
    for pair in range(PAIRS):
        both = slice(pair * 128, (pair + 1) * 128)
        place = slice(HALF + (pair & 1) * 128, HALF + (pair & 1) * 128 + 128)
        chunk = slice((pair >> 1) * HALF, (pair >> 1) * HALF + HALF)
        key = jnp.concatenate([ref[:HALF, both] for ref in blocks], axis=0)
        value = jnp.concatenate([ref[place, chunk] for ref in blocks], axis=1)
        for part in range(2):
            start = pair * 128 + part * HEAD_DIM
            now = slice(start, start + HEAD_DIM)
            at = (2 * pair + part) * 32
            keys = jnp.concatenate([key, sides[part]], axis=1)
            queries = all_queries(qe_ref[now, :], part, plan_ref[at : at + 32, :])
            stat = pair * 8 + 2 * part
            before = stat_ref[stat : stat + 1, :]
            out, total, top = softmax_columns(
                keys, queries, value[part * HEAD_DIM : (part + 1) * HEAD_DIM], None, before
            )
            rescale = jnp.exp(before - top)
            out = out + oe_ref[now, :] * rescale
            total = total + stat_ref[stat + 1 : stat + 2, :] * rescale
            done = out / total * ve_ref[:1, part * HALF : (part + 1) * HALF]
            rows_ref[now, part * HALF : (part + 1) * HALF] = done.astype(BF16)
            rows_ref[now, (1 - part) * HALF : (2 - part) * HALF] = oo_ref[now, :]
    out_ref[...] = dot_t(unsorting(), rows_ref[...]).astype(BF16)


def state_kernel(v_ref, steps_ref, rates_ref, valid_ref, into_ref, place_ref, *out_refs):
    full_ref = out_refs[4]
    later = one(iota((ROWS, ROWS), 0) > iota((ROWS, ROWS), 1), BF16)
    rates = jnp.concatenate([rates_ref[...], jnp.zeros((4, ROWS), F32)], axis=0)
    sums = dot(jnp.concatenate(split(rates, 3), axis=0), later)
    to_end = sums[:16] + sums[16:32] + sums[32:]
    steps = jnp.concatenate([steps_ref[...], jnp.zeros((4, ROWS), F32)], axis=0)
    weight = jnp.exp(-to_end) * steps * valid_ref[...].astype(F32)
    width = HEADS_HERE * HEAD_DIM
    spread = one((iota((32, width), 0) & 15) == (iota((32, width), 1) >> 6), BF16)
    scale = t_dot(jnp.concatenate(split(weight, 2), axis=0), spread)
    driven = (v_ref[...].astype(F32) * scale).astype(BF16)
    full_ref[...] = t_dot(driven, into_ref[...])
    decay = jnp.exp(-jnp.sum(rates, axis=1, keepdims=True))
    decay = jnp.concatenate(split(jnp.broadcast_to(decay, (16, STATE)), 2), axis=0)
    row, source = iota((16, 32), 0), iota((16, 32), 1)
    for step in range(4):
        part = place_ref[0] ^ step
        wanted = jnp.where(row < 3, part * 3 + row, jnp.where(row < 6, 13 + part * 3 + row, -1))
        start = pl.multiple_of(part * QUARTER, 64)
        out_refs[step][:QUARTER, :] = full_ref[pl.ds(start, QUARTER), :].astype(BF16)
        out_refs[step][QUARTER:, :] = dot(one(source == wanted, BF16), decay).astype(BF16)


def decay_rows(ref_value):
    tail = ref_value[QUARTER:].astype(F32)
    return [tail[k : k + 1] + tail[k + 3 : k + 4] for k in range(3)]


def spread_rows(decays):
    return jnp.concatenate([jnp.broadcast_to(d, (HEAD_DIM, STATE)) for d in decays], axis=0)


def pack_piece(state, decays):
    high, low = zip(*(split(d, 2) for d in decays))
    tail = jnp.concatenate(
        [d.astype(F32) for d in high + low] + [jnp.zeros((10, STATE), F32)], axis=0
    )
    return jnp.concatenate([state, tail], axis=0).astype(BF16)


def block_kernel(place_ref, a0, a1, a2, a3, total_ref, before_ref, fade_ref, held):
    for step, ref in enumerate((a0, a1, a2, a3)):
        held[place_ref[0] ^ step] = ref[...].astype(F32)
    state = jnp.zeros((QUARTER, STATE), F32)
    decays = [jnp.ones((1, STATE), F32)] * 3
    for at in range(4):
        before_ref[at] = state
        fade_ref[at] = spread_rows(decays)
        now = decay_rows(held[at])
        state = state * spread_rows(now) + held[at, :QUARTER, :]
        decays = [a * b for a, b in zip(decays, now)]
    total_ref[...] = pack_piece(state, decays)


def chain(place, held):
    state = jnp.zeros((QUARTER, STATE), F32)
    decays = [jnp.ones((1, STATE), F32)] * 3
    before, before_decays = state, decays
    for at in range(4):
        here = place == at
        before = jnp.where(here, state, before)
        before_decays = [jnp.where(here, a, b) for a, b in zip(decays, before_decays)]
        now = decay_rows(held[at])
        state = state * spread_rows(now) + held[at, :QUARTER, :]
        decays = [a * b for a, b in zip(decays, now)]
    return before, before_decays, state, decays


def line_kernel(place_ref, a0, a1, a2, a3, total_ref, before_ref, fade_ref, held):
    for step, ref in enumerate((a0, a1, a2, a3)):
        held[(place_ref[1] - step) & 3] = ref[...].astype(F32)
    before, before_decays, state, decays = chain(place_ref[1], held)
    before_ref[...] = before
    fade_ref[...] = spread_rows(before_decays)
    total_ref[...] = pack_piece(state, decays)


def plane_kernel(place_ref, a0, a1, a2, a3, line_before, line_fade, block_before, block_fade, *rest):
    outs, held = rest[:4], rest[4]
    for step, ref in enumerate((a0, a1, a2, a3)):
        held[(place_ref[2] - step) & 3] = ref[...].astype(F32)
    before = chain(place_ref[2], held)[0]
    start = line_fade[...] * before + line_before[...]
    for step in range(4):
        part = place_ref[0] ^ step
        outs[step][...] = (block_fade[part] * start + block_before[part]).astype(BF16)


def within_kernel(
    v_ref, gate_ref, steps_ref, rates_ref, valid_ref, into_ref, read_ref, skip_ref,
    base_ref, lift_ref, couple_ref, col_ref, row_ref,
):
    pair = pl.program_id(0)

    @pl.when(pair == 0)
    def _():
        couple_ref[...] = dot_t(read_ref[...], into_ref[...])
        upto = one(iota((ROWS, ROWS), 0) <= iota((ROWS, ROWS), 1), BF16)
        rates = jnp.concatenate([rates_ref[...], jnp.zeros((4, ROWS), F32)], axis=0)
        sums = dot(jnp.concatenate(split(rates, 3), axis=0), upto)
        fall = -(sums[:16] + sums[16:32] + sums[32:])
        steps = jnp.concatenate([steps_ref[...], jnp.ones((4, ROWS), F32)], axis=0)
        col_ref[...] = fall
        row_ref[...] = jnp.where(valid_ref[...] > 0, fall - jnp.log(steps), -NEG)

    value = v_ref[...]
    lane = iota((ROWS, 128), 1)
    results = []
    falls = []
    tile = 128
    causal = iota((tile, tile), 0) >= iota((tile, tile), 1)
    for part in range(2):
        head = 2 * pair + part
        fall = jnp.broadcast_to(col_ref[pl.ds(head, 1), :], (128, ROWS)).T
        line = row_ref[pl.ds(head, 1), :]
        pieces = []
        for at in range(ROWS // tile):
            fall_now = fall[at * tile : (at + 1) * tile]
            weights = []
            for src in range(at + 1):
                gap = fall_now - line[:, src * tile : (src + 1) * tile]
                if src == at:
                    gap = jnp.where(causal, gap, NEG)
                weights.append(
                    (
                        jnp.exp(gap)
                        * couple_ref[at * tile : (at + 1) * tile, src * tile : (src + 1) * tile]
                    ).astype(BF16)
                )
            pieces.append(dot(jnp.concatenate(weights, axis=1), value[: (at + 1) * tile]))
        results.append(jnp.concatenate(pieces, axis=0))
        falls.append(fall)
    low = lane < HEAD_DIM
    gate = gate_ref[...].astype(F32)
    gate = gate / (1.0 + jnp.exp(-gate))
    skip = jnp.where(low, skip_ref[2 * pair], skip_ref[2 * pair + 1])
    within = jnp.where(low, results[0], results[1])
    base_ref[...] = (within + skip * value.astype(F32)) * gate
    lift_ref[...] = jnp.exp(jnp.where(low, falls[0], falls[1])) * gate


def finish_kernel(place_ref, f0, f1, f2, f3, read_ref, base_ref, lift_ref, gain_ref, out_ref, held):
    @pl.when(pl.program_id(0) == 0)
    def _():
        for step, ref in enumerate((f0, f1, f2, f3)):
            part = place_ref[0] ^ step
            held[pl.ds(pl.multiple_of(part * QUARTER, 64), QUARTER), :] = ref[...]

    together = one((iota((128, 128), 0) >> 6) == (iota((128, 128), 1) >> 6), BF16)
    for pair in range(PAIRS):
        now = slice(pair * 128, (pair + 1) * 128)
        carried = dot_t(read_ref[...], held[now, :])
        gated = base_ref[:, now] + lift_ref[:, now] * carried
        high, low = split(gated * gated, 2)
        mean = (dot(high, together) + dot(low, together)) * (1.0 / HEAD_DIM)
        out_ref[:, now] = (gated * lax.rsqrt(mean + 1e-05) * gain_ref[:, now]).astype(BF16)


def shape(*dims, kind=BF16):
    return jax.ShapeDtypeStruct(dims, kind)


def lanes(rows, row_block=0):
    return pl.BlockSpec((rows, 128), lambda pair: (row_block, pair))


def whole(*dims):
    return pl.BlockSpec(dims, lambda pair: (0,) * len(dims))


def call_pack(key_rows, value_rows, valid):
    return pl.pallas_call(
        pack_kernel,
        out_shape=shape(ROWS + 16, WIDTH),
        in_specs=[VMEM] * 3,
        out_specs=VMEM,
        compiler_params=params(),
        name="pack",
    )(key_rows, value_rows, valid)


def call_state(*args):
    return pl.pallas_call(
        state_kernel,
        out_shape=[shape(PIECE, STATE)] * 4,
        in_specs=[VMEM] * 5 + [SMEM],
        out_specs=[VMEM] * 4,
        scratch_shapes=[pltpu.VMEM((WIDTH, STATE), F32)],
        compiler_params=params(),
        name="state",
    )(*args)


HOLD = [pltpu.VMEM((4, PIECE, STATE), F32)]


def call_block(place, *pieces):
    return pl.pallas_call(
        block_kernel,
        out_shape=[shape(PIECE, STATE), shape(4, QUARTER, STATE, kind=F32), shape(4, QUARTER, STATE, kind=F32)],
        in_specs=[SMEM] + [VMEM] * 4,
        out_specs=[VMEM] * 3,
        scratch_shapes=HOLD,
        compiler_params=params(),
        name="block",
    )(place, *pieces)


def call_line(place, *totals):
    return pl.pallas_call(
        line_kernel,
        out_shape=[shape(PIECE, STATE), shape(QUARTER, STATE, kind=F32), shape(QUARTER, STATE, kind=F32)],
        in_specs=[SMEM] + [VMEM] * 4,
        out_specs=[VMEM] * 3,
        scratch_shapes=HOLD,
        compiler_params=params(),
        name="line",
    )(place, *totals)


def call_plane(place, *args):
    return pl.pallas_call(
        plane_kernel,
        out_shape=[shape(QUARTER, STATE)] * 4,
        in_specs=[SMEM] + [VMEM] * 8,
        out_specs=[VMEM] * 4,
        scratch_shapes=HOLD,
        compiler_params=params(),
        name="plane",
    )(place, *args)


KEPT = [
    shape(WIDTH, HALF),
    shape(HEADS_HERE * 32, HALF),
    shape(WIDTH, HALF, kind=F32),
    shape(8 * PAIRS, HALF, kind=F32),
    shape(WIDTH, HALF),
    shape(8, ROWS, kind=F32),
]


def call_local(*args):
    return pl.pallas_call(
        local_kernel,
        out_shape=KEPT,
        in_specs=[VMEM] * 4 + [SMEM] * 3,
        out_specs=[VMEM] * 6,
        scratch_shapes=[
            pltpu.VMEM((ROWS, ROWS), BF16),
            pltpu.VMEM((WIDTH, ROWS), F32),
            pltpu.VMEM((WIDTH, ROWS), F32),
            pltpu.VMEM((WIDTH, ROWS), BF16),
        ],
        compiler_params=params(24),
        name="local",
    )(*args)


def call_within(*args):
    return pl.pallas_call(
        within_kernel,
        grid=(PAIRS,),
        out_shape=[shape(ROWS, WIDTH, kind=F32)] * 2,
        in_specs=[lanes(ROWS)] * 2
        + [whole(HEADS_HERE, ROWS)] * 2
        + [whole(1, ROWS), whole(ROWS, STATE), whole(ROWS, STATE), SMEM],
        out_specs=[lanes(ROWS)] * 2,
        scratch_shapes=[pltpu.VMEM((ROWS, ROWS), F32), pltpu.VMEM((16, ROWS), F32), pltpu.VMEM((16, ROWS), F32)],
        compiler_params=params(),
        name="within",
    )(*args)


def call_finish(*args):
    def rows(width):
        return pl.BlockSpec((HALF, width), lambda at: (at, 0))

    return pl.pallas_call(
        finish_kernel,
        grid=(ROWS // HALF,),
        out_shape=shape(ROWS, WIDTH),
        in_specs=[SMEM]
        + [whole(QUARTER, STATE)] * 4
        + [rows(STATE), rows(WIDTH), rows(WIDTH), whole(1, WIDTH)],
        out_specs=rows(WIDTH),
        scratch_shapes=[pltpu.VMEM((WIDTH, STATE), BF16)],
        compiler_params=params(),
        name="finish",
    )(*args)


def call_remote(kept, arrived):
    return pl.pallas_call(
        remote_kernel,
        out_shape=shape(ROWS, WIDTH),
        in_specs=[VMEM] * 9,
        out_specs=VMEM,
        scratch_shapes=[pltpu.VMEM((WIDTH, ROWS), BF16)],
        compiler_params=params(24),
        name="remote",
    )(*kept, *arrived)


def per_device(
    query_rows,
    key_rows,
    value_rows,
    patch_valid,
    segment_lengths,
    dilation,
    step_sizes,
    decay_rates,
    state_in,
    state_out,
    gate_in,
    skip_weight,
    norm_gain,
):
    count = lax.axis_size("seq")
    seq_rank = lax.axis_index("seq").astype(jnp.int32)
    rank = jnp.reshape(lax.axis_index("head").astype(jnp.int32), (1,))
    place = jnp.stack([seq_rank & 3, (seq_rank >> 2) & 3, seq_rank >> 4])
    valid = patch_valid.reshape(1, ROWS)
    gain = norm_gain.reshape(1, WIDTH)

    def cross(block, mask):
        return lax.ppermute(block, "seq", [(i, i ^ mask) for i in range(count)])

    def turn(block, step, span):
        unit = span // 4
        route = [(i, i // span * span + (i % span + step * unit) % span) for i in range(count)]
        return lax.ppermute(block, "seq", route)

    after = lax.optimization_barrier

    pieces = call_state(value_rows, step_sizes, decay_rates, valid, state_in, place)
    packed, pieces = after((call_pack(key_rows, value_rows, valid), pieces))
    pieces = [pieces[0]] + [cross(pieces[mask], mask) for mask in range(1, SPAN_DEV)]
    near = cross(packed, 1)
    total, block_before, block_fade = call_block(place, *pieces)
    totals = [total] + [turn(total, step, 16) for step in range(1, 4)]
    packed, totals[1] = after((packed, totals[1]))
    arrived = [near] + [cross(packed, mask) for mask in range(2, SPAN_DEV)]
    base, lift = call_within(
        value_rows, gate_in, step_sizes, decay_rates, after((valid, total))[0], state_in, state_out, skip_weight
    )
    totals, base = after((totals, base))
    total, line_before, line_fade = call_line(place, *totals)
    kept = call_local(
        query_rows, key_rows, value_rows, after((valid, total))[0], segment_lengths, dilation, rank
    )
    totals = [total] + [turn(total, step, 64) for step in range(1, 4)]
    totals, kept = after((totals, kept))
    carried = call_plane(place, *totals, line_before, line_fade, block_before, block_fade)
    carried = [carried[0]] + [cross(carried[mask], mask) for mask in range(1, SPAN_DEV)]
    scanned = call_finish(place, *carried, state_out, base, lift, gain)
    attended = call_remote(kept, arrived)
    return (attended, scanned)


def solution(mesh):
    return jax.shard_map(
        per_device,
        mesh=mesh,
        in_specs=(
            P(("slide", "seq"), "head"),
            P(("slide", "seq"), "head"),
            P(("slide", "seq"), "head"),
            P(("slide", "seq")),
            P(),
            P(),
            P("head", ("slide", "seq")),
            P("head", ("slide", "seq")),
            P(("slide", "seq"), None),
            P(("slide", "seq"), None),
            P(("slide", "seq"), "head"),
            P("head"),
            P("head"),
        ),
        out_specs=(P(("slide", "seq"), "head"), P(("slide", "seq"), "head")),
        check_vma=False,
    )
```

```python
import functools
import math

import jax
import jax.numpy as jnp
import numpy as np
from jax import lax
from jax.experimental import pallas as pl
from jax.experimental.pallas import tpu as pltpu
from jax.sharding import PartitionSpec as P

HEAD_DIM = 64
STATE = 128
HEADS_PER_GROUP = 6
SPAN_DEV = 4
ROWS = 512
HALF = 256
PAIRS = 6
HEADS_HERE = 12
QUARTER = 192
WIDTH = HEADS_HERE * HEAD_DIM
PIECE = 208
NEG = -1e30
F32 = jnp.float32
BF16 = jnp.bfloat16

LN2_HI = float(np.float32(jnp.bfloat16(math.log(2.0))))
LN2_LO = float(np.float32(jnp.bfloat16(math.log(2.0) - LN2_HI)))
LN3_HI = float(np.float32(jnp.bfloat16(math.log(3.0))))
LN3_LO = float(np.float32(jnp.bfloat16(math.log(3.0) - LN3_HI)))

VMEM = pl.BlockSpec(memory_space=pltpu.VMEM)
SMEM = pl.BlockSpec(memory_space=pltpu.SMEM)


def iota(shape, dim):
    return lax.broadcasted_iota(jnp.int32, shape, dim)


def dot(a, b):
    return lax.dot_general(a, b, (((1,), (0,)), ((), ())), preferred_element_type=F32)


def dot_t(a, b):
    return lax.dot_general(a, b, (((1,), (1,)), ((), ())), preferred_element_type=F32)


def t_dot(a, b):
    return lax.dot_general(a, b, (((0,), (0,)), ((), ())), preferred_element_type=F32)


def one(mask, kind=F32):
    return jnp.where(mask, 1.0, 0.0).astype(kind)


def residue_of(block):
    return ((block & 1) << 2) | (block & 2) | (block >> 2)


def sorting():
    row = iota((ROWS, ROWS), 0)
    token = 8 * (row & 63) + residue_of(row >> 6)
    return one(iota((ROWS, ROWS), 1) == token, BF16)


def unsorting():
    column = iota((ROWS, ROWS), 1)
    token = 8 * (column & 63) + residue_of(column >> 6)
    return one(iota((ROWS, ROWS), 0) == token, BF16)


def split(x, parts):
    out = []
    for _ in range(parts):
        head = x.astype(BF16)
        out.append(head)
        x = x - head.astype(F32)
    return out


FREE = pl.CostEstimate(flops=1, bytes_accessed=1, transcendentals=0)


def params(mib=8):
    return pltpu.CompilerParams(vmem_limit_bytes=mib * 1024 * 1024)


def pack_kernel(k_ref, v_ref, valid_ref, out_ref):
    sort = sorting()
    unsort = unsorting()
    low = (iota((HALF, WIDTH), 1) & 127) < HEAD_DIM
    rows = dot(sort, k_ref[...])
    out_ref[:HALF, :] = jnp.where(low, rows[:HALF], rows[HALF:]).astype(BF16)
    columns = t_dot(v_ref[...], unsort)
    even = (iota((WIDTH, HALF), 0) & 127) < HEAD_DIM
    columns = jnp.where(even, columns[:, :HALF], columns[:, HALF:]).astype(BF16)
    for at in range(0, WIDTH, HALF):
        out_ref[HALF:ROWS, at : at + HALF] = columns[at : at + HALF]
    valid = jnp.broadcast_to(valid_ref[...].astype(F32), (16, ROWS)).astype(BF16)
    line = dot_t(valid, sort)
    out_ref[ROWS : ROWS + 16, :] = jnp.concatenate(
        [line, jnp.zeros((16, WIDTH - ROWS), F32)], axis=1
    ).astype(BF16)


def log_count(count):
    high = jnp.where(count == 0, NEG, jnp.where(count == 2, LN2_HI, jnp.where(count == 3, LN3_HI, 0.0)))
    low = jnp.where(count == 2, LN2_LO, jnp.where(count == 3, LN3_LO, 0.0))
    return high, low


def plan_of(head, seg_ref, dil_ref):
    group = head // HEADS_PER_GROUP
    return dil_ref[group, 1], dil_ref[group, 2], seg_ref[group, 0], seg_ref[group, 1]


def local_plan(head, seg_ref, dil_ref):
    r1, r2, w0, w1 = plan_of(head, seg_ref, dil_ref)
    key, query = iota((16, ROWS), 0), iota((16, ROWS), 1) >> 5
    same = (key & 1) == (query & 1)
    key_off, query_off = residue_of(key >> 1) - head, residue_of(query >> 1) - head

    def on(stride):
        return (key_off & (stride - 1)) + (query_off & (stride - 1)) == 0

    count = one(same | (w0 >= ROWS)) + one(on(r1) & (same | (w1 >= ROWS))) + one(on(r2))
    return jnp.concatenate([*log_count(count), jnp.ones((16, ROWS), F32)], axis=0)


def remote_plan(head, seg_ref, dil_ref):
    r1, r2, _, w1 = plan_of(head, seg_ref, dil_ref)
    row = iota((8, HALF), 0)
    shift = (head & 1) - head
    key_off = residue_of(row & 3) + shift
    query_off = residue_of(iota((8, HALF), 1) >> 6) + shift

    def on(stride):
        return (key_off & (stride - 1)) + (query_off & (stride - 1)) == 0

    parts = []
    for reach in (2 * ROWS, 4 * ROWS):
        high, low = log_count(one(on(r1) & (w1 >= reach)) + one(on(r2)))
        parts.append(jnp.where(row < 4, high, low))
    return jnp.concatenate(parts + [jnp.ones((16, HALF), F32)], axis=0)


def own_bias(head, dil_ref):
    group = head // HEADS_PER_GROUP
    off = residue_of(iota((1, ROWS), 1) >> 6) - head
    count = 1 + jnp.where((off & (dil_ref[group, 1] - 1)) == 0, 1, 0)
    count = count + jnp.where((off & (dil_ref[group, 2] - 1)) == 0, 1, 0)
    return jnp.where(count == 1, 0.0, jnp.where(count == 2, LN2_HI + LN2_LO, LN3_HI + LN3_LO))


def softmax_columns(keys, queries, values, own, before):
    scores = dot(keys, queries)
    if own is not None:
        tile = 128
        diagonal = iota((tile, tile), 0) == iota((tile, tile), 1)
        rows = []
        for at in range(0, scores.shape[0], tile):
            line = scores[at : at + tile]
            here = jnp.where(diagonal, own[:, at : at + tile], line[:, at : at + tile])
            parts = [line[:, :at], here, line[:, at + tile :]]
            rows.append(jnp.concatenate([x for x in parts if x.shape[1]], axis=1))
        scores = jnp.concatenate(rows, axis=0)
    top = jnp.max(scores, axis=0, keepdims=True)
    if before is not None:
        top = jnp.maximum(top, before)
    values = jnp.concatenate([values, jnp.ones((16, values.shape[1]), BF16)], axis=0)
    out = dot(values, jnp.exp(scores - top).astype(BF16))
    return out[:HEAD_DIM], out[HEAD_DIM : HEAD_DIM + 1], top


def all_queries(rows, part, plan):
    blank = jnp.zeros((HEAD_DIM, rows.shape[1]), BF16)
    pieces = [rows, blank] if part == 0 else [blank, rows]
    rest = jnp.zeros((128 - plan.shape[0], rows.shape[1]), BF16)
    return jnp.concatenate(pieces + [plan.astype(BF16), rest], axis=0)


def local_kernel(
    q_ref, k_ref, v_ref, valid_ref, seg_ref, dil_ref, rank_ref,
    qe_ref, plan_ref, oe_ref, stat_ref, oo_ref, ve_ref,
    unsort_ref, sq_ref, sk_ref, sv_ref,
):
    unsort_ref[...] = unsorting()
    valid = jnp.broadcast_to(valid_ref[...].astype(F32), (128, ROWS)).astype(BF16)
    flags = dot(valid, unsort_ref[...])
    ve_ref[...] = flags[:8]
    row, lane = iota((ROWS, 128), 0), iota((ROWS, 128), 1)
    key_side = one(((row >> 5) == (lane & 15)) & (lane < 32))
    key_side = jnp.where(lane == 32, (1.0 - flags.T) * NEG, key_side).astype(BF16)
    sq_ref[...] = t_dot(q_ref[...], unsort_ref[...]) * (HEAD_DIM**-0.5)
    sk_ref[...] = t_dot(k_ref[...], unsort_ref[...])
    sv_ref[...] = t_dot(v_ref[...], unsort_ref[...]).astype(BF16)
    for pair in range(PAIRS):
        both = slice(pair * 128, (pair + 1) * 128)
        key = sk_ref[both, :].T.astype(BF16)
        keys = jnp.concatenate([key, key_side], axis=1)
        stats = []
        for part in range(2):
            head = rank_ref[0] * HEADS_HERE + 2 * pair + part
            start = pair * 128 + part * HEAD_DIM
            now = slice(start, start + HEAD_DIM)
            query = sq_ref[now, :]
            queries = all_queries(query.astype(BF16), part, local_plan(head, seg_ref, dil_ref))
            own = jnp.sum(query * sk_ref[now, :], axis=0, keepdims=True) + own_bias(head, dil_ref)
            out, total, top = softmax_columns(keys, queries, sv_ref[now, :], own, None)
            inside = slice(part * HALF, (part + 1) * HALF)
            outside = slice((1 - part) * HALF, (2 - part) * HALF)
            qe_ref[now, :] = query[:, inside].astype(BF16)
            oe_ref[now, :] = out[:, inside]
            oo_ref[now, :] = (out[:, outside] / total[:, outside] * flags[:1, outside]).astype(BF16)
            stats += [top[:, inside], total[:, inside]]
            at = (2 * pair + part) * 32
            plan_ref[at : at + 32, :] = remote_plan(head, seg_ref, dil_ref).astype(BF16)
        stat_ref[pair * 8 : pair * 8 + 8, :] = jnp.concatenate(stats + [jnp.zeros((4, HALF), F32)], axis=0)


def remote_kernel(near, qe_ref, plan_ref, oe_ref, stat_ref, oo_ref, ve_ref, *rest):
    blocks, outs = (rest[:1], rest[1:]) if near else (rest[:2], rest[2:])
    spread = one((iota((16, 128), 0) == 0) & (iota((16, 128), 1) == 16), BF16)
    row, lane = iota((HALF, 128), 0), iota((HALF, 128), 1)
    wanted = ((lane & 3) == (row >> 6)) & (lane < 16)
    wanted = one(wanted & (lane < 8) if near else wanted & (lane >= 8))
    sides = []
    for parity in range(2):
        pieces = []
        for ref in blocks:
            flags = ref[ROWS : ROWS + 16, parity * HALF : (parity + 1) * HALF].astype(F32)
            pieces.append(t_dot(((1.0 - flags) * NEG).astype(BF16), spread) + wanted)
        sides.append(jnp.concatenate(pieces, axis=0).astype(BF16))
    for pair in range(PAIRS):
        both = slice(pair * 128, (pair + 1) * 128)
        place = slice(HALF + (pair & 1) * 128, HALF + (pair & 1) * 128 + 128)
        chunk = slice((pair >> 1) * HALF, (pair >> 1) * HALF + HALF)
        key = jnp.concatenate([ref[:HALF, both] for ref in blocks], axis=0)
        value = jnp.concatenate([ref[place, chunk] for ref in blocks], axis=1)
        stats = []
        for part in range(2):
            start = pair * 128 + part * HEAD_DIM
            now = slice(start, start + HEAD_DIM)
            at = (2 * pair + part) * 32
            keys = jnp.concatenate([key, sides[part]], axis=1)
            queries = all_queries(qe_ref[now, :], part, plan_ref[at : at + 32, :])
            stat = pair * 8 + 2 * part
            before = stat_ref[stat : stat + 1, :]
            out, total, top = softmax_columns(
                keys, queries, value[part * HEAD_DIM : (part + 1) * HEAD_DIM], None, before
            )
            rescale = jnp.exp(before - top)
            out = out + oe_ref[now, :] * rescale
            total = total + stat_ref[stat + 1 : stat + 2, :] * rescale
            if near:
                outs[0][now, :] = out
                stats += [top, total]
                continue
            done = out / total * ve_ref[:1, part * HALF : (part + 1) * HALF]
            outs[1][now, part * HALF : (part + 1) * HALF] = done.astype(BF16)
            outs[1][now, (1 - part) * HALF : (2 - part) * HALF] = oo_ref[now, :]
        if near:
            outs[1][pair * 8 : pair * 8 + 8, :] = jnp.concatenate(
                stats + [jnp.zeros((4, HALF), F32)], axis=0
            )
    if not near:
        outs[0][...] = dot_t(unsorting(), outs[1][...]).astype(BF16)


def state_kernel(v_hbm, steps_hbm, rates_hbm, valid_hbm, into_hbm, place_ref, *rest):
    out_refs = rest[:4]
    full_ref, v_ref, steps_ref, rates_ref, valid_ref, into_ref, arrived = rest[4:]
    copies = [
        pltpu.make_async_copy(source, target, arrived.at[at])
        for at, (source, target) in enumerate(
            (
                (rates_hbm, rates_ref),
                (steps_hbm, steps_ref),
                (valid_hbm, valid_ref),
                (into_hbm, into_ref),
                (v_hbm, v_ref),
            )
        )
    ]
    for copy in copies:
        copy.start()
    for copy in copies[:3]:
        copy.wait()
    later = one(iota((ROWS, ROWS), 0) > iota((ROWS, ROWS), 1), BF16)
    rates = jnp.concatenate([rates_ref[...], jnp.zeros((4, ROWS), F32)], axis=0)
    sums = dot(jnp.concatenate(split(rates, 3), axis=0), later)
    to_end = sums[:16] + sums[16:32] + sums[32:]
    steps = jnp.concatenate([steps_ref[...], jnp.zeros((4, ROWS), F32)], axis=0)
    weight = jnp.exp(-to_end) * steps * valid_ref[...].astype(F32)
    width = HEADS_HERE * HEAD_DIM
    spread = one((iota((32, width), 0) & 15) == (iota((32, width), 1) >> 6), BF16)
    scale = t_dot(jnp.concatenate(split(weight, 2), axis=0), spread)
    for copy in copies[3:]:
        copy.wait()
    driven = (v_ref[...].astype(F32) * scale).astype(BF16)
    full_ref[...] = t_dot(driven, into_ref[...])
    decay = jnp.exp(-jnp.sum(rates, axis=1, keepdims=True))
    decay = jnp.concatenate(split(jnp.broadcast_to(decay, (16, STATE)), 2), axis=0)
    row, source = iota((16, 32), 0), iota((16, 32), 1)
    for step in range(4):
        part = place_ref[0] ^ step
        wanted = jnp.where(row < 3, part * 3 + row, jnp.where(row < 6, 13 + part * 3 + row, -1))
        start = pl.multiple_of(part * QUARTER, 64)
        out_refs[step][:QUARTER, :] = full_ref[pl.ds(start, QUARTER), :].astype(BF16)
        out_refs[step][QUARTER:, :] = dot(one(source == wanted, BF16), decay).astype(BF16)


def decay_rows(ref_value):
    tail = ref_value[QUARTER:].astype(F32)
    return [tail[k : k + 1] + tail[k + 3 : k + 4] for k in range(3)]


def tall(decays):
    return jnp.concatenate(decays + [jnp.zeros((5, STATE), F32)], axis=0)


def spread_rows(decays):
    return jnp.concatenate([jnp.broadcast_to(d, (HEAD_DIM, STATE)) for d in decays], axis=0)


def pack_piece(state, decays):
    high, low = zip(*(split(d, 2) for d in decays))
    tail = jnp.concatenate(
        [d.astype(F32) for d in high + low] + [jnp.zeros((10, STATE), F32)], axis=0
    )
    return jnp.concatenate([state, tail], axis=0).astype(BF16)


def block_kernel(place_ref, a0, a1, a2, a3, total_ref, before_ref, fade_ref, held):
    for step, ref in enumerate((a0, a1, a2, a3)):
        held[place_ref[0] ^ step] = ref[...].astype(F32)
    state = jnp.zeros((QUARTER, STATE), F32)
    decays = [jnp.ones((1, STATE), F32)] * 3
    for at in range(4):
        before_ref[at] = state
        fade_ref[at] = tall(decays)
        now = decay_rows(held[at])
        state = state * spread_rows(now) + held[at, :QUARTER, :]
        decays = [a * b for a, b in zip(decays, now)]
    total_ref[...] = pack_piece(state, decays)


def chain(place, held):
    state = jnp.zeros((QUARTER, STATE), F32)
    decays = [jnp.ones((1, STATE), F32)] * 3
    before, before_decays = state, decays
    for at in range(4):
        here = place == at
        before = jnp.where(here, state, before)
        before_decays = [jnp.where(here, a, b) for a, b in zip(decays, before_decays)]
        now = decay_rows(held[at])
        state = state * spread_rows(now) + held[at, :QUARTER, :]
        decays = [a * b for a, b in zip(decays, now)]
    return before, before_decays, state, decays


def line_kernel(place_ref, a0, a1, a2, a3, total_ref, before_ref, fade_ref, held):
    for step, ref in enumerate((a0, a1, a2, a3)):
        held[(place_ref[1] - step) & 3] = ref[...].astype(F32)
    before, before_decays, state, decays = chain(place_ref[1], held)
    before_ref[...] = before
    fade_ref[...] = tall(before_decays)
    total_ref[...] = pack_piece(state, decays)


def plane_kernel(place_ref, a0, a1, a2, a3, line_before, line_fade, block_before, block_fade, *rest):
    outs, held = rest[:4], rest[4]
    for step, ref in enumerate((a0, a1, a2, a3)):
        held[(place_ref[2] - step) & 3] = ref[...].astype(F32)
    before = chain(place_ref[2], held)[0]
    start = spread_rows([line_fade[k : k + 1, :] for k in range(3)]) * before + line_before[...]
    for step in range(4):
        part = place_ref[0] ^ step
        fade = block_fade[part]
        fade = spread_rows([fade[k : k + 1] for k in range(3)])
        outs[step][...] = (fade * start + block_before[part]).astype(BF16)


def within_kernel(
    first,
    v_ref, gate_ref, steps_ref, rates_ref, valid_ref, into_ref, read_ref, skip_ref,
    base_ref, lift_ref, couple_ref, col_ref, row_ref,
):
    pair = pl.program_id(0) + first

    @pl.when(pl.program_id(0) == 0)
    def _():
        couple_ref[...] = dot_t(read_ref[...], into_ref[...])
        upto = one(iota((ROWS, ROWS), 0) <= iota((ROWS, ROWS), 1), BF16)
        rates = jnp.concatenate([rates_ref[...], jnp.zeros((4, ROWS), F32)], axis=0)
        sums = dot(jnp.concatenate(split(rates, 3), axis=0), upto)
        fall = -(sums[:16] + sums[16:32] + sums[32:])
        steps = jnp.concatenate([steps_ref[...], jnp.ones((4, ROWS), F32)], axis=0)
        col_ref[...] = fall
        row_ref[...] = jnp.where(valid_ref[...] > 0, fall - jnp.log(steps), -NEG)

    value = v_ref[...]
    lane = iota((ROWS, 128), 1)
    results = []
    falls = []
    tile = 128
    causal = iota((tile, tile), 0) >= iota((tile, tile), 1)
    for part in range(2):
        head = 2 * pair + part
        fall = jnp.broadcast_to(col_ref[pl.ds(head, 1), :], (128, ROWS)).T
        line = row_ref[pl.ds(head, 1), :]
        pieces = []
        for at in range(ROWS // tile):
            fall_now = fall[at * tile : (at + 1) * tile]
            weights = []
            for src in range(at + 1):
                gap = fall_now - line[:, src * tile : (src + 1) * tile]
                if src == at:
                    gap = jnp.where(causal, gap, NEG)
                weights.append(
                    (
                        jnp.exp(gap)
                        * couple_ref[at * tile : (at + 1) * tile, src * tile : (src + 1) * tile]
                    ).astype(BF16)
                )
            pieces.append(dot(jnp.concatenate(weights, axis=1), value[: (at + 1) * tile]))
        results.append(jnp.concatenate(pieces, axis=0))
        falls.append(fall)
    low = lane < HEAD_DIM
    gate = gate_ref[...].astype(F32)
    gate = gate / (1.0 + jnp.exp(-gate))
    skip = jnp.where(low, skip_ref[2 * pair], skip_ref[2 * pair + 1])
    within = jnp.where(low, results[0], results[1])
    base_ref[...] = ((within + skip * value.astype(F32)) * gate).astype(BF16)
    lift_ref[...] = (jnp.exp(jnp.where(low, falls[0], falls[1])) * gate).astype(BF16)


def finish_kernel(place_ref, f0, f1, f2, f3, read_ref, *rest):
    gain_ref, out_ref, held = rest[4:]

    @pl.when(pl.program_id(0) == 0)
    def _():
        for step, ref in enumerate((f0, f1, f2, f3)):
            part = place_ref[0] ^ step
            held[pl.ds(pl.multiple_of(part * QUARTER, 64), QUARTER), :] = ref[...]

    together = one((iota((128, 128), 0) >> 6) == (iota((128, 128), 1) >> 6), BF16)
    for pair in range(PAIRS):
        now = slice(pair * 128, (pair + 1) * 128)
        half = slice(pair % 3 * 128, (pair % 3 + 1) * 128)
        base_ref, lift_ref = rest[pair // 3 * 2 : pair // 3 * 2 + 2]
        carried = dot_t(read_ref[...], held[now, :])
        gated = base_ref[:, half].astype(F32) + lift_ref[:, half].astype(F32) * carried
        high, low = split(gated * gated, 2)
        mean = (dot(high, together) + dot(low, together)) * (1.0 / HEAD_DIM)
        out_ref[:, now] = (gated * lax.rsqrt(mean + 1e-05) * gain_ref[:, now]).astype(BF16)


def shape(*dims, kind=BF16):
    return jax.ShapeDtypeStruct(dims, kind)


def lanes(rows, row_block=0):
    return pl.BlockSpec((rows, 128), lambda pair: (row_block, pair))


def whole(*dims):
    return pl.BlockSpec(dims, lambda pair: (0,) * len(dims))


def call_pack(key_rows, value_rows, valid):
    return pl.pallas_call(
        pack_kernel,
        out_shape=shape(ROWS + 16, WIDTH),
        in_specs=[VMEM] * 3,
        out_specs=VMEM,
        cost_estimate=FREE,
        compiler_params=params(),
        name="pack",
    )(key_rows, value_rows, valid)


def call_state(*args):
    far = pl.BlockSpec(memory_space=pltpu.HBM)
    return pl.pallas_call(
        state_kernel,
        out_shape=[shape(PIECE, STATE)] * 4,
        in_specs=[far] * 5 + [SMEM],
        out_specs=[VMEM] * 4,
        scratch_shapes=[
            pltpu.VMEM((WIDTH, STATE), F32),
            pltpu.VMEM((ROWS, WIDTH), BF16),
            pltpu.VMEM((HEADS_HERE, ROWS), F32),
            pltpu.VMEM((HEADS_HERE, ROWS), F32),
            pltpu.VMEM((1, ROWS), jnp.int32),
            pltpu.VMEM((ROWS, STATE), BF16),
            pltpu.SemaphoreType.DMA((5,)),
        ],
        cost_estimate=FREE,
        compiler_params=params(),
        name="state",
    )(*args)


HOLD = [pltpu.VMEM((4, PIECE, STATE), F32)]


def call_block(place, *pieces):
    return pl.pallas_call(
        block_kernel,
        out_shape=[shape(PIECE, STATE), shape(4, QUARTER, STATE, kind=F32), shape(4, 8, STATE, kind=F32)],
        in_specs=[SMEM] + [VMEM] * 4,
        out_specs=[VMEM] * 3,
        scratch_shapes=HOLD,
        cost_estimate=FREE,
        compiler_params=params(),
        name="block",
    )(place, *pieces)


def call_line(place, *totals):
    return pl.pallas_call(
        line_kernel,
        out_shape=[shape(PIECE, STATE), shape(QUARTER, STATE, kind=F32), shape(8, STATE, kind=F32)],
        in_specs=[SMEM] + [VMEM] * 4,
        out_specs=[VMEM] * 3,
        scratch_shapes=HOLD,
        cost_estimate=FREE,
        compiler_params=params(),
        name="line",
    )(place, *totals)


def call_plane(place, *args):
    return pl.pallas_call(
        plane_kernel,
        out_shape=[shape(QUARTER, STATE)] * 4,
        in_specs=[SMEM] + [VMEM] * 8,
        out_specs=[VMEM] * 4,
        scratch_shapes=HOLD,
        cost_estimate=FREE,
        compiler_params=params(),
        name="plane",
    )(place, *args)


KEPT = [
    shape(WIDTH, HALF),
    shape(HEADS_HERE * 32, HALF),
    shape(WIDTH, HALF, kind=F32),
    shape(8 * PAIRS, HALF, kind=F32),
    shape(WIDTH, HALF),
    shape(8, ROWS, kind=F32),
]


def call_local(*args):
    return pl.pallas_call(
        local_kernel,
        out_shape=KEPT,
        in_specs=[VMEM] * 4 + [SMEM] * 3,
        out_specs=[VMEM] * 6,
        scratch_shapes=[
            pltpu.VMEM((ROWS, ROWS), BF16),
            pltpu.VMEM((WIDTH, ROWS), F32),
            pltpu.VMEM((WIDTH, ROWS), F32),
            pltpu.VMEM((WIDTH, ROWS), BF16),
        ],
        cost_estimate=FREE,
        compiler_params=params(14),
        name="local",
    )(*args)


def call_within(first, *args):
    def columns(rows):
        return pl.BlockSpec((rows, 128), lambda pair: (0, first + pair))

    return pl.pallas_call(
        functools.partial(within_kernel, first),
        grid=(PAIRS // 2,),
        out_shape=[shape(ROWS, WIDTH // 2)] * 2,
        in_specs=[columns(ROWS)] * 2
        + [whole(HEADS_HERE, ROWS)] * 2
        + [whole(1, ROWS), whole(ROWS, STATE), whole(ROWS, STATE), SMEM],
        out_specs=[lanes(ROWS)] * 2,
        scratch_shapes=[pltpu.VMEM((ROWS, ROWS), F32), pltpu.VMEM((16, ROWS), F32), pltpu.VMEM((16, ROWS), F32)],
        cost_estimate=FREE,
        compiler_params=params(8),
        name="within",
    )(*args)


def call_finish(*args):
    def rows(width):
        return pl.BlockSpec((HALF, width), lambda at: (at, 0))

    return pl.pallas_call(
        finish_kernel,
        grid=(ROWS // HALF,),
        out_shape=shape(ROWS, WIDTH),
        in_specs=[SMEM]
        + [whole(QUARTER, STATE)] * 4
        + [rows(STATE)]
        + [rows(WIDTH // 2)] * 4
        + [whole(1, WIDTH)],
        out_specs=rows(WIDTH),
        scratch_shapes=[pltpu.VMEM((WIDTH, STATE), BF16)],
        cost_estimate=FREE,
        compiler_params=params(),
        name="finish",
    )(*args)


def call_near(kept, arrived):
    out, stat = pl.pallas_call(
        functools.partial(remote_kernel, True),
        out_shape=[KEPT[2], KEPT[3]],
        in_specs=[VMEM] * 7,
        out_specs=[VMEM] * 2,
        cost_estimate=FREE,
        compiler_params=params(14),
        name="near",
    )(*kept, arrived)
    return [kept[0], kept[1], out, stat, kept[4], kept[5]]


def call_remote(kept, arrived):
    return pl.pallas_call(
        functools.partial(remote_kernel, False),
        out_shape=shape(ROWS, WIDTH),
        in_specs=[VMEM] * 8,
        out_specs=VMEM,
        scratch_shapes=[pltpu.VMEM((WIDTH, ROWS), BF16)],
        cost_estimate=FREE,
        compiler_params=params(14),
        name="remote",
    )(*kept, *arrived)


def per_device(
    query_rows,
    key_rows,
    value_rows,
    patch_valid,
    segment_lengths,
    dilation,
    step_sizes,
    decay_rates,
    state_in,
    state_out,
    gate_in,
    skip_weight,
    norm_gain,
):
    count = lax.axis_size("seq")
    seq_rank = lax.axis_index("seq").astype(jnp.int32)
    rank = jnp.reshape(lax.axis_index("head").astype(jnp.int32), (1,))
    place = jnp.stack([seq_rank & 3, (seq_rank >> 2) & 3, seq_rank >> 4])
    valid = patch_valid.reshape(1, ROWS)
    gain = norm_gain.reshape(1, WIDTH)

    def cross(block, mask):
        return lax.ppermute(block, "seq", [(i, i ^ mask) for i in range(count)])

    def turn(block, step, span):
        unit = span // 4
        route = [(i, i // span * span + (i % span + step * unit) % span) for i in range(count)]
        return lax.ppermute(block, "seq", route)

    after = lax.optimization_barrier
    scan_inputs = (step_sizes, decay_rates, valid, state_in)

    pieces = call_state(value_rows, *scan_inputs, place)
    packed = call_pack(key_rows, value_rows, after((valid, pieces))[0])
    pieces = [pieces[0]] + [cross(pieces[mask], mask) for mask in range(1, SPAN_DEV)]
    near = cross(packed, 1)
    pieces = after((pieces, packed))[0]
    total, block_before, block_fade = call_block(place, *pieces)
    totals = [total] + [turn(total, step, 16) for step in range(1, 4)]
    halves = list(scan_inputs)
    halves[2] = after((valid, total))[0]
    first = call_within(0, value_rows, gate_in, *halves, state_out, skip_weight)
    totals = after((totals, first))[0]
    packed, totals = after((packed, totals))
    arrived = [cross(packed, mask) for mask in range(2, SPAN_DEV)]
    total, line_before, line_fade = call_line(place, *totals)
    kept = call_local(
        query_rows, key_rows, value_rows, after((valid, total))[0], segment_lengths, dilation, rank
    )
    totals = [total] + [turn(total, step, 64) for step in range(1, 4)]
    totals = after((totals, kept))[0]
    carried = call_plane(place, *totals, line_before, line_fade, block_before, block_fade)
    halves[2] = after((valid, carried))[0]
    second = call_within(3, value_rows, gate_in, *halves, state_out, skip_weight)
    carried = [carried[0]] + [cross(carried[mask], mask) for mask in range(1, SPAN_DEV)]
    kept = call_near(after((kept, second))[0], near)
    carried = after((carried, kept))[0]
    scanned = call_finish(place, *carried, state_out, *first, *second, gain)
    attended = call_remote(kept, arrived)
    return (attended, scanned)


def solution(mesh):
    return jax.shard_map(
        per_device,
        mesh=mesh,
        in_specs=(
            P(("slide", "seq"), "head"),
            P(("slide", "seq"), "head"),
            P(("slide", "seq"), "head"),
            P(("slide", "seq")),
            P(),
            P(),
            P("head", ("slide", "seq")),
            P("head", ("slide", "seq")),
            P(("slide", "seq"), None),
            P(("slide", "seq"), None),
            P(("slide", "seq"), "head"),
            P("head"),
            P("head"),
        ),
        out_specs=(P(("slide", "seq"), "head"), P(("slide", "seq"), "head")),
        check_vma=False,
    )
```

```python
import functools
import math

import jax
import jax.numpy as jnp
import numpy as np
from jax import lax
from jax.experimental import pallas as pl
from jax.experimental.pallas import tpu as pltpu
from jax.sharding import PartitionSpec as P

HEAD_DIM = 64
STATE = 128
HEADS_PER_GROUP = 6
SPAN_DEV = 4
ROWS = 512
HALF = 256
PAIRS = 6
HEADS_HERE = 12
QUARTER = 192
WIDTH = HEADS_HERE * HEAD_DIM
PIECE = 208
NEG = -1e30
F32 = jnp.float32
BF16 = jnp.bfloat16

LN2_HI = float(np.float32(jnp.bfloat16(math.log(2.0))))
LN2_LO = float(np.float32(jnp.bfloat16(math.log(2.0) - LN2_HI)))
LN3_HI = float(np.float32(jnp.bfloat16(math.log(3.0))))
LN3_LO = float(np.float32(jnp.bfloat16(math.log(3.0) - LN3_HI)))

VMEM = pl.BlockSpec(memory_space=pltpu.VMEM)
SMEM = pl.BlockSpec(memory_space=pltpu.SMEM)


def iota(shape, dim):
    return lax.broadcasted_iota(jnp.int32, shape, dim)


def dot(a, b):
    return lax.dot_general(a, b, (((1,), (0,)), ((), ())), preferred_element_type=F32)


def dot_t(a, b):
    return lax.dot_general(a, b, (((1,), (1,)), ((), ())), preferred_element_type=F32)


def t_dot(a, b):
    return lax.dot_general(a, b, (((0,), (0,)), ((), ())), preferred_element_type=F32)


def one(mask, kind=F32):
    return jnp.where(mask, 1.0, 0.0).astype(kind)


def residue_of(block):
    return ((block & 1) << 2) | (block & 2) | (block >> 2)


def sorting():
    row = iota((ROWS, ROWS), 0)
    token = 8 * (row & 63) + residue_of(row >> 6)
    return one(iota((ROWS, ROWS), 1) == token, BF16)


def unsorting():
    column = iota((ROWS, ROWS), 1)
    token = 8 * (column & 63) + residue_of(column >> 6)
    return one(iota((ROWS, ROWS), 0) == token, BF16)


def split(x, parts):
    out = []
    for _ in range(parts):
        head = x.astype(BF16)
        out.append(head)
        x = x - head.astype(F32)
    return out


FREE = pl.CostEstimate(flops=1, bytes_accessed=1, transcendentals=0)


def params(mib=8):
    return pltpu.CompilerParams(vmem_limit_bytes=mib * 1024 * 1024)


def pack_kernel(k_ref, v_ref, valid_ref, out_ref):
    sort = sorting()
    unsort = unsorting()
    low = (iota((HALF, WIDTH), 1) & 127) < HEAD_DIM
    rows = dot(sort, k_ref[...])
    out_ref[:HALF, :] = jnp.where(low, rows[:HALF], rows[HALF:]).astype(BF16)
    columns = t_dot(v_ref[...], unsort)
    even = (iota((WIDTH, HALF), 0) & 127) < HEAD_DIM
    columns = jnp.where(even, columns[:, :HALF], columns[:, HALF:]).astype(BF16)
    for at in range(0, WIDTH, HALF):
        out_ref[HALF:ROWS, at : at + HALF] = columns[at : at + HALF]
    valid = jnp.broadcast_to(valid_ref[...].astype(F32), (16, ROWS)).astype(BF16)
    line = dot_t(valid, sort)
    out_ref[ROWS : ROWS + 16, :] = jnp.concatenate(
        [line, jnp.zeros((16, WIDTH - ROWS), F32)], axis=1
    ).astype(BF16)


def log_count(count):
    high = jnp.where(count == 0, NEG, jnp.where(count == 2, LN2_HI, jnp.where(count == 3, LN3_HI, 0.0)))
    low = jnp.where(count == 2, LN2_LO, jnp.where(count == 3, LN3_LO, 0.0))
    return high, low


def plan_of(head, seg_ref, dil_ref):
    group = head // HEADS_PER_GROUP
    return dil_ref[group, 1], dil_ref[group, 2], seg_ref[group, 0], seg_ref[group, 1]


def local_plan(head, seg_ref, dil_ref):
    r1, r2, w0, w1 = plan_of(head, seg_ref, dil_ref)
    key, query = iota((16, ROWS), 0), iota((16, ROWS), 1) >> 5
    same = (key & 1) == (query & 1)
    key_off, query_off = residue_of(key >> 1) - head, residue_of(query >> 1) - head

    def on(stride):
        return (key_off & (stride - 1)) + (query_off & (stride - 1)) == 0

    count = one(same | (w0 >= ROWS)) + one(on(r1) & (same | (w1 >= ROWS))) + one(on(r2))
    return jnp.concatenate([*log_count(count), jnp.ones((16, ROWS), F32)], axis=0)


def remote_plan(head, seg_ref, dil_ref):
    r1, r2, _, w1 = plan_of(head, seg_ref, dil_ref)
    row = iota((8, HALF), 0)
    shift = (head & 1) - head
    key_off = residue_of(row & 3) + shift
    query_off = residue_of(iota((8, HALF), 1) >> 6) + shift

    def on(stride):
        return (key_off & (stride - 1)) + (query_off & (stride - 1)) == 0

    parts = []
    for reach in (2 * ROWS, 4 * ROWS):
        high, low = log_count(one(on(r1) & (w1 >= reach)) + one(on(r2)))
        parts.append(jnp.where(row < 4, high, low))
    return jnp.concatenate(parts + [jnp.ones((16, HALF), F32)], axis=0)


def own_bias(head, dil_ref):
    group = head // HEADS_PER_GROUP
    off = residue_of(iota((1, ROWS), 1) >> 6) - head
    count = 1 + jnp.where((off & (dil_ref[group, 1] - 1)) == 0, 1, 0)
    count = count + jnp.where((off & (dil_ref[group, 2] - 1)) == 0, 1, 0)
    return jnp.where(count == 1, 0.0, jnp.where(count == 2, LN2_HI + LN2_LO, LN3_HI + LN3_LO))


def softmax_columns(keys, queries, values, own, before):
    scores = dot(keys, queries)
    if own is not None:
        tile = 128
        diagonal = iota((tile, tile), 0) == iota((tile, tile), 1)
        rows = []
        for at in range(0, scores.shape[0], tile):
            line = scores[at : at + tile]
            here = jnp.where(diagonal, own[:, at : at + tile], line[:, at : at + tile])
            parts = [line[:, :at], here, line[:, at + tile :]]
            rows.append(jnp.concatenate([x for x in parts if x.shape[1]], axis=1))
        scores = jnp.concatenate(rows, axis=0)
    top = jnp.max(scores, axis=0, keepdims=True)
    if before is not None:
        top = jnp.maximum(top, before)
    values = jnp.concatenate([values, jnp.ones((16, values.shape[1]), BF16)], axis=0)
    out = dot(values, jnp.exp(scores - top).astype(BF16))
    return out[:HEAD_DIM], out[HEAD_DIM : HEAD_DIM + 1], top


def all_queries(rows, part, plan):
    blank = jnp.zeros((HEAD_DIM, rows.shape[1]), BF16)
    pieces = [rows, blank] if part == 0 else [blank, rows]
    rest = jnp.zeros((128 - plan.shape[0], rows.shape[1]), BF16)
    return jnp.concatenate(pieces + [plan.astype(BF16), rest], axis=0)


def local_kernel(
    q_ref, k_ref, v_ref, valid_ref, seg_ref, dil_ref, rank_ref,
    qe_ref, plan_ref, oe_ref, stat_ref, oo_ref, ve_ref,
    unsort_ref, sq_ref, sk_ref, sv_ref,
):
    unsort_ref[...] = unsorting()
    valid = jnp.broadcast_to(valid_ref[...].astype(F32), (128, ROWS)).astype(BF16)
    flags = dot(valid, unsort_ref[...])
    ve_ref[...] = flags[:8]
    row, lane = iota((ROWS, 128), 0), iota((ROWS, 128), 1)
    key_side = one(((row >> 5) == (lane & 15)) & (lane < 32))
    key_side = jnp.where(lane == 32, (1.0 - flags.T) * NEG, key_side).astype(BF16)
    sq_ref[...] = t_dot(q_ref[...], unsort_ref[...]) * (HEAD_DIM**-0.5)
    sk_ref[...] = t_dot(k_ref[...], unsort_ref[...])
    sv_ref[...] = t_dot(v_ref[...], unsort_ref[...]).astype(BF16)
    for pair in range(PAIRS):
        both = slice(pair * 128, (pair + 1) * 128)
        key = sk_ref[both, :].T.astype(BF16)
        keys = jnp.concatenate([key, key_side], axis=1)
        stats = []
        for part in range(2):
            head = rank_ref[0] * HEADS_HERE + 2 * pair + part
            start = pair * 128 + part * HEAD_DIM
            now = slice(start, start + HEAD_DIM)
            query = sq_ref[now, :]
            queries = all_queries(query.astype(BF16), part, local_plan(head, seg_ref, dil_ref))
            own = jnp.sum(query * sk_ref[now, :], axis=0, keepdims=True) + own_bias(head, dil_ref)
            out, total, top = softmax_columns(keys, queries, sv_ref[now, :], own, None)
            inside = slice(part * HALF, (part + 1) * HALF)
            outside = slice((1 - part) * HALF, (2 - part) * HALF)
            qe_ref[now, :] = query[:, inside].astype(BF16)
            oe_ref[now, :] = out[:, inside]
            oo_ref[now, :] = (out[:, outside] / total[:, outside] * flags[:1, outside]).astype(BF16)
            stats += [top[:, inside], total[:, inside]]
            at = (2 * pair + part) * 32
            plan_ref[at : at + 32, :] = remote_plan(head, seg_ref, dil_ref).astype(BF16)
        stat_ref[pair * 8 : pair * 8 + 8, :] = jnp.concatenate(stats + [jnp.zeros((4, HALF), F32)], axis=0)


def remote_kernel(near, qe_ref, plan_ref, oe_ref, stat_ref, oo_ref, ve_ref, *rest):
    blocks, outs = (rest[:2], rest[2:]) if near else (rest[:1], rest[1:])
    spread = one((iota((16, 128), 0) == 0) & (iota((16, 128), 1) == 16), BF16)
    row, lane = iota((HALF, 128), 0), iota((HALF, 128), 1)
    wanted = ((lane & 3) == (row >> 6)) & (lane < 16)
    close, distant = one(wanted & (lane < 8)), one(wanted & (lane >= 8))
    sides = []
    for parity in range(2):
        pieces = []
        for ref, group in zip(blocks, (close, distant) if near else (distant,)):
            flags = ref[ROWS : ROWS + 16, parity * HALF : (parity + 1) * HALF].astype(F32)
            pieces.append(t_dot(((1.0 - flags) * NEG).astype(BF16), spread) + group)
        sides.append(jnp.concatenate(pieces, axis=0).astype(BF16))
    for pair in range(PAIRS):
        both = slice(pair * 128, (pair + 1) * 128)
        place = slice(HALF + (pair & 1) * 128, HALF + (pair & 1) * 128 + 128)
        chunk = slice((pair >> 1) * HALF, (pair >> 1) * HALF + HALF)
        key = jnp.concatenate([ref[:HALF, both] for ref in blocks], axis=0)
        value = jnp.concatenate([ref[place, chunk] for ref in blocks], axis=1)
        stats = []
        for part in range(2):
            start = pair * 128 + part * HEAD_DIM
            now = slice(start, start + HEAD_DIM)
            at = (2 * pair + part) * 32
            keys = jnp.concatenate([key, sides[part]], axis=1)
            queries = all_queries(qe_ref[now, :], part, plan_ref[at : at + 32, :])
            stat = pair * 8 + 2 * part
            before = stat_ref[stat : stat + 1, :]
            out, total, top = softmax_columns(
                keys, queries, value[part * HEAD_DIM : (part + 1) * HEAD_DIM], None, before
            )
            rescale = jnp.exp(before - top)
            out = out + oe_ref[now, :] * rescale
            total = total + stat_ref[stat + 1 : stat + 2, :] * rescale
            if near:
                outs[0][now, :] = out
                stats += [top, total]
                continue
            done = out / total * ve_ref[:1, part * HALF : (part + 1) * HALF]
            outs[1][now, part * HALF : (part + 1) * HALF] = done.astype(BF16)
            outs[1][now, (1 - part) * HALF : (2 - part) * HALF] = oo_ref[now, :]
        if near:
            outs[1][pair * 8 : pair * 8 + 8, :] = jnp.concatenate(
                stats + [jnp.zeros((4, HALF), F32)], axis=0
            )
    if not near:
        outs[0][...] = dot_t(unsorting(), outs[1][...]).astype(BF16)


def state_kernel(v_hbm, steps_hbm, rates_hbm, valid_hbm, into_hbm, place_ref, *rest):
    out_refs = rest[:4]
    full_ref, v_ref, steps_ref, rates_ref, valid_ref, into_ref, arrived = rest[4:]
    copies = [
        pltpu.make_async_copy(source, target, arrived.at[at])
        for at, (source, target) in enumerate(
            (
                (rates_hbm, rates_ref),
                (steps_hbm, steps_ref),
                (valid_hbm, valid_ref),
                (into_hbm, into_ref),
                (v_hbm, v_ref),
            )
        )
    ]
    for copy in copies:
        copy.start()
    for copy in copies[:3]:
        copy.wait()
    later = one(iota((ROWS, ROWS), 0) > iota((ROWS, ROWS), 1), BF16)
    rates = jnp.concatenate([rates_ref[...], jnp.zeros((4, ROWS), F32)], axis=0)
    sums = dot(jnp.concatenate(split(rates, 3), axis=0), later)
    to_end = sums[:16] + sums[16:32] + sums[32:]
    steps = jnp.concatenate([steps_ref[...], jnp.zeros((4, ROWS), F32)], axis=0)
    weight = jnp.exp(-to_end) * steps * valid_ref[...].astype(F32)
    width = HEADS_HERE * HEAD_DIM
    spread = one((iota((32, width), 0) & 15) == (iota((32, width), 1) >> 6), BF16)
    scale = t_dot(jnp.concatenate(split(weight, 2), axis=0), spread)
    for copy in copies[3:]:
        copy.wait()
    driven = (v_ref[...].astype(F32) * scale).astype(BF16)
    full_ref[...] = t_dot(driven, into_ref[...])
    decay = jnp.exp(-jnp.sum(rates, axis=1, keepdims=True))
    decay = jnp.concatenate(split(jnp.broadcast_to(decay, (16, STATE)), 2), axis=0)
    row, source = iota((16, 32), 0), iota((16, 32), 1)
    for step in range(4):
        part = place_ref[0] ^ step
        wanted = jnp.where(row < 3, part * 3 + row, jnp.where(row < 6, 13 + part * 3 + row, -1))
        start = pl.multiple_of(part * QUARTER, 64)
        out_refs[step][:QUARTER, :] = full_ref[pl.ds(start, QUARTER), :].astype(BF16)
        out_refs[step][QUARTER:, :] = dot(one(source == wanted, BF16), decay).astype(BF16)


def decay_rows(ref_value):
    tail = ref_value[QUARTER:].astype(F32)
    return [tail[k : k + 1] + tail[k + 3 : k + 4] for k in range(3)]


def tall(decays):
    return jnp.concatenate(decays + [jnp.zeros((5, STATE), F32)], axis=0)


def spread_rows(decays):
    return jnp.concatenate([jnp.broadcast_to(d, (HEAD_DIM, STATE)) for d in decays], axis=0)


def pack_piece(state, decays):
    high, low = zip(*(split(d, 2) for d in decays))
    tail = jnp.concatenate(
        [d.astype(F32) for d in high + low] + [jnp.zeros((10, STATE), F32)], axis=0
    )
    return jnp.concatenate([state, tail], axis=0).astype(BF16)


def block_kernel(place_ref, a0, a1, a2, a3, total_ref, before_ref, fade_ref, held):
    for step, ref in enumerate((a0, a1, a2, a3)):
        held[place_ref[0] ^ step] = ref[...].astype(F32)
    state = jnp.zeros((QUARTER, STATE), F32)
    decays = [jnp.ones((1, STATE), F32)] * 3
    for at in range(4):
        before_ref[at] = state
        fade_ref[at] = tall(decays)
        now = decay_rows(held[at])
        state = state * spread_rows(now) + held[at, :QUARTER, :]
        decays = [a * b for a, b in zip(decays, now)]
    total_ref[...] = pack_piece(state, decays)


def chain(place, held):
    state = jnp.zeros((QUARTER, STATE), F32)
    decays = [jnp.ones((1, STATE), F32)] * 3
    before, before_decays = state, decays
    for at in range(4):
        here = place == at
        before = jnp.where(here, state, before)
        before_decays = [jnp.where(here, a, b) for a, b in zip(decays, before_decays)]
        now = decay_rows(held[at])
        state = state * spread_rows(now) + held[at, :QUARTER, :]
        decays = [a * b for a, b in zip(decays, now)]
    return before, before_decays, state, decays


def line_kernel(place_ref, a0, a1, a2, a3, total_ref, before_ref, fade_ref, held):
    for step, ref in enumerate((a0, a1, a2, a3)):
        held[(place_ref[1] - step) & 3] = ref[...].astype(F32)
    before, before_decays, state, decays = chain(place_ref[1], held)
    before_ref[...] = before
    fade_ref[...] = tall(before_decays)
    total_ref[...] = pack_piece(state, decays)


def plane_kernel(place_ref, a0, a1, a2, a3, line_before, line_fade, block_before, block_fade, *rest):
    outs, held = rest[:4], rest[4]
    for step, ref in enumerate((a0, a1, a2, a3)):
        held[(place_ref[2] - step) & 3] = ref[...].astype(F32)
    before = chain(place_ref[2], held)[0]
    start = spread_rows([line_fade[k : k + 1, :] for k in range(3)]) * before + line_before[...]
    for step in range(4):
        part = place_ref[0] ^ step
        fade = block_fade[part]
        fade = spread_rows([fade[k : k + 1] for k in range(3)])
        outs[step][...] = (fade * start + block_before[part]).astype(BF16)


def within_kernel(
    v_ref, gate_ref, steps_ref, rates_ref, valid_ref, into_ref, read_ref, skip_ref,
    base_ref, lift_ref, couple_ref, col_ref, row_ref,
):
    pair = pl.program_id(0)

    @pl.when(pair == 0)
    def _():
        couple_ref[...] = dot_t(read_ref[...], into_ref[...])
        upto = one(iota((ROWS, ROWS), 0) <= iota((ROWS, ROWS), 1), BF16)
        rates = jnp.concatenate([rates_ref[...], jnp.zeros((4, ROWS), F32)], axis=0)
        sums = dot(jnp.concatenate(split(rates, 3), axis=0), upto)
        fall = -(sums[:16] + sums[16:32] + sums[32:])
        steps = jnp.concatenate([steps_ref[...], jnp.ones((4, ROWS), F32)], axis=0)
        col_ref[...] = fall
        row_ref[...] = jnp.where(valid_ref[...] > 0, fall - jnp.log(steps), -NEG)

    value = v_ref[...]
    lane = iota((ROWS, 128), 1)
    results = []
    falls = []
    tile = 128
    causal = iota((tile, tile), 0) >= iota((tile, tile), 1)
    for part in range(2):
        head = 2 * pair + part
        fall = jnp.broadcast_to(col_ref[pl.ds(head, 1), :], (128, ROWS)).T
        line = row_ref[pl.ds(head, 1), :]
        pieces = []
        for at in range(ROWS // tile):
            fall_now = fall[at * tile : (at + 1) * tile]
            weights = []
            for src in range(at + 1):
                gap = fall_now - line[:, src * tile : (src + 1) * tile]
                if src == at:
                    gap = jnp.where(causal, gap, NEG)
                weights.append(
                    (
                        jnp.exp(gap)
                        * couple_ref[at * tile : (at + 1) * tile, src * tile : (src + 1) * tile]
                    ).astype(BF16)
                )
            pieces.append(dot(jnp.concatenate(weights, axis=1), value[: (at + 1) * tile]))
        results.append(jnp.concatenate(pieces, axis=0))
        falls.append(fall)
    low = lane < HEAD_DIM
    gate = gate_ref[...].astype(F32)
    gate = gate / (1.0 + jnp.exp(-gate))
    skip = jnp.where(low, skip_ref[2 * pair], skip_ref[2 * pair + 1])
    within = jnp.where(low, results[0], results[1])
    base_ref[...] = ((within + skip * value.astype(F32)) * gate).astype(BF16)
    lift_ref[...] = (jnp.exp(jnp.where(low, falls[0], falls[1])) * gate).astype(BF16)


def finish_kernel(place_ref, f0, f1, f2, f3, read_ref, base_ref, lift_ref, gain_ref, out_ref, held):
    @pl.when(pl.program_id(0) == 0)
    def _():
        for step, ref in enumerate((f0, f1, f2, f3)):
            part = place_ref[0] ^ step
            held[pl.ds(pl.multiple_of(part * QUARTER, 64), QUARTER), :] = ref[...]

    together = one((iota((128, 128), 0) >> 6) == (iota((128, 128), 1) >> 6), BF16)
    for pair in range(PAIRS):
        now = slice(pair * 128, (pair + 1) * 128)
        carried = dot_t(read_ref[...], held[now, :])
        gated = base_ref[:, now].astype(F32) + lift_ref[:, now].astype(F32) * carried
        high, low = split(gated * gated, 2)
        mean = (dot(high, together) + dot(low, together)) * (1.0 / HEAD_DIM)
        out_ref[:, now] = (gated * lax.rsqrt(mean + 1e-05) * gain_ref[:, now]).astype(BF16)


def shape(*dims, kind=BF16):
    return jax.ShapeDtypeStruct(dims, kind)


def lanes(rows, row_block=0):
    return pl.BlockSpec((rows, 128), lambda pair: (row_block, pair))


def whole(*dims):
    return pl.BlockSpec(dims, lambda pair: (0,) * len(dims))


def call_pack(key_rows, value_rows, valid):
    return pl.pallas_call(
        pack_kernel,
        out_shape=shape(ROWS + 16, WIDTH),
        in_specs=[VMEM] * 3,
        out_specs=VMEM,
        cost_estimate=FREE,
        compiler_params=params(),
        name="pack",
    )(key_rows, value_rows, valid)


def call_state(*args):
    far = pl.BlockSpec(memory_space=pltpu.HBM)
    return pl.pallas_call(
        state_kernel,
        out_shape=[shape(PIECE, STATE)] * 4,
        in_specs=[far] * 5 + [SMEM],
        out_specs=[VMEM] * 4,
        scratch_shapes=[
            pltpu.VMEM((WIDTH, STATE), F32),
            pltpu.VMEM((ROWS, WIDTH), BF16),
            pltpu.VMEM((HEADS_HERE, ROWS), F32),
            pltpu.VMEM((HEADS_HERE, ROWS), F32),
            pltpu.VMEM((1, ROWS), jnp.int32),
            pltpu.VMEM((ROWS, STATE), BF16),
            pltpu.SemaphoreType.DMA((5,)),
        ],
        cost_estimate=FREE,
        compiler_params=params(58),
        name="state",
    )(*args)


HOLD = [pltpu.VMEM((4, PIECE, STATE), F32)]


def call_block(place, *pieces):
    return pl.pallas_call(
        block_kernel,
        out_shape=[shape(PIECE, STATE), shape(4, QUARTER, STATE, kind=F32), shape(4, 8, STATE, kind=F32)],
        in_specs=[SMEM] + [VMEM] * 4,
        out_specs=[VMEM] * 3,
        scratch_shapes=HOLD,
        cost_estimate=FREE,
        compiler_params=params(),
        name="block",
    )(place, *pieces)


def call_line(place, *totals):
    return pl.pallas_call(
        line_kernel,
        out_shape=[shape(PIECE, STATE), shape(QUARTER, STATE, kind=F32), shape(8, STATE, kind=F32)],
        in_specs=[SMEM] + [VMEM] * 4,
        out_specs=[VMEM] * 3,
        scratch_shapes=HOLD,
        cost_estimate=FREE,
        compiler_params=params(),
        name="line",
    )(place, *totals)


def call_plane(place, *args):
    return pl.pallas_call(
        plane_kernel,
        out_shape=[shape(QUARTER, STATE)] * 4,
        in_specs=[SMEM] + [VMEM] * 8,
        out_specs=[VMEM] * 4,
        scratch_shapes=HOLD,
        cost_estimate=FREE,
        compiler_params=params(),
        name="plane",
    )(place, *args)


KEPT = [
    shape(WIDTH, HALF),
    shape(HEADS_HERE * 32, HALF),
    shape(WIDTH, HALF, kind=F32),
    shape(8 * PAIRS, HALF, kind=F32),
    shape(WIDTH, HALF),
    shape(8, ROWS, kind=F32),
]


def call_local(*args):
    return pl.pallas_call(
        local_kernel,
        out_shape=KEPT,
        in_specs=[VMEM] * 4 + [SMEM] * 3,
        out_specs=[VMEM] * 6,
        scratch_shapes=[
            pltpu.VMEM((ROWS, ROWS), BF16),
            pltpu.VMEM((WIDTH, ROWS), F32),
            pltpu.VMEM((WIDTH, ROWS), F32),
            pltpu.VMEM((WIDTH, ROWS), BF16),
        ],
        cost_estimate=FREE,
        compiler_params=params(14),
        name="local",
    )(*args)


def call_within(*args):
    return pl.pallas_call(
        within_kernel,
        grid=(PAIRS,),
        out_shape=[shape(ROWS, WIDTH)] * 2,
        in_specs=[lanes(ROWS)] * 2
        + [whole(HEADS_HERE, ROWS)] * 2
        + [whole(1, ROWS), whole(ROWS, STATE), whole(ROWS, STATE), SMEM],
        out_specs=[lanes(ROWS)] * 2,
        scratch_shapes=[pltpu.VMEM((ROWS, ROWS), F32), pltpu.VMEM((16, ROWS), F32), pltpu.VMEM((16, ROWS), F32)],
        cost_estimate=FREE,
        compiler_params=params(8),
        name="within",
    )(*args)


def call_finish(*args):
    def rows(width):
        return pl.BlockSpec((HALF, width), lambda at: (at, 0))

    return pl.pallas_call(
        finish_kernel,
        grid=(ROWS // HALF,),
        out_shape=shape(ROWS, WIDTH),
        in_specs=[SMEM]
        + [whole(QUARTER, STATE)] * 4
        + [rows(STATE)]
        + [rows(WIDTH)] * 2
        + [whole(1, WIDTH)],
        out_specs=rows(WIDTH),
        scratch_shapes=[pltpu.VMEM((WIDTH, STATE), BF16)],
        cost_estimate=FREE,
        compiler_params=params(),
        name="finish",
    )(*args)


def call_near(kept, arrived):
    out, stat = pl.pallas_call(
        functools.partial(remote_kernel, True),
        out_shape=[KEPT[2], KEPT[3]],
        in_specs=[VMEM] * 8,
        out_specs=[VMEM] * 2,
        cost_estimate=FREE,
        compiler_params=params(14),
        name="near",
    )(*kept, *arrived)
    return [kept[0], kept[1], out, stat, kept[4], kept[5]]


def call_remote(kept, arrived):
    return pl.pallas_call(
        functools.partial(remote_kernel, False),
        out_shape=shape(ROWS, WIDTH),
        in_specs=[VMEM] * 7,
        out_specs=VMEM,
        scratch_shapes=[pltpu.VMEM((WIDTH, ROWS), BF16)],
        cost_estimate=FREE,
        compiler_params=params(14),
        name="remote",
    )(*kept, arrived)


def per_device(
    query_rows,
    key_rows,
    value_rows,
    patch_valid,
    segment_lengths,
    dilation,
    step_sizes,
    decay_rates,
    state_in,
    state_out,
    gate_in,
    skip_weight,
    norm_gain,
):
    count = lax.axis_size("seq")
    seq_rank = lax.axis_index("seq").astype(jnp.int32)
    rank = jnp.reshape(lax.axis_index("head").astype(jnp.int32), (1,))
    place = jnp.stack([seq_rank & 3, (seq_rank >> 2) & 3, seq_rank >> 4])
    valid = patch_valid.reshape(1, ROWS)
    gain = norm_gain.reshape(1, WIDTH)

    def cross(block, mask):
        return lax.ppermute(block, "seq", [(i, i ^ mask) for i in range(count)])

    def turn(block, step, span):
        unit = span // 4
        route = [(i, i // span * span + (i % span + step * unit) % span) for i in range(count)]
        return lax.ppermute(block, "seq", route)

    after = lax.optimization_barrier
    scan_inputs = (step_sizes, decay_rates, valid, state_in)

    pieces = call_state(value_rows, *scan_inputs, place)
    packed = call_pack(key_rows, value_rows, after((valid, pieces))[0])
    pieces = [pieces[0]] + [cross(pieces[mask], mask) for mask in range(1, SPAN_DEV)]
    near = [cross(packed, 1)]
    pieces = after((pieces, packed))[0]
    total, block_before, block_fade = call_block(place, *pieces)
    totals = [total] + [turn(total, step, 16) for step in range(1, 4)]
    packed, totals = after((packed, totals))
    near.append(cross(packed, 2))
    far = cross(packed, 3)
    total, line_before, line_fade = call_line(place, *totals)
    kept = call_local(
        query_rows, key_rows, value_rows, after((valid, total))[0], segment_lengths, dilation, rank
    )
    totals = [total] + [turn(total, step, 64) for step in range(1, 4)]
    totals = after((totals, kept))[0]
    carried = call_plane(place, *totals, line_before, line_fade, block_before, block_fade)
    scan_inputs = (*scan_inputs[:2], after((valid, carried))[0], state_in)
    within = call_within(value_rows, gate_in, *scan_inputs, state_out, skip_weight)
    carried = [carried[0]] + [cross(carried[mask], mask) for mask in range(1, SPAN_DEV)]
    kept = call_near(after((kept, within))[0], near)
    carried = after((carried, kept))[0]
    scanned = call_finish(place, *carried, state_out, *within, gain)
    attended = call_remote(kept, far)
    return (attended, scanned)


def solution(mesh):
    return jax.shard_map(
        per_device,
        mesh=mesh,
        in_specs=(
            P(("slide", "seq"), "head"),
            P(("slide", "seq"), "head"),
            P(("slide", "seq"), "head"),
            P(("slide", "seq")),
            P(),
            P(),
            P("head", ("slide", "seq")),
            P("head", ("slide", "seq")),
            P(("slide", "seq"), None),
            P(("slide", "seq"), None),
            P(("slide", "seq"), "head"),
            P("head"),
            P("head"),
        ),
        out_specs=(P(("slide", "seq"), "head"), P(("slide", "seq"), "head")),
        check_vma=False,
    )
```

```python
import functools
import math

import jax
import jax.numpy as jnp
import numpy as np
from jax import lax
from jax.experimental import pallas as pl
from jax.experimental.pallas import tpu as pltpu
from jax.sharding import PartitionSpec as P

HEAD_DIM = 64
STATE = 128
HEADS_PER_GROUP = 6
SPAN_DEV = 4
ROWS = 512
HALF = 256
PAIRS = 6
HEADS_HERE = 12
QUARTER = 192
WIDTH = HEADS_HERE * HEAD_DIM
PIECE = 208
NEG = -1e30
F32 = jnp.float32
BF16 = jnp.bfloat16

LN2_HI = float(np.float32(jnp.bfloat16(math.log(2.0))))
LN2_LO = float(np.float32(jnp.bfloat16(math.log(2.0) - LN2_HI)))
LN3_HI = float(np.float32(jnp.bfloat16(math.log(3.0))))
LN3_LO = float(np.float32(jnp.bfloat16(math.log(3.0) - LN3_HI)))

VMEM = pl.BlockSpec(memory_space=pltpu.VMEM)
SMEM = pl.BlockSpec(memory_space=pltpu.SMEM)


def iota(shape, dim):
    return lax.broadcasted_iota(jnp.int32, shape, dim)


def dot(a, b):
    return lax.dot_general(a, b, (((1,), (0,)), ((), ())), preferred_element_type=F32)


def dot_t(a, b):
    return lax.dot_general(a, b, (((1,), (1,)), ((), ())), preferred_element_type=F32)


def t_dot(a, b):
    return lax.dot_general(a, b, (((0,), (0,)), ((), ())), preferred_element_type=F32)


def one(mask, kind=F32):
    return jnp.where(mask, 1.0, 0.0).astype(kind)


def residue_of(block):
    return ((block & 1) << 2) | (block & 2) | (block >> 2)


def sorting():
    row = iota((ROWS, ROWS), 0)
    token = 8 * (row & 63) + residue_of(row >> 6)
    return one(iota((ROWS, ROWS), 1) == token, BF16)


def unsorting():
    column = iota((ROWS, ROWS), 1)
    token = 8 * (column & 63) + residue_of(column >> 6)
    return one(iota((ROWS, ROWS), 0) == token, BF16)


def split(x, parts):
    out = []
    for _ in range(parts):
        head = x.astype(BF16)
        out.append(head)
        x = x - head.astype(F32)
    return out


FREE = pl.CostEstimate(flops=1, bytes_accessed=1, transcendentals=0)


def params(mib=8):
    return pltpu.CompilerParams(vmem_limit_bytes=mib * 1024 * 1024)


def pack_kernel(k_ref, v_ref, valid_ref, out_ref):
    sort = sorting()
    unsort = unsorting()
    low = (iota((HALF, WIDTH), 1) & 127) < HEAD_DIM
    rows = dot(sort, k_ref[...])
    out_ref[:HALF, :] = jnp.where(low, rows[:HALF], rows[HALF:]).astype(BF16)
    columns = t_dot(v_ref[...], unsort)
    even = (iota((WIDTH, HALF), 0) & 127) < HEAD_DIM
    columns = jnp.where(even, columns[:, :HALF], columns[:, HALF:]).astype(BF16)
    for at in range(0, WIDTH, HALF):
        out_ref[HALF:ROWS, at : at + HALF] = columns[at : at + HALF]
    valid = jnp.broadcast_to(valid_ref[...].astype(F32), (16, ROWS)).astype(BF16)
    line = dot_t(valid, sort)
    out_ref[ROWS : ROWS + 16, :] = jnp.concatenate(
        [line, jnp.zeros((16, WIDTH - ROWS), F32)], axis=1
    ).astype(BF16)


def log_count(count):
    high = jnp.where(count == 0, NEG, jnp.where(count == 2, LN2_HI, jnp.where(count == 3, LN3_HI, 0.0)))
    low = jnp.where(count == 2, LN2_LO, jnp.where(count == 3, LN3_LO, 0.0))
    return high, low


def plan_of(head, seg_ref, dil_ref):
    group = head // HEADS_PER_GROUP
    return dil_ref[group, 1], dil_ref[group, 2], seg_ref[group, 0], seg_ref[group, 1]


def local_plan(head, seg_ref, dil_ref):
    r1, r2, w0, w1 = plan_of(head, seg_ref, dil_ref)
    key, query = iota((16, ROWS), 0), iota((16, ROWS), 1) >> 5
    same = (key & 1) == (query & 1)
    key_off, query_off = residue_of(key >> 1) - head, residue_of(query >> 1) - head

    def on(stride):
        return (key_off & (stride - 1)) + (query_off & (stride - 1)) == 0

    count = one(same | (w0 >= ROWS)) + one(on(r1) & (same | (w1 >= ROWS))) + one(on(r2))
    return jnp.concatenate([*log_count(count), jnp.ones((16, ROWS), F32)], axis=0)


def remote_plan(head, seg_ref, dil_ref):
    r1, r2, _, w1 = plan_of(head, seg_ref, dil_ref)
    row = iota((8, HALF), 0)
    shift = (head & 1) - head
    key_off = residue_of(row & 3) + shift
    query_off = residue_of(iota((8, HALF), 1) >> 6) + shift

    def on(stride):
        return (key_off & (stride - 1)) + (query_off & (stride - 1)) == 0

    parts = []
    for reach in (2 * ROWS, 4 * ROWS):
        high, low = log_count(one(on(r1) & (w1 >= reach)) + one(on(r2)))
        parts.append(jnp.where(row < 4, high, low))
    return jnp.concatenate(parts + [jnp.ones((16, HALF), F32)], axis=0)


def own_bias(head, dil_ref):
    group = head // HEADS_PER_GROUP
    off = residue_of(iota((1, ROWS), 1) >> 6) - head
    count = 1 + jnp.where((off & (dil_ref[group, 1] - 1)) == 0, 1, 0)
    count = count + jnp.where((off & (dil_ref[group, 2] - 1)) == 0, 1, 0)
    return jnp.where(count == 1, 0.0, jnp.where(count == 2, LN2_HI + LN2_LO, LN3_HI + LN3_LO))


def staggered(jobs, depth=2):
    waiting = []
    for keys, queries, finish in jobs:
        waiting.append((finish, dot(keys(), queries())))
        if len(waiting) > depth:
            finish, scores = waiting.pop(0)
            finish(scores)
    for finish, scores in waiting:
        finish(scores)


def softmax_columns(scores, values, own, before):
    if own is not None:
        tile = 128
        diagonal = iota((tile, tile), 0) == iota((tile, tile), 1)
        rows = []
        for at in range(0, scores.shape[0], tile):
            line = scores[at : at + tile]
            here = jnp.where(diagonal, own[:, at : at + tile], line[:, at : at + tile])
            parts = [line[:, :at], here, line[:, at + tile :]]
            rows.append(jnp.concatenate([x for x in parts if x.shape[1]], axis=1))
        scores = jnp.concatenate(rows, axis=0)
    top = jnp.max(scores, axis=0, keepdims=True)
    if before is not None:
        top = jnp.maximum(top, before)
    values = jnp.concatenate([values, jnp.ones((16, values.shape[1]), BF16)], axis=0)
    out = dot(values, jnp.exp(scores - top).astype(BF16))
    return out[:HEAD_DIM], out[HEAD_DIM : HEAD_DIM + 1], top


def all_queries(rows, part, plan):
    rest = jnp.zeros((HEAD_DIM - plan.shape[0], rows.shape[1]), BF16)
    pieces = [plan.astype(BF16), rest]
    return jnp.concatenate([rows] + pieces if part == 0 else pieces + [rows], axis=0)


def own_lanes(rows, part):
    lane = iota((rows, 128), 1)
    return one((lane < HEAD_DIM) == (part == 0), BF16)


def plan_lane(rows, part):
    return iota((rows, 128), 1) - (HEAD_DIM if part == 0 else 0)


def local_kernel(
    q_ref, k_ref, v_ref, valid_ref, seg_ref, dil_ref, rank_ref,
    qe_ref, plan_ref, oe_ref, stat_ref, oo_ref, ve_ref,
    unsort_ref, sq_ref, sk_ref, sv_ref,
):
    unsort_ref[...] = unsorting()
    valid = jnp.broadcast_to(valid_ref[...].astype(F32), (128, ROWS)).astype(BF16)
    flags = dot(valid, unsort_ref[...])
    ve_ref[...] = flags[:8]
    row = iota((ROWS, 128), 0)
    hidden = (1.0 - flags.T) * NEG
    sides, masks = [], []
    for part in range(2):
        lane = plan_lane(ROWS, part)
        side = one(((row >> 5) == (lane & 15)) & (lane >= 0) & (lane < 32))
        sides.append(jnp.where(lane == 32, hidden, side).astype(BF16))
        masks.append(own_lanes(ROWS, part))
    sq_ref[...] = t_dot(q_ref[...], unsort_ref[...]) * (HEAD_DIM**-0.5)
    sk_ref[...] = t_dot(k_ref[...], unsort_ref[...])
    sv_ref[...] = t_dot(v_ref[...], unsort_ref[...]).astype(BF16)
    def job(pair, part):
        both = slice(pair * 128, (pair + 1) * 128)
        head = rank_ref[0] * HEADS_HERE + 2 * pair + part
        start = pair * 128 + part * HEAD_DIM
        now = slice(start, start + HEAD_DIM)
        inside = slice(part * HALF, (part + 1) * HALF)
        outside = slice((1 - part) * HALF, (2 - part) * HALF)

        def keys():
            return sk_ref[both, :].T.astype(BF16) * masks[part] + sides[part]

        def queries():
            return all_queries(sq_ref[now, :].astype(BF16), part, local_plan(head, seg_ref, dil_ref))

        def finish(scores):
            query = sq_ref[now, :]
            own = jnp.sum(query * sk_ref[now, :], axis=0, keepdims=True) + own_bias(head, dil_ref)
            out, total, top = softmax_columns(scores, sv_ref[now, :], own, None)
            qe_ref[now, :] = query[:, inside].astype(BF16)
            oe_ref[now, :] = out[:, inside]
            oo_ref[now, :] = (out[:, outside] / total[:, outside] * flags[:1, outside]).astype(BF16)
            at = (2 * pair + part) * 32
            plan_ref[at : at + 32, :] = remote_plan(head, seg_ref, dil_ref).astype(BF16)
            stat = pair * 8 + 2 * part
            stat_ref[stat : stat + 1, :] = top[:, inside]
            stat_ref[stat + 1 : stat + 2, :] = total[:, inside]

        return keys, queries, finish

    staggered([job(pair, part) for pair in range(PAIRS) for part in range(2)])


def remote_kernel(near, qe_ref, plan_ref, oe_ref, stat_ref, oo_ref, ve_ref, *rest):
    blocks, outs = (rest[:2], rest[2:]) if near else (rest[:1], rest[1:])
    row = iota((HALF, 128), 0)
    sides, masks = [], []
    for part in range(2):
        lane = plan_lane(HALF, part)
        first = one((iota((16, 128), 0) == 0) & (plan_lane(16, part) == 16), BF16)
        same = ((lane & 3) == (row >> 6)) & (lane >= 0)
        close, distant = one(same & (lane < 8)), one(same & (lane >= 8) & (lane < 16))
        pieces = []
        for ref, group in zip(blocks, (close, distant) if near else (distant,)):
            flags = ref[ROWS : ROWS + 16, part * HALF : (part + 1) * HALF].astype(F32)
            pieces.append(t_dot(((1.0 - flags) * NEG).astype(BF16), first) + group)
        sides.append(jnp.concatenate(pieces, axis=0).astype(BF16))
        masks.append(own_lanes(HALF * len(blocks), part))
    def job(pair, part):
        both = slice(pair * 128, (pair + 1) * 128)
        start = pair * 128 + part * HEAD_DIM
        now = slice(start, start + HEAD_DIM)
        place = start % HALF + HALF
        place = slice(place, place + HEAD_DIM)
        chunk = slice((pair >> 1) * HALF, (pair >> 1) * HALF + HALF)
        at = (2 * pair + part) * 32
        stat = pair * 8 + 2 * part

        def keys():
            key = jnp.concatenate([ref[:HALF, both] for ref in blocks], axis=0)
            return key * masks[part] + sides[part]

        def queries():
            return all_queries(qe_ref[now, :], part, plan_ref[at : at + 32, :])

        def finish(scores):
            value = jnp.concatenate([ref[place, chunk] for ref in blocks], axis=1)
            before = stat_ref[stat : stat + 1, :]
            out, total, top = softmax_columns(scores, value, None, before)
            rescale = jnp.exp(before - top)
            out = out + oe_ref[now, :] * rescale
            total = total + stat_ref[stat + 1 : stat + 2, :] * rescale
            if near:
                outs[0][now, :] = out
                outs[1][stat : stat + 1, :] = top
                outs[1][stat + 1 : stat + 2, :] = total
                return
            done = out / total * ve_ref[:1, part * HALF : (part + 1) * HALF]
            outs[1][now, part * HALF : (part + 1) * HALF] = done.astype(BF16)
            outs[1][now, (1 - part) * HALF : (2 - part) * HALF] = oo_ref[now, :]

        return keys, queries, finish

    staggered([job(pair, part) for pair in range(PAIRS) for part in range(2)])
    if not near:
        outs[0][...] = dot_t(unsorting(), outs[1][...]).astype(BF16)


def state_kernel(v_hbm, steps_hbm, rates_hbm, valid_hbm, into_hbm, place_ref, *rest):
    out_refs = rest[:4]
    full_ref, v_ref, steps_ref, rates_ref, valid_ref, into_ref, arrived = rest[4:]
    copies = [
        pltpu.make_async_copy(source, target, arrived.at[at])
        for at, (source, target) in enumerate(
            (
                (rates_hbm, rates_ref),
                (steps_hbm, steps_ref),
                (valid_hbm, valid_ref),
                (into_hbm, into_ref),
                (v_hbm, v_ref),
            )
        )
    ]
    for copy in copies:
        copy.start()
    for copy in copies[:3]:
        copy.wait()
    later = one(iota((ROWS, ROWS), 0) > iota((ROWS, ROWS), 1), BF16)
    rates = jnp.concatenate([rates_ref[...], jnp.zeros((4, ROWS), F32)], axis=0)
    sums = dot(jnp.concatenate(split(rates, 3), axis=0), later)
    to_end = sums[:16] + sums[16:32] + sums[32:]
    steps = jnp.concatenate([steps_ref[...], jnp.zeros((4, ROWS), F32)], axis=0)
    weight = jnp.exp(-to_end) * steps * valid_ref[...].astype(F32)
    width = HEADS_HERE * HEAD_DIM
    spread = one((iota((32, width), 0) & 15) == (iota((32, width), 1) >> 6), BF16)
    scale = t_dot(jnp.concatenate(split(weight, 2), axis=0), spread)
    for copy in copies[3:]:
        copy.wait()
    driven = (v_ref[...].astype(F32) * scale).astype(BF16)
    full_ref[...] = t_dot(driven, into_ref[...])
    decay = jnp.exp(-jnp.sum(rates, axis=1, keepdims=True))
    decay = jnp.concatenate(split(jnp.broadcast_to(decay, (16, STATE)), 2), axis=0)
    row, source = iota((16, 32), 0), iota((16, 32), 1)
    for step in range(4):
        part = place_ref[0] ^ step
        wanted = jnp.where(row < 3, part * 3 + row, jnp.where(row < 6, 13 + part * 3 + row, -1))
        start = pl.multiple_of(part * QUARTER, 64)
        out_refs[step][:QUARTER, :] = full_ref[pl.ds(start, QUARTER), :].astype(BF16)
        out_refs[step][QUARTER:, :] = dot(one(source == wanted, BF16), decay).astype(BF16)


def decay_rows(ref_value):
    tail = ref_value[QUARTER:].astype(F32)
    return [tail[k : k + 1] + tail[k + 3 : k + 4] for k in range(3)]


def tall(decays):
    return jnp.concatenate(decays + [jnp.zeros((5, STATE), F32)], axis=0)


def spread_rows(decays):
    return jnp.concatenate([jnp.broadcast_to(d, (HEAD_DIM, STATE)) for d in decays], axis=0)


def pack_piece(state, decays):
    high, low = zip(*(split(d, 2) for d in decays))
    tail = jnp.concatenate(
        [d.astype(F32) for d in high + low] + [jnp.zeros((10, STATE), F32)], axis=0
    )
    return jnp.concatenate([state, tail], axis=0).astype(BF16)


def block_kernel(place_ref, a0, a1, a2, a3, total_ref, before_ref, fade_ref, held):
    for step, ref in enumerate((a0, a1, a2, a3)):
        held[place_ref[0] ^ step] = ref[...].astype(F32)
    state = jnp.zeros((QUARTER, STATE), F32)
    decays = [jnp.ones((1, STATE), F32)] * 3
    for at in range(4):
        before_ref[at] = state
        fade_ref[at] = tall(decays)
        now = decay_rows(held[at])
        state = state * spread_rows(now) + held[at, :QUARTER, :]
        decays = [a * b for a, b in zip(decays, now)]
    total_ref[...] = pack_piece(state, decays)


def chain(place, held):
    state = jnp.zeros((QUARTER, STATE), F32)
    decays = [jnp.ones((1, STATE), F32)] * 3
    before, before_decays = state, decays
    for at in range(4):
        here = place == at
        before = jnp.where(here, state, before)
        before_decays = [jnp.where(here, a, b) for a, b in zip(decays, before_decays)]
        now = decay_rows(held[at])
        state = state * spread_rows(now) + held[at, :QUARTER, :]
        decays = [a * b for a, b in zip(decays, now)]
    return before, before_decays, state, decays


def line_kernel(place_ref, a0, a1, a2, a3, total_ref, before_ref, fade_ref, held):
    for step, ref in enumerate((a0, a1, a2, a3)):
        held[(place_ref[1] - step) & 3] = ref[...].astype(F32)
    before, before_decays, state, decays = chain(place_ref[1], held)
    before_ref[...] = before
    fade_ref[...] = tall(before_decays)
    total_ref[...] = pack_piece(state, decays)


def plane_kernel(place_ref, a0, a1, a2, a3, line_before, line_fade, block_before, block_fade, *rest):
    outs, held = rest[:4], rest[4]
    for step, ref in enumerate((a0, a1, a2, a3)):
        held[(place_ref[2] - step) & 3] = ref[...].astype(F32)
    before = chain(place_ref[2], held)[0]
    start = spread_rows([line_fade[k : k + 1, :] for k in range(3)]) * before + line_before[...]
    for step in range(4):
        part = place_ref[0] ^ step
        fade = block_fade[part]
        fade = spread_rows([fade[k : k + 1] for k in range(3)])
        outs[step][...] = (fade * start + block_before[part]).astype(BF16)


def within_kernel(
    v_ref, gate_ref, steps_ref, rates_ref, valid_ref, into_ref, read_ref, skip_ref,
    base_ref, lift_ref, couple_ref, col_ref, row_ref,
):
    pair = pl.program_id(0)

    @pl.when(pair == 0)
    def _():
        couple_ref[...] = dot_t(read_ref[...], into_ref[...])
        upto = one(iota((ROWS, ROWS), 0) <= iota((ROWS, ROWS), 1), BF16)
        rates = jnp.concatenate([rates_ref[...], jnp.zeros((4, ROWS), F32)], axis=0)
        sums = dot(jnp.concatenate(split(rates, 3), axis=0), upto)
        fall = -(sums[:16] + sums[16:32] + sums[32:])
        steps = jnp.concatenate([steps_ref[...], jnp.ones((4, ROWS), F32)], axis=0)
        col_ref[...] = fall
        row_ref[...] = jnp.where(valid_ref[...] > 0, fall - jnp.log(steps), -NEG)

    value = v_ref[...]
    lane = iota((ROWS, 128), 1)
    results = []
    falls = []
    tile = 128
    causal = iota((tile, tile), 0) >= iota((tile, tile), 1)
    for part in range(2):
        head = 2 * pair + part
        fall = jnp.broadcast_to(col_ref[pl.ds(head, 1), :], (128, ROWS)).T
        line = row_ref[pl.ds(head, 1), :]
        pieces = []
        for at in range(ROWS // tile):
            fall_now = fall[at * tile : (at + 1) * tile]
            weights = []
            for src in range(at + 1):
                gap = fall_now - line[:, src * tile : (src + 1) * tile]
                if src == at:
                    gap = jnp.where(causal, gap, NEG)
                weights.append(
                    (
                        jnp.exp(gap)
                        * couple_ref[at * tile : (at + 1) * tile, src * tile : (src + 1) * tile]
                    ).astype(BF16)
                )
            pieces.append(dot(jnp.concatenate(weights, axis=1), value[: (at + 1) * tile]))
        results.append(jnp.concatenate(pieces, axis=0))
        falls.append(fall)
    low = lane < HEAD_DIM
    gate = gate_ref[...].astype(F32)
    gate = gate / (1.0 + jnp.exp(-gate))
    skip = jnp.where(low, skip_ref[2 * pair], skip_ref[2 * pair + 1])
    within = jnp.where(low, results[0], results[1])
    base_ref[...] = ((within + skip * value.astype(F32)) * gate).astype(BF16)
    lift_ref[...] = (jnp.exp(jnp.where(low, falls[0], falls[1])) * gate).astype(BF16)


def finish_kernel(place_ref, f0, f1, f2, f3, read_ref, base_ref, lift_ref, gain_ref, out_ref, held):
    @pl.when(pl.program_id(0) == 0)
    def _():
        for step, ref in enumerate((f0, f1, f2, f3)):
            part = place_ref[0] ^ step
            held[pl.ds(pl.multiple_of(part * QUARTER, 64), QUARTER), :] = ref[...]

    together = one((iota((128, 128), 0) >> 6) == (iota((128, 128), 1) >> 6), BF16)
    for pair in range(PAIRS):
        now = slice(pair * 128, (pair + 1) * 128)
        carried = dot_t(read_ref[...], held[now, :])
        gated = base_ref[:, now].astype(F32) + lift_ref[:, now].astype(F32) * carried
        high, low = split(gated * gated, 2)
        mean = (dot(high, together) + dot(low, together)) * (1.0 / HEAD_DIM)
        out_ref[:, now] = (gated * lax.rsqrt(mean + 1e-05) * gain_ref[:, now]).astype(BF16)


def shape(*dims, kind=BF16):
    return jax.ShapeDtypeStruct(dims, kind)


def lanes(rows, row_block=0):
    return pl.BlockSpec((rows, 128), lambda pair: (row_block, pair))


def whole(*dims):
    return pl.BlockSpec(dims, lambda pair: (0,) * len(dims))


def call_pack(key_rows, value_rows, valid):
    return pl.pallas_call(
        pack_kernel,
        out_shape=shape(ROWS + 16, WIDTH),
        in_specs=[VMEM] * 3,
        out_specs=VMEM,
        cost_estimate=FREE,
        compiler_params=params(),
        name="pack",
    )(key_rows, value_rows, valid)


def call_state(*args):
    far = pl.BlockSpec(memory_space=pltpu.HBM)
    return pl.pallas_call(
        state_kernel,
        out_shape=[shape(PIECE, STATE)] * 4,
        in_specs=[far] * 5 + [SMEM],
        out_specs=[VMEM] * 4,
        scratch_shapes=[
            pltpu.VMEM((WIDTH, STATE), F32),
            pltpu.VMEM((ROWS, WIDTH), BF16),
            pltpu.VMEM((HEADS_HERE, ROWS), F32),
            pltpu.VMEM((HEADS_HERE, ROWS), F32),
            pltpu.VMEM((1, ROWS), jnp.int32),
            pltpu.VMEM((ROWS, STATE), BF16),
            pltpu.SemaphoreType.DMA((5,)),
        ],
        cost_estimate=FREE,
        compiler_params=params(58),
        name="state",
    )(*args)


HOLD = [pltpu.VMEM((4, PIECE, STATE), F32)]


def call_block(place, *pieces):
    return pl.pallas_call(
        block_kernel,
        out_shape=[shape(PIECE, STATE), shape(4, QUARTER, STATE, kind=F32), shape(4, 8, STATE, kind=F32)],
        in_specs=[SMEM] + [VMEM] * 4,
        out_specs=[VMEM] * 3,
        scratch_shapes=HOLD,
        cost_estimate=FREE,
        compiler_params=params(),
        name="block",
    )(place, *pieces)


def call_line(place, *totals):
    return pl.pallas_call(
        line_kernel,
        out_shape=[shape(PIECE, STATE), shape(QUARTER, STATE, kind=F32), shape(8, STATE, kind=F32)],
        in_specs=[SMEM] + [VMEM] * 4,
        out_specs=[VMEM] * 3,
        scratch_shapes=HOLD,
        cost_estimate=FREE,
        compiler_params=params(),
        name="line",
    )(place, *totals)


def call_plane(place, *args):
    return pl.pallas_call(
        plane_kernel,
        out_shape=[shape(QUARTER, STATE)] * 4,
        in_specs=[SMEM] + [VMEM] * 8,
        out_specs=[VMEM] * 4,
        scratch_shapes=HOLD,
        cost_estimate=FREE,
        compiler_params=params(),
        name="plane",
    )(place, *args)


KEPT = [
    shape(WIDTH, HALF),
    shape(HEADS_HERE * 32, HALF),
    shape(WIDTH, HALF, kind=F32),
    shape(8 * PAIRS, HALF, kind=F32),
    shape(WIDTH, HALF),
    shape(8, ROWS, kind=F32),
]


def call_local(*args):
    return pl.pallas_call(
        local_kernel,
        out_shape=KEPT,
        in_specs=[VMEM] * 4 + [SMEM] * 3,
        out_specs=[VMEM] * 6,
        scratch_shapes=[
            pltpu.VMEM((ROWS, ROWS), BF16),
            pltpu.VMEM((WIDTH, ROWS), F32),
            pltpu.VMEM((WIDTH, ROWS), F32),
            pltpu.VMEM((WIDTH, ROWS), BF16),
        ],
        cost_estimate=FREE,
        compiler_params=params(14),
        name="local",
    )(*args)


def call_within(*args):
    return pl.pallas_call(
        within_kernel,
        grid=(PAIRS,),
        out_shape=[shape(ROWS, WIDTH)] * 2,
        in_specs=[lanes(ROWS)] * 2
        + [whole(HEADS_HERE, ROWS)] * 2
        + [whole(1, ROWS), whole(ROWS, STATE), whole(ROWS, STATE), SMEM],
        out_specs=[lanes(ROWS)] * 2,
        scratch_shapes=[pltpu.VMEM((ROWS, ROWS), F32), pltpu.VMEM((16, ROWS), F32), pltpu.VMEM((16, ROWS), F32)],
        cost_estimate=FREE,
        compiler_params=params(8),
        name="within",
    )(*args)


def call_finish(*args):
    def rows(width):
        return pl.BlockSpec((HALF, width), lambda at: (at, 0))

    return pl.pallas_call(
        finish_kernel,
        grid=(ROWS // HALF,),
        out_shape=shape(ROWS, WIDTH),
        in_specs=[SMEM]
        + [whole(QUARTER, STATE)] * 4
        + [rows(STATE)]
        + [rows(WIDTH)] * 2
        + [whole(1, WIDTH)],
        out_specs=rows(WIDTH),
        scratch_shapes=[pltpu.VMEM((WIDTH, STATE), BF16)],
        cost_estimate=FREE,
        compiler_params=params(),
        name="finish",
    )(*args)


def call_near(kept, arrived):
    out, stat = pl.pallas_call(
        functools.partial(remote_kernel, True),
        out_shape=[KEPT[2], KEPT[3]],
        in_specs=[VMEM] * 8,
        out_specs=[VMEM] * 2,
        cost_estimate=FREE,
        compiler_params=params(14),
        name="near",
    )(*kept, *arrived)
    return [kept[0], kept[1], out, stat, kept[4], kept[5]]


def call_remote(kept, arrived):
    return pl.pallas_call(
        functools.partial(remote_kernel, False),
        out_shape=shape(ROWS, WIDTH),
        in_specs=[VMEM] * 7,
        out_specs=VMEM,
        scratch_shapes=[pltpu.VMEM((WIDTH, ROWS), BF16)],
        cost_estimate=FREE,
        compiler_params=params(14),
        name="remote",
    )(*kept, arrived)


def per_device(
    query_rows,
    key_rows,
    value_rows,
    patch_valid,
    segment_lengths,
    dilation,
    step_sizes,
    decay_rates,
    state_in,
    state_out,
    gate_in,
    skip_weight,
    norm_gain,
):
    count = lax.axis_size("seq")
    seq_rank = lax.axis_index("seq").astype(jnp.int32)
    rank = jnp.reshape(lax.axis_index("head").astype(jnp.int32), (1,))
    place = jnp.stack([seq_rank & 3, (seq_rank >> 2) & 3, seq_rank >> 4])
    valid = patch_valid.reshape(1, ROWS)
    gain = norm_gain.reshape(1, WIDTH)

    def cross(block, mask):
        return lax.ppermute(block, "seq", [(i, i ^ mask) for i in range(count)])

    def turn(block, step, span):
        unit = span // 4
        route = [(i, i // span * span + (i % span + step * unit) % span) for i in range(count)]
        return lax.ppermute(block, "seq", route)

    after = lax.optimization_barrier
    scan_inputs = (step_sizes, decay_rates, valid, state_in)

    pieces = call_state(value_rows, *scan_inputs, place)
    packed = call_pack(key_rows, value_rows, after((valid, pieces))[0])
    pieces = [pieces[0]] + [cross(pieces[mask], mask) for mask in range(1, SPAN_DEV)]
    near = [cross(packed, 1)]
    pieces = after((pieces, packed))[0]
    total, block_before, block_fade = call_block(place, *pieces)
    totals = [total] + [turn(total, step, 16) for step in range(1, 4)]
    packed, totals = after((packed, totals))
    near.append(cross(packed, 2))
    far = cross(packed, 3)
    total, line_before, line_fade = call_line(place, *totals)
    kept = call_local(
        query_rows, key_rows, value_rows, after((valid, total))[0], segment_lengths, dilation, rank
    )
    totals = [total] + [turn(total, step, 64) for step in range(1, 4)]
    totals = after((totals, kept))[0]
    carried = call_plane(place, *totals, line_before, line_fade, block_before, block_fade)
    scan_inputs = (*scan_inputs[:2], after((valid, carried))[0], state_in)
    within = call_within(value_rows, gate_in, *scan_inputs, state_out, skip_weight)
    carried = [carried[0]] + [cross(carried[mask], mask) for mask in range(1, SPAN_DEV)]
    kept = call_near(after((kept, within))[0], near)
    carried = after((carried, kept))[0]
    scanned = call_finish(place, *carried, state_out, *within, gain)
    attended = call_remote(kept, far)
    return (attended, scanned)


def solution(mesh):
    return jax.shard_map(
        per_device,
        mesh=mesh,
        in_specs=(
            P(("slide", "seq"), "head"),
            P(("slide", "seq"), "head"),
            P(("slide", "seq"), "head"),
            P(("slide", "seq")),
            P(),
            P(),
            P("head", ("slide", "seq")),
            P("head", ("slide", "seq")),
            P(("slide", "seq"), None),
            P(("slide", "seq"), None),
            P(("slide", "seq"), "head"),
            P("head"),
            P("head"),
        ),
        out_specs=(P(("slide", "seq"), "head"), P(("slide", "seq"), "head")),
        check_vma=False,
    )
```

```python
import functools
import math

import jax
import jax.numpy as jnp
import numpy as np
from jax import lax
from jax.experimental import pallas as pl
from jax.experimental.pallas import tpu as pltpu
from jax.sharding import PartitionSpec as P

HEAD_DIM = 64
STATE = 128
HEADS_PER_GROUP = 6
SPAN_DEV = 4
ROWS = 512
HALF = 256
PAIRS = 6
HEADS_HERE = 12
QUARTER = 192
WIDTH = HEADS_HERE * HEAD_DIM
PIECE = 208
NEG = -1e30
F32 = jnp.float32
BF16 = jnp.bfloat16

LN2_HI = float(np.float32(jnp.bfloat16(math.log(2.0))))
LN2_LO = float(np.float32(jnp.bfloat16(math.log(2.0) - LN2_HI)))
LN3_HI = float(np.float32(jnp.bfloat16(math.log(3.0))))
LN3_LO = float(np.float32(jnp.bfloat16(math.log(3.0) - LN3_HI)))

VMEM = pl.BlockSpec(memory_space=pltpu.VMEM)
SMEM = pl.BlockSpec(memory_space=pltpu.SMEM)


def iota(shape, dim):
    return lax.broadcasted_iota(jnp.int32, shape, dim)


def dot(a, b):
    return lax.dot_general(a, b, (((1,), (0,)), ((), ())), preferred_element_type=F32)


def dot_t(a, b):
    return lax.dot_general(a, b, (((1,), (1,)), ((), ())), preferred_element_type=F32)


def t_dot(a, b):
    return lax.dot_general(a, b, (((0,), (0,)), ((), ())), preferred_element_type=F32)


def one(mask, kind=F32):
    return jnp.where(mask, 1.0, 0.0).astype(kind)


def residue_of(block):
    return ((block & 1) << 2) | (block & 2) | (block >> 2)


def sorting():
    row = iota((ROWS, ROWS), 0)
    token = 8 * (row & 63) + residue_of(row >> 6)
    return one(iota((ROWS, ROWS), 1) == token, BF16)


def unsorting():
    column = iota((ROWS, ROWS), 1)
    token = 8 * (column & 63) + residue_of(column >> 6)
    return one(iota((ROWS, ROWS), 0) == token, BF16)


def split(x, parts):
    out = []
    for _ in range(parts):
        head = x.astype(BF16)
        out.append(head)
        x = x - head.astype(F32)
    return out


FREE = pl.CostEstimate(flops=1, bytes_accessed=1, transcendentals=0)


def params(mib=8):
    return pltpu.CompilerParams(vmem_limit_bytes=mib * 1024 * 1024)


def pack_kernel(k_ref, v_ref, valid_ref, out_ref):
    sort = sorting()
    unsort = unsorting()
    low = (iota((HALF, WIDTH), 1) & 127) < HEAD_DIM
    rows = dot(sort, k_ref[...])
    out_ref[:HALF, :] = jnp.where(low, rows[:HALF], rows[HALF:]).astype(BF16)
    columns = t_dot(v_ref[...], unsort)
    even = (iota((WIDTH, HALF), 0) & 127) < HEAD_DIM
    columns = jnp.where(even, columns[:, :HALF], columns[:, HALF:]).astype(BF16)
    for at in range(0, WIDTH, HALF):
        out_ref[HALF:ROWS, at : at + HALF] = columns[at : at + HALF]
    valid = jnp.broadcast_to(valid_ref[...].astype(F32), (16, ROWS)).astype(BF16)
    line = dot_t(valid, sort)
    out_ref[ROWS : ROWS + 16, :] = jnp.concatenate(
        [line, jnp.zeros((16, WIDTH - ROWS), F32)], axis=1
    ).astype(BF16)


def log_count(count):
    high = jnp.where(count == 0, NEG, jnp.where(count == 2, LN2_HI, jnp.where(count == 3, LN3_HI, 0.0)))
    low = jnp.where(count == 2, LN2_LO, jnp.where(count == 3, LN3_LO, 0.0))
    return high, low


def plan_of(head, seg_ref, dil_ref):
    group = head // HEADS_PER_GROUP
    return dil_ref[group, 1], dil_ref[group, 2], seg_ref[group, 0], seg_ref[group, 1]


def local_plan(head, seg_ref, dil_ref):
    r1, r2, w0, w1 = plan_of(head, seg_ref, dil_ref)
    key, query = iota((16, ROWS), 0), iota((16, ROWS), 1) >> 5
    same = (key & 1) == (query & 1)
    key_off, query_off = residue_of(key >> 1) - head, residue_of(query >> 1) - head

    def on(stride):
        return (key_off & (stride - 1)) + (query_off & (stride - 1)) == 0

    count = one(same | (w0 >= ROWS)) + one(on(r1) & (same | (w1 >= ROWS))) + one(on(r2))
    return jnp.concatenate([*log_count(count), jnp.ones((16, ROWS), F32)], axis=0)


def remote_plan(head, seg_ref, dil_ref):
    r1, r2, _, w1 = plan_of(head, seg_ref, dil_ref)
    row = iota((8, HALF), 0)
    shift = (head & 1) - head
    key_off = residue_of(row & 3) + shift
    query_off = residue_of(iota((8, HALF), 1) >> 6) + shift

    def on(stride):
        return (key_off & (stride - 1)) + (query_off & (stride - 1)) == 0

    parts = []
    for reach in (2 * ROWS, 4 * ROWS):
        high, low = log_count(one(on(r1) & (w1 >= reach)) + one(on(r2)))
        parts.append(jnp.where(row < 4, high, low))
    return jnp.concatenate(parts + [jnp.ones((16, HALF), F32)], axis=0)


def own_bias(head, dil_ref):
    group = head // HEADS_PER_GROUP
    off = residue_of(iota((1, ROWS), 1) >> 6) - head
    count = 1 + jnp.where((off & (dil_ref[group, 1] - 1)) == 0, 1, 0)
    count = count + jnp.where((off & (dil_ref[group, 2] - 1)) == 0, 1, 0)
    return jnp.where(count == 1, 0.0, jnp.where(count == 2, LN2_HI + LN2_LO, LN3_HI + LN3_LO))


def staggered(jobs, depth=2):
    waiting = []
    for keys, queries, finish in jobs:
        waiting.append((finish, dot(keys(), queries())))
        if len(waiting) > depth:
            finish, scores = waiting.pop(0)
            finish(scores)
    for finish, scores in waiting:
        finish(scores)


def softmax_columns(scores, values, own, before):
    if own is not None:
        tile = 128
        diagonal = iota((tile, tile), 0) == iota((tile, tile), 1)
        rows = []
        for at in range(0, scores.shape[0], tile):
            line = scores[at : at + tile]
            here = jnp.where(diagonal, own[:, at : at + tile], line[:, at : at + tile])
            parts = [line[:, :at], here, line[:, at + tile :]]
            rows.append(jnp.concatenate([x for x in parts if x.shape[1]], axis=1))
        scores = jnp.concatenate(rows, axis=0)
    top = jnp.max(scores, axis=0, keepdims=True)
    if before is not None:
        top = jnp.maximum(top, before)
    values = jnp.concatenate([values, jnp.ones((16, values.shape[1]), BF16)], axis=0)
    out = dot(values, jnp.exp(scores - top).astype(BF16))
    return out[:HEAD_DIM], out[HEAD_DIM : HEAD_DIM + 1], top


def all_queries(rows, part, plan):
    rest = jnp.zeros((HEAD_DIM - plan.shape[0], rows.shape[1]), BF16)
    pieces = [plan.astype(BF16), rest]
    return jnp.concatenate([rows] + pieces if part == 0 else pieces + [rows], axis=0)


def own_lanes(rows, part):
    lane = iota((rows, 128), 1)
    return one((lane < HEAD_DIM) == (part == 0), BF16)


def plan_lane(rows, part):
    return iota((rows, 128), 1) - (HEAD_DIM if part == 0 else 0)


def local_kernel(
    q_ref, k_ref, v_ref, valid_ref, seg_ref, dil_ref, rank_ref,
    qe_ref, plan_ref, oe_ref, stat_ref, oo_ref, ve_ref,
    unsort_ref, sq_ref, sk_ref, sv_ref,
):
    unsort_ref[...] = unsorting()
    valid = jnp.broadcast_to(valid_ref[...].astype(F32), (128, ROWS)).astype(BF16)
    flags = dot(valid, unsort_ref[...])
    ve_ref[...] = flags[:8]
    row = iota((ROWS, 128), 0)
    hidden = (1.0 - flags.T) * NEG
    sides, masks = [], []
    for part in range(2):
        lane = plan_lane(ROWS, part)
        side = one(((row >> 5) == (lane & 15)) & (lane >= 0) & (lane < 32))
        sides.append(jnp.where(lane == 32, hidden, side).astype(BF16))
        masks.append(own_lanes(ROWS, part))
    sq_ref[...] = t_dot(q_ref[...], unsort_ref[...]) * (HEAD_DIM**-0.5)
    sk_ref[...] = t_dot(k_ref[...], unsort_ref[...])
    sv_ref[...] = t_dot(v_ref[...], unsort_ref[...]).astype(BF16)
    def job(pair, part):
        both = slice(pair * 128, (pair + 1) * 128)
        head = rank_ref[0] * HEADS_HERE + 2 * pair + part
        start = pair * 128 + part * HEAD_DIM
        now = slice(start, start + HEAD_DIM)
        inside = slice(part * HALF, (part + 1) * HALF)
        outside = slice((1 - part) * HALF, (2 - part) * HALF)

        def keys():
            return sk_ref[both, :].T.astype(BF16) * masks[part] + sides[part]

        def queries():
            return all_queries(sq_ref[now, :].astype(BF16), part, local_plan(head, seg_ref, dil_ref))

        def finish(scores):
            query = sq_ref[now, :]
            own = jnp.sum(query * sk_ref[now, :], axis=0, keepdims=True) + own_bias(head, dil_ref)
            out, total, top = softmax_columns(scores, sv_ref[now, :], own, None)
            qe_ref[now, :] = query[:, inside].astype(BF16)
            oe_ref[now, :] = out[:, inside]
            oo_ref[now, :] = (out[:, outside] / total[:, outside] * flags[:1, outside]).astype(BF16)
            at = (2 * pair + part) * 32
            plan_ref[at : at + 32, :] = remote_plan(head, seg_ref, dil_ref).astype(BF16)
            stat = pair * 8 + 2 * part
            stat_ref[stat : stat + 1, :] = top[:, inside]
            stat_ref[stat + 1 : stat + 2, :] = total[:, inside]

        return keys, queries, finish

    staggered([job(pair, part) for pair in range(PAIRS) for part in range(2)])


def remote_kernel(near, qe_ref, plan_ref, oe_ref, stat_ref, oo_ref, ve_ref, *rest):
    blocks, outs = (rest[:2], rest[2:]) if near else (rest[:1], rest[1:])
    row = iota((HALF, 128), 0)
    sides, masks = [], []
    for part in range(2):
        lane = plan_lane(HALF, part)
        first = one((iota((16, 128), 0) == 0) & (plan_lane(16, part) == 16), BF16)
        same = ((lane & 3) == (row >> 6)) & (lane >= 0)
        close, distant = one(same & (lane < 8)), one(same & (lane >= 8) & (lane < 16))
        pieces = []
        for ref, group in zip(blocks, (close, distant) if near else (distant,)):
            flags = ref[ROWS : ROWS + 16, part * HALF : (part + 1) * HALF].astype(F32)
            pieces.append(t_dot(((1.0 - flags) * NEG).astype(BF16), first) + group)
        sides.append(jnp.concatenate(pieces, axis=0).astype(BF16))
        masks.append(own_lanes(HALF * len(blocks), part))
    def job(pair, part):
        both = slice(pair * 128, (pair + 1) * 128)
        start = pair * 128 + part * HEAD_DIM
        now = slice(start, start + HEAD_DIM)
        place = start % HALF + HALF
        place = slice(place, place + HEAD_DIM)
        chunk = slice((pair >> 1) * HALF, (pair >> 1) * HALF + HALF)
        at = (2 * pair + part) * 32
        stat = pair * 8 + 2 * part

        def keys():
            key = jnp.concatenate([ref[:HALF, both] for ref in blocks], axis=0)
            return key * masks[part] + sides[part]

        def queries():
            return all_queries(qe_ref[now, :], part, plan_ref[at : at + 32, :])

        def finish(scores):
            value = jnp.concatenate([ref[place, chunk] for ref in blocks], axis=1)
            before = stat_ref[stat : stat + 1, :]
            out, total, top = softmax_columns(scores, value, None, before)
            rescale = jnp.exp(before - top)
            out = out + oe_ref[now, :] * rescale
            total = total + stat_ref[stat + 1 : stat + 2, :] * rescale
            if near:
                outs[0][now, :] = out
                outs[1][stat : stat + 1, :] = top
                outs[1][stat + 1 : stat + 2, :] = total
                return
            done = out / total * ve_ref[:1, part * HALF : (part + 1) * HALF]
            outs[1][now, part * HALF : (part + 1) * HALF] = done.astype(BF16)
            outs[1][now, (1 - part) * HALF : (2 - part) * HALF] = oo_ref[now, :]

        return keys, queries, finish

    staggered([job(pair, part) for pair in range(PAIRS) for part in range(2)])
    if not near:
        outs[0][...] = dot_t(unsorting(), outs[1][...]).astype(BF16)


def state_kernel(v_hbm, steps_hbm, rates_hbm, valid_hbm, into_hbm, place_ref, *rest):
    out_refs = rest[:4]
    full_ref, v_ref, steps_ref, rates_ref, valid_ref, into_ref, arrived = rest[4:]
    copies = [
        pltpu.make_async_copy(source, target, arrived.at[at])
        for at, (source, target) in enumerate(
            (
                (rates_hbm, rates_ref),
                (steps_hbm, steps_ref),
                (valid_hbm, valid_ref),
                (into_hbm, into_ref),
                (v_hbm, v_ref),
            )
        )
    ]
    for copy in copies:
        copy.start()
    for copy in copies[:3]:
        copy.wait()
    later = one(iota((ROWS, ROWS), 0) > iota((ROWS, ROWS), 1), BF16)
    rates = jnp.concatenate([rates_ref[...], jnp.zeros((4, ROWS), F32)], axis=0)
    sums = dot(jnp.concatenate(split(rates, 3), axis=0), later)
    to_end = sums[:16] + sums[16:32] + sums[32:]
    steps = jnp.concatenate([steps_ref[...], jnp.zeros((4, ROWS), F32)], axis=0)
    weight = jnp.exp(-to_end) * steps * valid_ref[...].astype(F32)
    width = HEADS_HERE * HEAD_DIM
    spread = one((iota((32, width), 0) & 15) == (iota((32, width), 1) >> 6), BF16)
    scale = t_dot(jnp.concatenate(split(weight, 2), axis=0), spread)
    for copy in copies[3:]:
        copy.wait()
    driven = (v_ref[...].astype(F32) * scale).astype(BF16)
    full_ref[...] = t_dot(driven, into_ref[...])
    decay = jnp.exp(-jnp.sum(rates, axis=1, keepdims=True))
    decay = jnp.concatenate(split(jnp.broadcast_to(decay, (16, STATE)), 2), axis=0)
    row, source = iota((16, 32), 0), iota((16, 32), 1)
    for step in range(4):
        part = place_ref[0] ^ step
        wanted = jnp.where(row < 3, part * 3 + row, jnp.where(row < 6, 13 + part * 3 + row, -1))
        start = pl.multiple_of(part * QUARTER, 64)
        out_refs[step][:QUARTER, :] = full_ref[pl.ds(start, QUARTER), :].astype(BF16)
        out_refs[step][QUARTER:, :] = dot(one(source == wanted, BF16), decay).astype(BF16)


def decay_rows(ref_value):
    tail = ref_value[QUARTER:].astype(F32)
    return [tail[k : k + 1] + tail[k + 3 : k + 4] for k in range(3)]


def tall(decays):
    return jnp.concatenate(decays + [jnp.zeros((5, STATE), F32)], axis=0)


def spread_rows(decays):
    return jnp.concatenate([jnp.broadcast_to(d, (HEAD_DIM, STATE)) for d in decays], axis=0)


def pack_piece(state, decays):
    high, low = zip(*(split(d, 2) for d in decays))
    tail = jnp.concatenate(
        [d.astype(F32) for d in high + low] + [jnp.zeros((10, STATE), F32)], axis=0
    )
    return jnp.concatenate([state, tail], axis=0).astype(BF16)


def block_kernel(place_ref, a0, a1, a2, a3, total_ref, before_ref, fade_ref, held):
    for step, ref in enumerate((a0, a1, a2, a3)):
        held[place_ref[0] ^ step] = ref[...].astype(F32)
    state = jnp.zeros((QUARTER, STATE), F32)
    decays = [jnp.ones((1, STATE), F32)] * 3
    for at in range(4):
        before_ref[at] = state
        fade_ref[at] = tall(decays)
        now = decay_rows(held[at])
        state = state * spread_rows(now) + held[at, :QUARTER, :]
        decays = [a * b for a, b in zip(decays, now)]
    total_ref[...] = pack_piece(state, decays)


def chain(place, held):
    state = jnp.zeros((QUARTER, STATE), F32)
    decays = [jnp.ones((1, STATE), F32)] * 3
    before, before_decays = state, decays
    for at in range(4):
        here = place == at
        before = jnp.where(here, state, before)
        before_decays = [jnp.where(here, a, b) for a, b in zip(decays, before_decays)]
        now = decay_rows(held[at])
        state = state * spread_rows(now) + held[at, :QUARTER, :]
        decays = [a * b for a, b in zip(decays, now)]
    return before, before_decays, state, decays


def line_kernel(place_ref, a0, a1, a2, a3, total_ref, before_ref, fade_ref, held):
    for step, ref in enumerate((a0, a1, a2, a3)):
        held[(place_ref[1] - step) & 3] = ref[...].astype(F32)
    before, before_decays, state, decays = chain(place_ref[1], held)
    before_ref[...] = before
    fade_ref[...] = tall(before_decays)
    total_ref[...] = pack_piece(state, decays)


def plane_kernel(place_ref, a0, a1, a2, a3, line_before, line_fade, block_before, block_fade, *rest):
    outs, held = rest[:4], rest[4]
    for step, ref in enumerate((a0, a1, a2, a3)):
        held[(place_ref[2] - step) & 3] = ref[...].astype(F32)
    before = chain(place_ref[2], held)[0]
    start = spread_rows([line_fade[k : k + 1, :] for k in range(3)]) * before + line_before[...]
    for step in range(4):
        part = place_ref[0] ^ step
        fade = block_fade[part]
        fade = spread_rows([fade[k : k + 1] for k in range(3)])
        outs[step][...] = (fade * start + block_before[part]).astype(BF16)


def within_kernel(
    v_ref, gate_ref, steps_ref, rates_ref, valid_ref, into_ref, read_ref, skip_ref,
    base_ref, lift_ref, couple_ref, col_ref, row_ref,
):
    pair = pl.program_id(0)

    @pl.when(pair == 0)
    def _():
        couple_ref[...] = dot_t(read_ref[...], into_ref[...])
        upto = one(iota((ROWS, ROWS), 0) <= iota((ROWS, ROWS), 1), BF16)
        rates = jnp.concatenate([rates_ref[...], jnp.zeros((4, ROWS), F32)], axis=0)
        sums = dot(jnp.concatenate(split(rates, 3), axis=0), upto)
        fall = -(sums[:16] + sums[16:32] + sums[32:])
        steps = jnp.concatenate([steps_ref[...], jnp.ones((4, ROWS), F32)], axis=0)
        col_ref[...] = fall
        row_ref[...] = jnp.where(valid_ref[...] > 0, fall - jnp.log(steps), -NEG)

    value = v_ref[...]
    lane = iota((ROWS, 128), 1)
    results = []
    falls = []
    tile = 128
    causal = iota((tile, tile), 0) >= iota((tile, tile), 1)
    for part in range(2):
        head = 2 * pair + part
        fall = jnp.broadcast_to(col_ref[pl.ds(head, 1), :], (128, ROWS)).T
        line = row_ref[pl.ds(head, 1), :]
        pieces = []
        for at in range(ROWS // tile):
            fall_now = fall[at * tile : (at + 1) * tile]
            weights = []
            for src in range(at + 1):
                gap = fall_now - line[:, src * tile : (src + 1) * tile]
                if src == at:
                    gap = jnp.where(causal, gap, NEG)
                weights.append(
                    (
                        jnp.exp(gap)
                        * couple_ref[at * tile : (at + 1) * tile, src * tile : (src + 1) * tile]
                    ).astype(BF16)
                )
            pieces.append(dot(jnp.concatenate(weights, axis=1), value[: (at + 1) * tile]))
        results.append(jnp.concatenate(pieces, axis=0))
        falls.append(fall)
    low = lane < HEAD_DIM
    gate = gate_ref[...].astype(F32)
    gate = gate / (1.0 + jnp.exp(-gate))
    skip = jnp.where(low, skip_ref[2 * pair], skip_ref[2 * pair + 1])
    within = jnp.where(low, results[0], results[1])
    base_ref[...] = ((within + skip * value.astype(F32)) * gate).astype(BF16)
    lift_ref[...] = (jnp.exp(jnp.where(low, falls[0], falls[1])) * gate).astype(BF16)


def finish_kernel(place_ref, f0, f1, f2, f3, read_ref, base_ref, lift_ref, gain_ref, out_ref, held):
    @pl.when(pl.program_id(0) == 0)
    def _():
        for step, ref in enumerate((f0, f1, f2, f3)):
            part = place_ref[0] ^ step
            held[pl.ds(pl.multiple_of(part * QUARTER, 64), QUARTER), :] = ref[...]

    together = one((iota((128, 128), 0) >> 6) == (iota((128, 128), 1) >> 6), BF16)
    pairs = [slice(pair * 128, (pair + 1) * 128) for pair in range(PAIRS)]
    carried = [dot_t(read_ref[...], held[now, :]) for now in pairs]
    gated = [
        base_ref[:, now].astype(F32) + lift_ref[:, now].astype(F32) * state
        for now, state in zip(pairs, carried)
    ]
    squares = [split(x * x, 2) for x in gated]
    means = [(dot(high, together) + dot(low, together)) * (1.0 / HEAD_DIM) for high, low in squares]
    for now, x, mean in zip(pairs, gated, means):
        out_ref[:, now] = (x * lax.rsqrt(mean + 1e-05) * gain_ref[:, now]).astype(BF16)


def shape(*dims, kind=BF16):
    return jax.ShapeDtypeStruct(dims, kind)


def lanes(rows, row_block=0):
    return pl.BlockSpec((rows, 128), lambda pair: (row_block, pair))


def whole(*dims):
    return pl.BlockSpec(dims, lambda pair: (0,) * len(dims))


def call_pack(key_rows, value_rows, valid):
    return pl.pallas_call(
        pack_kernel,
        out_shape=shape(ROWS + 16, WIDTH),
        in_specs=[VMEM] * 3,
        out_specs=VMEM,
        cost_estimate=FREE,
        compiler_params=params(),
        name="pack",
    )(key_rows, value_rows, valid)


def call_state(*args):
    far = pl.BlockSpec(memory_space=pltpu.HBM)
    return pl.pallas_call(
        state_kernel,
        out_shape=[shape(PIECE, STATE)] * 4,
        in_specs=[far] * 5 + [SMEM],
        out_specs=[VMEM] * 4,
        scratch_shapes=[
            pltpu.VMEM((WIDTH, STATE), F32),
            pltpu.VMEM((ROWS, WIDTH), BF16),
            pltpu.VMEM((HEADS_HERE, ROWS), F32),
            pltpu.VMEM((HEADS_HERE, ROWS), F32),
            pltpu.VMEM((1, ROWS), jnp.int32),
            pltpu.VMEM((ROWS, STATE), BF16),
            pltpu.SemaphoreType.DMA((5,)),
        ],
        cost_estimate=FREE,
        compiler_params=params(58),
        name="state",
    )(*args)


HOLD = [pltpu.VMEM((4, PIECE, STATE), F32)]


def call_block(place, *pieces):
    return pl.pallas_call(
        block_kernel,
        out_shape=[shape(PIECE, STATE), shape(4, QUARTER, STATE, kind=F32), shape(4, 8, STATE, kind=F32)],
        in_specs=[SMEM] + [VMEM] * 4,
        out_specs=[VMEM] * 3,
        scratch_shapes=HOLD,
        cost_estimate=FREE,
        compiler_params=params(),
        name="block",
    )(place, *pieces)


def call_line(place, *totals):
    return pl.pallas_call(
        line_kernel,
        out_shape=[shape(PIECE, STATE), shape(QUARTER, STATE, kind=F32), shape(8, STATE, kind=F32)],
        in_specs=[SMEM] + [VMEM] * 4,
        out_specs=[VMEM] * 3,
        scratch_shapes=HOLD,
        cost_estimate=FREE,
        compiler_params=params(),
        name="line",
    )(place, *totals)


def call_plane(place, *args):
    return pl.pallas_call(
        plane_kernel,
        out_shape=[shape(QUARTER, STATE)] * 4,
        in_specs=[SMEM] + [VMEM] * 8,
        out_specs=[VMEM] * 4,
        scratch_shapes=HOLD,
        cost_estimate=FREE,
        compiler_params=params(),
        name="plane",
    )(place, *args)


KEPT = [
    shape(WIDTH, HALF),
    shape(HEADS_HERE * 32, HALF),
    shape(WIDTH, HALF, kind=F32),
    shape(8 * PAIRS, HALF, kind=F32),
    shape(WIDTH, HALF),
    shape(8, ROWS, kind=F32),
]


def call_local(*args):
    return pl.pallas_call(
        local_kernel,
        out_shape=KEPT,
        in_specs=[VMEM] * 4 + [SMEM] * 3,
        out_specs=[VMEM] * 6,
        scratch_shapes=[
            pltpu.VMEM((ROWS, ROWS), BF16),
            pltpu.VMEM((WIDTH, ROWS), F32),
            pltpu.VMEM((WIDTH, ROWS), F32),
            pltpu.VMEM((WIDTH, ROWS), BF16),
        ],
        cost_estimate=FREE,
        compiler_params=params(14),
        name="local",
    )(*args)


def call_within(*args):
    return pl.pallas_call(
        within_kernel,
        grid=(PAIRS,),
        out_shape=[shape(ROWS, WIDTH)] * 2,
        in_specs=[lanes(ROWS)] * 2
        + [whole(HEADS_HERE, ROWS)] * 2
        + [whole(1, ROWS), whole(ROWS, STATE), whole(ROWS, STATE), SMEM],
        out_specs=[lanes(ROWS)] * 2,
        scratch_shapes=[pltpu.VMEM((ROWS, ROWS), F32), pltpu.VMEM((16, ROWS), F32), pltpu.VMEM((16, ROWS), F32)],
        cost_estimate=FREE,
        compiler_params=params(8),
        name="within",
    )(*args)


def call_finish(*args):
    def rows(width):
        return pl.BlockSpec((HALF, width), lambda at: (at, 0))

    return pl.pallas_call(
        finish_kernel,
        grid=(ROWS // HALF,),
        out_shape=shape(ROWS, WIDTH),
        in_specs=[SMEM]
        + [whole(QUARTER, STATE)] * 4
        + [rows(STATE)]
        + [rows(WIDTH)] * 2
        + [whole(1, WIDTH)],
        out_specs=rows(WIDTH),
        scratch_shapes=[pltpu.VMEM((WIDTH, STATE), BF16)],
        cost_estimate=FREE,
        compiler_params=params(),
        name="finish",
    )(*args)


def call_near(kept, arrived):
    out, stat = pl.pallas_call(
        functools.partial(remote_kernel, True),
        out_shape=[KEPT[2], KEPT[3]],
        in_specs=[VMEM] * 8,
        out_specs=[VMEM] * 2,
        cost_estimate=FREE,
        compiler_params=params(14),
        name="near",
    )(*kept, *arrived)
    return [kept[0], kept[1], out, stat, kept[4], kept[5]]


def call_remote(kept, arrived):
    return pl.pallas_call(
        functools.partial(remote_kernel, False),
        out_shape=shape(ROWS, WIDTH),
        in_specs=[VMEM] * 7,
        out_specs=VMEM,
        scratch_shapes=[pltpu.VMEM((WIDTH, ROWS), BF16)],
        cost_estimate=FREE,
        compiler_params=params(14),
        name="remote",
    )(*kept, arrived)


def per_device(
    query_rows,
    key_rows,
    value_rows,
    patch_valid,
    segment_lengths,
    dilation,
    step_sizes,
    decay_rates,
    state_in,
    state_out,
    gate_in,
    skip_weight,
    norm_gain,
):
    count = lax.axis_size("seq")
    seq_rank = lax.axis_index("seq").astype(jnp.int32)
    rank = jnp.reshape(lax.axis_index("head").astype(jnp.int32), (1,))
    place = jnp.stack([seq_rank & 3, (seq_rank >> 2) & 3, seq_rank >> 4])
    valid = patch_valid.reshape(1, ROWS)
    gain = norm_gain.reshape(1, WIDTH)

    def cross(block, mask):
        return lax.ppermute(block, "seq", [(i, i ^ mask) for i in range(count)])

    def turn(block, step, span):
        unit = span // 4
        route = [(i, i // span * span + (i % span + step * unit) % span) for i in range(count)]
        return lax.ppermute(block, "seq", route)

    after = lax.optimization_barrier
    scan_inputs = (step_sizes, decay_rates, valid, state_in)

    pieces = call_state(value_rows, *scan_inputs, place)
    packed = call_pack(key_rows, value_rows, after((valid, pieces))[0])
    pieces = [pieces[0]] + [cross(pieces[mask], mask) for mask in range(1, SPAN_DEV)]
    near = [cross(packed, 1)]
    pieces = after((pieces, packed))[0]
    total, block_before, block_fade = call_block(place, *pieces)
    totals = [total] + [turn(total, step, 16) for step in range(1, 4)]
    packed, totals = after((packed, totals))
    near.append(cross(packed, 2))
    far = cross(packed, 3)
    total, line_before, line_fade = call_line(place, *totals)
    kept = call_local(
        query_rows, key_rows, value_rows, after((valid, total))[0], segment_lengths, dilation, rank
    )
    totals = [total] + [turn(total, step, 64) for step in range(1, 4)]
    totals = after((totals, kept))[0]
    carried = call_plane(place, *totals, line_before, line_fade, block_before, block_fade)
    scan_inputs = (*scan_inputs[:2], after((valid, carried))[0], state_in)
    within = call_within(value_rows, gate_in, *scan_inputs, state_out, skip_weight)
    carried = [carried[0]] + [cross(carried[mask], mask) for mask in range(1, SPAN_DEV)]
    kept = call_near(after((kept, within))[0], near)
    carried = after((carried, kept))[0]
    scanned = call_finish(place, *carried, state_out, *within, gain)
    attended = call_remote(kept, far)
    return (attended, scanned)


def solution(mesh):
    return jax.shard_map(
        per_device,
        mesh=mesh,
        in_specs=(
            P(("slide", "seq"), "head"),
            P(("slide", "seq"), "head"),
            P(("slide", "seq"), "head"),
            P(("slide", "seq")),
            P(),
            P(),
            P("head", ("slide", "seq")),
            P("head", ("slide", "seq")),
            P(("slide", "seq"), None),
            P(("slide", "seq"), None),
            P(("slide", "seq"), "head"),
            P("head"),
            P("head"),
        ),
        out_specs=(P(("slide", "seq"), "head"), P(("slide", "seq"), "head")),
        check_vma=False,
    )
```

```python
import functools
import math

import jax
import jax.numpy as jnp
import numpy as np
from jax import lax
from jax.experimental import pallas as pl
from jax.experimental.pallas import tpu as pltpu
from jax.sharding import PartitionSpec as P

HEAD_DIM = 64
STATE = 128
HEADS_PER_GROUP = 6
SPAN_DEV = 4
ROWS = 512
HALF = 256
PAIRS = 6
HEADS_HERE = 12
QUARTER = 192
WIDTH = HEADS_HERE * HEAD_DIM
PIECE = 208
NEG = -1e30
F32 = jnp.float32
BF16 = jnp.bfloat16

LN2_HI = float(np.float32(jnp.bfloat16(math.log(2.0))))
LN2_LO = float(np.float32(jnp.bfloat16(math.log(2.0) - LN2_HI)))
LN3_HI = float(np.float32(jnp.bfloat16(math.log(3.0))))
LN3_LO = float(np.float32(jnp.bfloat16(math.log(3.0) - LN3_HI)))

VMEM = pl.BlockSpec(memory_space=pltpu.VMEM)
SMEM = pl.BlockSpec(memory_space=pltpu.SMEM)


def iota(shape, dim):
    return lax.broadcasted_iota(jnp.int32, shape, dim)


def dot(a, b):
    return lax.dot_general(a, b, (((1,), (0,)), ((), ())), preferred_element_type=F32)


def dot_t(a, b):
    return lax.dot_general(a, b, (((1,), (1,)), ((), ())), preferred_element_type=F32)


def t_dot(a, b):
    return lax.dot_general(a, b, (((0,), (0,)), ((), ())), preferred_element_type=F32)


def one(mask, kind=F32):
    return jnp.where(mask, 1.0, 0.0).astype(kind)


def residue_of(block):
    return ((block & 1) << 2) | (block & 2) | (block >> 2)


def sorting():
    row = iota((ROWS, ROWS), 0)
    token = 8 * (row & 63) + residue_of(row >> 6)
    return one(iota((ROWS, ROWS), 1) == token, BF16)


def unsorting():
    column = iota((ROWS, ROWS), 1)
    token = 8 * (column & 63) + residue_of(column >> 6)
    return one(iota((ROWS, ROWS), 0) == token, BF16)


def split(x, parts):
    out = []
    for _ in range(parts):
        head = x.astype(BF16)
        out.append(head)
        x = x - head.astype(F32)
    return out


FREE = pl.CostEstimate(flops=1, bytes_accessed=1, transcendentals=0)


def params(mib=8):
    return pltpu.CompilerParams(vmem_limit_bytes=mib * 1024 * 1024)


def pack_kernel(k_ref, v_ref, valid_ref, out_ref):
    sort = sorting()
    unsort = unsorting()
    low = (iota((HALF, WIDTH), 1) & 127) < HEAD_DIM
    rows = dot(sort, k_ref[...])
    out_ref[:HALF, :] = jnp.where(low, rows[:HALF], rows[HALF:]).astype(BF16)
    columns = t_dot(v_ref[...], unsort)
    even = (iota((WIDTH, HALF), 0) & 127) < HEAD_DIM
    columns = jnp.where(even, columns[:, :HALF], columns[:, HALF:]).astype(BF16)
    for at in range(0, WIDTH, HALF):
        out_ref[HALF:ROWS, at : at + HALF] = columns[at : at + HALF]
    valid = jnp.broadcast_to(valid_ref[...].astype(F32), (16, ROWS)).astype(BF16)
    line = dot_t(valid, sort)
    out_ref[ROWS : ROWS + 16, :] = jnp.concatenate(
        [line, jnp.zeros((16, WIDTH - ROWS), F32)], axis=1
    ).astype(BF16)


def log_count(count):
    high = jnp.where(count == 0, NEG, jnp.where(count == 2, LN2_HI, jnp.where(count == 3, LN3_HI, 0.0)))
    low = jnp.where(count == 2, LN2_LO, jnp.where(count == 3, LN3_LO, 0.0))
    return high, low


def plan_of(head, seg_ref, dil_ref):
    group = head // HEADS_PER_GROUP
    return dil_ref[group, 1], dil_ref[group, 2], seg_ref[group, 0], seg_ref[group, 1]


def local_plan(head, seg_ref, dil_ref):
    r1, r2, w0, w1 = plan_of(head, seg_ref, dil_ref)
    key, query = iota((16, ROWS), 0), iota((16, ROWS), 1) >> 5
    same = (key & 1) == (query & 1)
    key_off, query_off = residue_of(key >> 1) - head, residue_of(query >> 1) - head

    def on(stride):
        return (key_off & (stride - 1)) + (query_off & (stride - 1)) == 0

    count = one(same | (w0 >= ROWS)) + one(on(r1) & (same | (w1 >= ROWS))) + one(on(r2))
    return jnp.concatenate([*log_count(count), jnp.ones((16, ROWS), F32)], axis=0)


def remote_plan(head, seg_ref, dil_ref):
    r1, r2, _, w1 = plan_of(head, seg_ref, dil_ref)
    row = iota((8, HALF), 0)
    shift = (head & 1) - head
    key_off = residue_of(row & 3) + shift
    query_off = residue_of(iota((8, HALF), 1) >> 6) + shift

    def on(stride):
        return (key_off & (stride - 1)) + (query_off & (stride - 1)) == 0

    parts = []
    for reach in (2 * ROWS, 4 * ROWS):
        high, low = log_count(one(on(r1) & (w1 >= reach)) + one(on(r2)))
        parts.append(jnp.where(row < 4, high, low))
    return jnp.concatenate(parts + [jnp.ones((16, HALF), F32)], axis=0)


def own_bias(head, dil_ref):
    group = head // HEADS_PER_GROUP
    off = residue_of(iota((1, ROWS), 1) >> 6) - head
    count = 1 + jnp.where((off & (dil_ref[group, 1] - 1)) == 0, 1, 0)
    count = count + jnp.where((off & (dil_ref[group, 2] - 1)) == 0, 1, 0)
    return jnp.where(count == 1, 0.0, jnp.where(count == 2, LN2_HI + LN2_LO, LN3_HI + LN3_LO))


def staggered(jobs, depth=2):
    waiting = []
    for keys, queries, finish in jobs:
        waiting.append((finish, dot(keys(), queries())))
        if len(waiting) > depth:
            finish, scores = waiting.pop(0)
            finish(scores)
    for finish, scores in waiting:
        finish(scores)


def softmax_columns(scores, values, own, before):
    if own is not None:
        tile = 128
        diagonal = iota((tile, tile), 0) == iota((tile, tile), 1)
        rows = []
        for at in range(0, scores.shape[0], tile):
            line = scores[at : at + tile]
            here = jnp.where(diagonal, own[:, at : at + tile], line[:, at : at + tile])
            parts = [line[:, :at], here, line[:, at + tile :]]
            rows.append(jnp.concatenate([x for x in parts if x.shape[1]], axis=1))
        scores = jnp.concatenate(rows, axis=0)
    top = jnp.max(scores, axis=0, keepdims=True)
    if before is not None:
        top = jnp.maximum(top, before)
    values = jnp.concatenate([values, jnp.ones((16, values.shape[1]), BF16)], axis=0)
    out = dot(values, jnp.exp(scores - top).astype(BF16))
    return out[:HEAD_DIM], out[HEAD_DIM : HEAD_DIM + 1], top


def all_queries(rows, part, plan):
    rest = jnp.zeros((HEAD_DIM - plan.shape[0], rows.shape[1]), BF16)
    pieces = [plan.astype(BF16), rest]
    return jnp.concatenate([rows] + pieces if part == 0 else pieces + [rows], axis=0)


def own_lanes(rows, part):
    lane = iota((rows, 128), 1)
    return one((lane < HEAD_DIM) == (part == 0), BF16)


def plan_lane(rows, part):
    return iota((rows, 128), 1) - (HEAD_DIM if part == 0 else 0)


def local_kernel(
    q_ref, k_ref, v_ref, valid_ref, seg_ref, dil_ref, rank_ref,
    qe_ref, plan_ref, oe_ref, stat_ref, oo_ref, ve_ref,
    unsort_ref, sq_ref, sk_ref, sv_ref,
):
    unsort_ref[...] = unsorting()
    valid = jnp.broadcast_to(valid_ref[...].astype(F32), (128, ROWS)).astype(BF16)
    flags = dot(valid, unsort_ref[...])
    ve_ref[...] = flags[:8]
    row = iota((ROWS, 128), 0)
    hidden = (1.0 - flags.T) * NEG
    sides, masks = [], []
    for part in range(2):
        lane = plan_lane(ROWS, part)
        side = one(((row >> 5) == (lane & 15)) & (lane >= 0) & (lane < 32))
        sides.append(jnp.where(lane == 32, hidden, side).astype(BF16))
        masks.append(own_lanes(ROWS, part))
    sq_ref[...] = t_dot(q_ref[...], unsort_ref[...]) * (HEAD_DIM**-0.5)
    sk_ref[...] = t_dot(k_ref[...], unsort_ref[...])
    sv_ref[...] = t_dot(v_ref[...], unsort_ref[...]).astype(BF16)
    def job(pair, part):
        both = slice(pair * 128, (pair + 1) * 128)
        head = rank_ref[0] * HEADS_HERE + 2 * pair + part
        start = pair * 128 + part * HEAD_DIM
        now = slice(start, start + HEAD_DIM)
        inside = slice(part * HALF, (part + 1) * HALF)
        outside = slice((1 - part) * HALF, (2 - part) * HALF)

        def keys():
            return sk_ref[both, :].T.astype(BF16) * masks[part] + sides[part]

        def queries():
            return all_queries(sq_ref[now, :].astype(BF16), part, local_plan(head, seg_ref, dil_ref))

        def finish(scores):
            query = sq_ref[now, :]
            own = jnp.sum(query * sk_ref[now, :], axis=0, keepdims=True) + own_bias(head, dil_ref)
            out, total, top = softmax_columns(scores, sv_ref[now, :], own, None)
            qe_ref[now, :] = query[:, inside].astype(BF16)
            oe_ref[now, :] = out[:, inside]
            oo_ref[now, :] = (out[:, outside] / total[:, outside] * flags[:1, outside]).astype(BF16)
            at = (2 * pair + part) * 32
            plan_ref[at : at + 32, :] = remote_plan(head, seg_ref, dil_ref).astype(BF16)
            stat = pair * 8 + 2 * part
            stat_ref[stat : stat + 1, :] = top[:, inside]
            stat_ref[stat + 1 : stat + 2, :] = total[:, inside]

        return keys, queries, finish

    staggered([job(pair, part) for pair in range(PAIRS) for part in range(2)])


def remote_kernel(near, qe_ref, plan_ref, oe_ref, stat_ref, oo_ref, ve_ref, *rest):
    blocks, outs = (rest[:2], rest[2:]) if near else (rest[:1], rest[1:])
    row = iota((HALF, 128), 0)
    sides, masks = [], []
    for part in range(2):
        lane = plan_lane(HALF, part)
        first = one((iota((16, 128), 0) == 0) & (plan_lane(16, part) == 16), BF16)
        same = ((lane & 3) == (row >> 6)) & (lane >= 0)
        close, distant = one(same & (lane < 8)), one(same & (lane >= 8) & (lane < 16))
        pieces = []
        for ref, group in zip(blocks, (close, distant) if near else (distant,)):
            flags = ref[ROWS : ROWS + 16, part * HALF : (part + 1) * HALF].astype(F32)
            pieces.append(t_dot(((1.0 - flags) * NEG).astype(BF16), first) + group)
        sides.append(jnp.concatenate(pieces, axis=0).astype(BF16))
        masks.append(own_lanes(HALF * len(blocks), part))
    def job(pair, part):
        both = slice(pair * 128, (pair + 1) * 128)
        start = pair * 128 + part * HEAD_DIM
        now = slice(start, start + HEAD_DIM)
        place = start % HALF + HALF
        place = slice(place, place + HEAD_DIM)
        chunk = slice((pair >> 1) * HALF, (pair >> 1) * HALF + HALF)
        at = (2 * pair + part) * 32
        stat = pair * 8 + 2 * part

        def keys():
            key = jnp.concatenate([ref[:HALF, both] for ref in blocks], axis=0)
            return key * masks[part] + sides[part]

        def queries():
            return all_queries(qe_ref[now, :], part, plan_ref[at : at + 32, :])

        def finish(scores):
            value = jnp.concatenate([ref[place, chunk] for ref in blocks], axis=1)
            before = stat_ref[stat : stat + 1, :]
            out, total, top = softmax_columns(scores, value, None, before)
            rescale = jnp.exp(before - top)
            out = out + oe_ref[now, :] * rescale
            total = total + stat_ref[stat + 1 : stat + 2, :] * rescale
            if near:
                outs[0][now, :] = out
                outs[1][stat : stat + 1, :] = top
                outs[1][stat + 1 : stat + 2, :] = total
                return
            done = out / total * ve_ref[:1, part * HALF : (part + 1) * HALF]
            outs[1][now, part * HALF : (part + 1) * HALF] = done.astype(BF16)
            outs[1][now, (1 - part) * HALF : (2 - part) * HALF] = oo_ref[now, :]

        return keys, queries, finish

    staggered([job(pair, part) for pair in range(PAIRS) for part in range(2)])
    if not near:
        outs[0][...] = dot_t(unsorting(), outs[1][...]).astype(BF16)


def state_kernel(v_hbm, steps_hbm, rates_hbm, valid_hbm, into_hbm, place_ref, *rest):
    out_refs = rest[:4]
    full_ref, v_ref, steps_ref, rates_ref, valid_ref, into_ref, arrived = rest[4:]
    copies = [
        pltpu.make_async_copy(source, target, arrived.at[at])
        for at, (source, target) in enumerate(
            (
                (rates_hbm, rates_ref),
                (steps_hbm, steps_ref),
                (valid_hbm, valid_ref),
                (into_hbm, into_ref),
                (v_hbm, v_ref),
            )
        )
    ]
    for copy in copies:
        copy.start()
    for copy in copies[:3]:
        copy.wait()
    later = one(iota((ROWS, ROWS), 0) > iota((ROWS, ROWS), 1), BF16)
    rates = jnp.concatenate([rates_ref[...], jnp.zeros((4, ROWS), F32)], axis=0)
    sums = dot(jnp.concatenate(split(rates, 3), axis=0), later)
    to_end = sums[:16] + sums[16:32] + sums[32:]
    steps = jnp.concatenate([steps_ref[...], jnp.zeros((4, ROWS), F32)], axis=0)
    weight = jnp.exp(-to_end) * steps * valid_ref[...].astype(F32)
    width = HEADS_HERE * HEAD_DIM
    spread = one((iota((32, width), 0) & 15) == (iota((32, width), 1) >> 6), BF16)
    scale = t_dot(jnp.concatenate(split(weight, 2), axis=0), spread)
    for copy in copies[3:]:
        copy.wait()
    driven = (v_ref[...].astype(F32) * scale).astype(BF16)
    full_ref[...] = t_dot(driven, into_ref[...])
    decay = jnp.exp(-jnp.sum(rates, axis=1, keepdims=True))
    decay = jnp.concatenate(split(jnp.broadcast_to(decay, (16, STATE)), 2), axis=0)
    row, source = iota((16, 32), 0), iota((16, 32), 1)
    for step in range(4):
        part = place_ref[0] ^ step
        wanted = jnp.where(row < 3, part * 3 + row, jnp.where(row < 6, 13 + part * 3 + row, -1))
        start = pl.multiple_of(part * QUARTER, 64)
        out_refs[step][:QUARTER, :] = full_ref[pl.ds(start, QUARTER), :].astype(BF16)
        out_refs[step][QUARTER:, :] = dot(one(source == wanted, BF16), decay).astype(BF16)


def decay_rows(ref_value):
    tail = ref_value[QUARTER:].astype(F32)
    return [tail[k : k + 1] + tail[k + 3 : k + 4] for k in range(3)]


def tall(decays):
    return jnp.concatenate(decays + [jnp.zeros((5, STATE), F32)], axis=0)


def spread_rows(decays):
    return jnp.concatenate([jnp.broadcast_to(d, (HEAD_DIM, STATE)) for d in decays], axis=0)


def pack_piece(state, decays):
    high, low = zip(*(split(d, 2) for d in decays))
    tail = jnp.concatenate(
        [d.astype(F32) for d in high + low] + [jnp.zeros((10, STATE), F32)], axis=0
    )
    return jnp.concatenate([state, tail], axis=0).astype(BF16)


def block_kernel(place_ref, a0, a1, a2, a3, total_ref, before_ref, fade_ref, held):
    for step, ref in enumerate((a0, a1, a2, a3)):
        held[place_ref[0] ^ step] = ref[...].astype(F32)
    state = jnp.zeros((QUARTER, STATE), F32)
    decays = [jnp.ones((1, STATE), F32)] * 3
    for at in range(4):
        before_ref[at] = state
        fade_ref[at] = tall(decays)
        now = decay_rows(held[at])
        state = state * spread_rows(now) + held[at, :QUARTER, :]
        decays = [a * b for a, b in zip(decays, now)]
    total_ref[...] = pack_piece(state, decays)


def chain(place, held):
    state = jnp.zeros((QUARTER, STATE), F32)
    decays = [jnp.ones((1, STATE), F32)] * 3
    before, before_decays = state, decays
    for at in range(4):
        here = place == at
        before = jnp.where(here, state, before)
        before_decays = [jnp.where(here, a, b) for a, b in zip(decays, before_decays)]
        now = decay_rows(held[at])
        state = state * spread_rows(now) + held[at, :QUARTER, :]
        decays = [a * b for a, b in zip(decays, now)]
    return before, before_decays, state, decays


def line_kernel(place_ref, a0, a1, a2, a3, total_ref, before_ref, fade_ref, held):
    for step, ref in enumerate((a0, a1, a2, a3)):
        held[(place_ref[1] - step) & 3] = ref[...].astype(F32)
    before, before_decays, state, decays = chain(place_ref[1], held)
    before_ref[...] = before
    fade_ref[...] = tall(before_decays)
    total_ref[...] = pack_piece(state, decays)


def plane_kernel(place_ref, a0, a1, a2, a3, line_before, line_fade, block_before, block_fade, *rest):
    outs, held = rest[:4], rest[4]
    for step, ref in enumerate((a0, a1, a2, a3)):
        held[(place_ref[2] - step) & 3] = ref[...].astype(F32)
    before = chain(place_ref[2], held)[0]
    start = spread_rows([line_fade[k : k + 1, :] for k in range(3)]) * before + line_before[...]
    for step in range(4):
        part = place_ref[0] ^ step
        fade = block_fade[part]
        fade = spread_rows([fade[k : k + 1] for k in range(3)])
        outs[step][...] = (fade * start + block_before[part]).astype(BF16)


def within_kernel(
    v_ref, gate_ref, steps_ref, rates_ref, valid_ref, into_ref, read_ref, skip_ref,
    base_ref, lift_ref, couple_ref, col_ref, row_ref,
):
    pair = pl.program_id(0)

    @pl.when(pair == 0)
    def _():
        couple_ref[...] = dot_t(read_ref[...], into_ref[...])
        upto = one(iota((ROWS, ROWS), 0) <= iota((ROWS, ROWS), 1), BF16)
        rates = jnp.concatenate([rates_ref[...], jnp.zeros((4, ROWS), F32)], axis=0)
        sums = dot(jnp.concatenate(split(rates, 3), axis=0), upto)
        fall = -(sums[:16] + sums[16:32] + sums[32:])
        steps = jnp.concatenate([steps_ref[...], jnp.ones((4, ROWS), F32)], axis=0)
        col_ref[...] = fall
        row_ref[...] = jnp.where(valid_ref[...] > 0, fall - jnp.log(steps), -NEG)

    value = v_ref[...]
    lane = iota((ROWS, 128), 1)
    results = []
    falls = []
    tile = 128
    causal = iota((tile, tile), 0) >= iota((tile, tile), 1)
    for part in range(2):
        head = 2 * pair + part
        fall = jnp.broadcast_to(col_ref[pl.ds(head, 1), :], (128, ROWS)).T
        line = row_ref[pl.ds(head, 1), :]
        pieces = []
        for at in range(ROWS // tile):
            fall_now = fall[at * tile : (at + 1) * tile]
            weights = []
            for src in range(at + 1):
                gap = fall_now - line[:, src * tile : (src + 1) * tile]
                if src == at:
                    gap = jnp.where(causal, gap, NEG)
                weights.append(
                    (
                        jnp.exp(gap)
                        * couple_ref[at * tile : (at + 1) * tile, src * tile : (src + 1) * tile]
                    ).astype(BF16)
                )
            pieces.append(dot(jnp.concatenate(weights, axis=1), value[: (at + 1) * tile]))
        results.append(jnp.concatenate(pieces, axis=0))
        falls.append(fall)
    low = lane < HEAD_DIM
    gate = gate_ref[...].astype(F32)
    gate = gate / (1.0 + jnp.exp(-gate))
    skip = jnp.where(low, skip_ref[2 * pair], skip_ref[2 * pair + 1])
    within = jnp.where(low, results[0], results[1])
    base_ref[...] = ((within + skip * value.astype(F32)) * gate).astype(BF16)
    lift_ref[...] = (jnp.exp(jnp.where(low, falls[0], falls[1])) * gate).astype(BF16)


def finish_kernel(place_ref, f0, f1, f2, f3, read_ref, base_ref, lift_ref, gain_ref, out_ref, held):
    @pl.when(pl.program_id(0) == 0)
    def _():
        for step, ref in enumerate((f0, f1, f2, f3)):
            part = place_ref[0] ^ step
            held[pl.ds(pl.multiple_of(part * QUARTER, 64), QUARTER), :] = ref[...]

    together = one((iota((128, 128), 0) >> 6) == (iota((128, 128), 1) >> 6), BF16)
    pairs = [slice(pair * 128, (pair + 1) * 128) for pair in range(PAIRS)]
    carried = [dot_t(read_ref[...], held[now, :]) for now in pairs]
    gated = [
        base_ref[:, now].astype(F32) + lift_ref[:, now].astype(F32) * state
        for now, state in zip(pairs, carried)
    ]
    squares = [split(x * x, 2) for x in gated]
    means = [(dot(high, together) + dot(low, together)) * (1.0 / HEAD_DIM) for high, low in squares]
    for now, x, mean in zip(pairs, gated, means):
        out_ref[:, now] = (x * lax.rsqrt(mean + 1e-05) * gain_ref[:, now]).astype(BF16)


def shape(*dims, kind=BF16):
    return jax.ShapeDtypeStruct(dims, kind)


def lanes(rows, row_block=0):
    return pl.BlockSpec((rows, 128), lambda pair: (row_block, pair))


def whole(*dims):
    return pl.BlockSpec(dims, lambda pair: (0,) * len(dims))


def call_pack(key_rows, value_rows, valid):
    return pl.pallas_call(
        pack_kernel,
        out_shape=shape(ROWS + 16, WIDTH),
        in_specs=[VMEM] * 3,
        out_specs=VMEM,
        cost_estimate=FREE,
        compiler_params=params(),
        name="pack",
    )(key_rows, value_rows, valid)


def call_state(*args):
    far = pl.BlockSpec(memory_space=pltpu.HBM)
    return pl.pallas_call(
        state_kernel,
        out_shape=[shape(PIECE, STATE)] * 4,
        in_specs=[far] * 5 + [SMEM],
        out_specs=[VMEM] * 4,
        scratch_shapes=[
            pltpu.VMEM((WIDTH, STATE), F32),
            pltpu.VMEM((ROWS, WIDTH), BF16),
            pltpu.VMEM((HEADS_HERE, ROWS), F32),
            pltpu.VMEM((HEADS_HERE, ROWS), F32),
            pltpu.VMEM((1, ROWS), jnp.int32),
            pltpu.VMEM((ROWS, STATE), BF16),
            pltpu.SemaphoreType.DMA((5,)),
        ],
        cost_estimate=FREE,
        compiler_params=params(58),
        name="state",
    )(*args)


HOLD = [pltpu.VMEM((4, PIECE, STATE), F32)]


def call_block(place, *pieces):
    return pl.pallas_call(
        block_kernel,
        out_shape=[shape(PIECE, STATE), shape(4, QUARTER, STATE, kind=F32), shape(4, 8, STATE, kind=F32)],
        in_specs=[SMEM] + [VMEM] * 4,
        out_specs=[VMEM] * 3,
        scratch_shapes=HOLD,
        cost_estimate=FREE,
        compiler_params=params(),
        name="block",
    )(place, *pieces)


def call_line(place, *totals):
    return pl.pallas_call(
        line_kernel,
        out_shape=[shape(PIECE, STATE), shape(QUARTER, STATE, kind=F32), shape(8, STATE, kind=F32)],
        in_specs=[SMEM] + [VMEM] * 4,
        out_specs=[VMEM] * 3,
        scratch_shapes=HOLD,
        cost_estimate=FREE,
        compiler_params=params(),
        name="line",
    )(place, *totals)


def call_plane(place, *args):
    return pl.pallas_call(
        plane_kernel,
        out_shape=[shape(QUARTER, STATE)] * 4,
        in_specs=[SMEM] + [VMEM] * 8,
        out_specs=[VMEM] * 4,
        scratch_shapes=HOLD,
        cost_estimate=FREE,
        compiler_params=params(),
        name="plane",
    )(place, *args)


KEPT = [
    shape(WIDTH, HALF),
    shape(HEADS_HERE * 32, HALF),
    shape(WIDTH, HALF, kind=F32),
    shape(8 * PAIRS, HALF, kind=F32),
    shape(WIDTH, HALF),
    shape(8, ROWS, kind=F32),
]


def call_local(*args):
    return pl.pallas_call(
        local_kernel,
        out_shape=KEPT,
        in_specs=[VMEM] * 4 + [SMEM] * 3,
        out_specs=[VMEM] * 6,
        scratch_shapes=[
            pltpu.VMEM((ROWS, ROWS), BF16),
            pltpu.VMEM((WIDTH, ROWS), F32),
            pltpu.VMEM((WIDTH, ROWS), F32),
            pltpu.VMEM((WIDTH, ROWS), BF16),
        ],
        cost_estimate=FREE,
        compiler_params=params(14),
        name="local",
    )(*args)


def call_within(*args):
    return pl.pallas_call(
        within_kernel,
        grid=(PAIRS,),
        out_shape=[shape(ROWS, WIDTH)] * 2,
        in_specs=[lanes(ROWS)] * 2
        + [whole(HEADS_HERE, ROWS)] * 2
        + [whole(1, ROWS), whole(ROWS, STATE), whole(ROWS, STATE), SMEM],
        out_specs=[lanes(ROWS)] * 2,
        scratch_shapes=[pltpu.VMEM((ROWS, ROWS), F32), pltpu.VMEM((16, ROWS), F32), pltpu.VMEM((16, ROWS), F32)],
        cost_estimate=FREE,
        compiler_params=params(8),
        name="within",
    )(*args)


def call_finish(*args):
    def rows(width):
        return pl.BlockSpec((ROWS, width), lambda at: (at, 0))

    return pl.pallas_call(
        finish_kernel,
        grid=(1,),
        out_shape=shape(ROWS, WIDTH),
        in_specs=[SMEM]
        + [whole(QUARTER, STATE)] * 4
        + [rows(STATE)]
        + [rows(WIDTH)] * 2
        + [whole(1, WIDTH)],
        out_specs=rows(WIDTH),
        scratch_shapes=[pltpu.VMEM((WIDTH, STATE), BF16)],
        cost_estimate=FREE,
        compiler_params=params(20),
        name="finish",
    )(*args)


def call_near(kept, arrived):
    out, stat = pl.pallas_call(
        functools.partial(remote_kernel, True),
        out_shape=[KEPT[2], KEPT[3]],
        in_specs=[VMEM] * 8,
        out_specs=[VMEM] * 2,
        cost_estimate=FREE,
        compiler_params=params(14),
        name="near",
    )(*kept, *arrived)
    return [kept[0], kept[1], out, stat, kept[4], kept[5]]


def call_remote(kept, arrived):
    return pl.pallas_call(
        functools.partial(remote_kernel, False),
        out_shape=shape(ROWS, WIDTH),
        in_specs=[VMEM] * 7,
        out_specs=VMEM,
        scratch_shapes=[pltpu.VMEM((WIDTH, ROWS), BF16)],
        cost_estimate=FREE,
        compiler_params=params(14),
        name="remote",
    )(*kept, arrived)


def per_device(
    query_rows,
    key_rows,
    value_rows,
    patch_valid,
    segment_lengths,
    dilation,
    step_sizes,
    decay_rates,
    state_in,
    state_out,
    gate_in,
    skip_weight,
    norm_gain,
):
    count = lax.axis_size("seq")
    seq_rank = lax.axis_index("seq").astype(jnp.int32)
    rank = jnp.reshape(lax.axis_index("head").astype(jnp.int32), (1,))
    place = jnp.stack([seq_rank & 3, (seq_rank >> 2) & 3, seq_rank >> 4])
    valid = patch_valid.reshape(1, ROWS)
    gain = norm_gain.reshape(1, WIDTH)

    def cross(block, mask):
        return lax.ppermute(block, "seq", [(i, i ^ mask) for i in range(count)])

    def turn(block, step, span):
        unit = span // 4
        route = [(i, i // span * span + (i % span + step * unit) % span) for i in range(count)]
        return lax.ppermute(block, "seq", route)

    after = lax.optimization_barrier
    scan_inputs = (step_sizes, decay_rates, valid, state_in)

    pieces = call_state(value_rows, *scan_inputs, place)
    packed = call_pack(key_rows, value_rows, after((valid, pieces))[0])
    pieces = [pieces[0]] + [cross(pieces[mask], mask) for mask in range(1, SPAN_DEV)]
    near = [cross(packed, 1)]
    pieces = after((pieces, packed))[0]
    total, block_before, block_fade = call_block(place, *pieces)
    totals = [total] + [turn(total, step, 16) for step in range(1, 4)]
    packed, totals = after((packed, totals))
    near.append(cross(packed, 2))
    far = cross(packed, 3)
    total, line_before, line_fade = call_line(place, *totals)
    kept = call_local(
        query_rows, key_rows, value_rows, after((valid, total))[0], segment_lengths, dilation, rank
    )
    totals = [total] + [turn(total, step, 64) for step in range(1, 4)]
    totals = after((totals, kept))[0]
    carried = call_plane(place, *totals, line_before, line_fade, block_before, block_fade)
    scan_inputs = (*scan_inputs[:2], after((valid, carried))[0], state_in)
    within = call_within(value_rows, gate_in, *scan_inputs, state_out, skip_weight)
    carried = [carried[0]] + [cross(carried[mask], mask) for mask in range(1, SPAN_DEV)]
    kept = call_near(after((kept, within))[0], near)
    carried = after((carried, kept))[0]
    scanned = call_finish(place, *carried, state_out, *within, gain)
    attended = call_remote(kept, far)
    return (attended, scanned)


def solution(mesh):
    return jax.shard_map(
        per_device,
        mesh=mesh,
        in_specs=(
            P(("slide", "seq"), "head"),
            P(("slide", "seq"), "head"),
            P(("slide", "seq"), "head"),
            P(("slide", "seq")),
            P(),
            P(),
            P("head", ("slide", "seq")),
            P("head", ("slide", "seq")),
            P(("slide", "seq"), None),
            P(("slide", "seq"), None),
            P(("slide", "seq"), "head"),
            P("head"),
            P("head"),
        ),
        out_specs=(P(("slide", "seq"), "head"), P(("slide", "seq"), "head")),
        check_vma=False,
    )
```
